32 devices in a mesh: group: 2 (over y), batch: 4 (over z), mp: 2 (over x), section: 2 (over core).
Axes of the slice: x: 2, y: 2, z: 4, core: 2. Of those that a mesh axis runs over, the one named last changes fastest.
Arguments:
- queries: bfloat16 [2, 192, 8192], P('section', ('group', 'batch'), 'mp'), parts along dimension 1, may hold values from -6 to 6
- new_keys: bfloat16 [2, 192, 1024], P('section', ('group', 'batch'), 'mp'), parts along dimension 1, may hold values from -6 to 6
- new_values: bfloat16 [2, 192, 1024], P('section', ('group', 'batch'), 'mp'), parts along dimension 1, may hold values from -6 to 6
- key_pages: bfloat16 [2, 768, 16, 1024], P('section', ('group', 'batch'), None, 'mp'), parts along dimension 1, may hold values from -6 to 6
- value_pages: bfloat16 [2, 768, 16, 1024], P('section', ('group', 'batch'), None, 'mp'), parts along dimension 1, may hold values from -6 to 6
- page_table: int32 [192, 4], P(('group', 'batch')), parts along dimension 0, may hold values from 0 to 95, as said below
- ancestry: int32 [192], P('group'), parts along dimension 0, may hold values from 0 to 95, as said below
- lengths: int32 [192], P('group'), parts along dimension 0, may hold values from 1 to 64, as said below
- step_rows: bfloat16 [8192, 4096], P(('group', 'batch', 'section'), 'mp'), parts along dimension 0, may hold values from -6 to 6
- norm_gain: float32 [4096], replicated, may hold values from 0.1 to 1.9
- head_weight: bfloat16 [4096, 4096], P(('batch', 'section'), 'mp'), may hold values from -0.09375 to 0.09375
- head_bias: float32 [4096], P('mp'), may hold values from -5 to 5
- class_weight: bfloat16 [4096, 2], P('mp'), may hold values from -0.125 to 0.125
- class_bias: float32 [2], replicated, may hold values from -4 to 4
Outputs:
- attention: bfloat16 [2, 192, 8192], P('section', ('group', 'batch'), 'mp'), parts along dimension 1
- log_odds: float32 [8192], P(('group', 'batch', 'section')), parts along dimension 0
The draws below stay inside these ranges and needn't reach their ends.
There are 2 independent parts, one for each index of `group`. The reference program is written for one: setup_inputs(seed, part) draws one part's arguments, and reference() takes and returns one part's arrays. A program takes and returns all parts, laid end to end along the dimension named above; an argument that names none is the same for every part. Nothing has to cross between parts.
Inputs may be any that keep to these rules, and one draw needn't show every extreme that they name: The pages of the particles on one index of batch lie on that index; the page_table rows of those 24 particles name each of its 96 pages exactly once. Particle j belongs to problem j % 24, and ancestry[j] % 24 == j % 24. Particles j // 24 == d stand on index d of batch; the 24 slots on one index take at most 12 ancestors from any one index, and in every draw some index gives exactly 12 ancestors to the slots of every index. `lengths`: some particle has all 64 positions live in every draw.
All inputs are finite; a program needn't handle non-finite values.
Results may differ from the reference program's by a relative error of at most 0.0043.
Values may be sent and summed in bfloat16 or wider, within the bound.
No kernel may reach another device: no remote copies, remote signals or barrier semaphores. Data moves between devices by JAX's collectives and lax.ppermute only.
A program may use at most 64 MiB of HBM per device.

```python
import jax
import jax.numpy as jnp
from jax import lax

QH = 64
KVH = 8
HD = 128
VD = 4096
PAGE = 16
CTX = 64
LAYERS = 2
P_DEV = 24
CAP = 12
PAGES = 4
PARTICLES = 96
POOL = 384
VROWS = 4096


def draw_queries(key, part):
    shape = (LAYERS, PARTICLES, QH, HD)
    base = jnp.clip(jax.random.normal(key, shape, jnp.float32), -6.0, 6.0)
    return base.reshape(LAYERS, PARTICLES, QH * HD).astype(jnp.bfloat16)


def draw_key_pages(key, part):
    shape = (LAYERS, POOL, PAGE, KVH, HD)
    base = jnp.clip(jax.random.normal(key, shape, jnp.float32), -6.0, 6.0)
    return base.reshape(LAYERS, POOL, PAGE, KVH * HD).astype(jnp.bfloat16)


def draw_page_table(key, part):
    device_count = PARTICLES // P_DEV
    per_device = P_DEV * PAGES
    priority = jax.random.randint(key, (device_count, per_device), 0, 65536) * per_device + jnp.arange(per_device)[None, :]
    ordering = jnp.argsort(priority, axis=1)
    return ordering.reshape(PARTICLES, PAGES).astype(jnp.int32)


def draw_ancestry(key, part):
    device_count = PARTICLES // P_DEV
    key_star = jax.random.fold_in(key, 11)
    key_bias = jax.random.fold_in(key, 12)
    noise_random_key = jax.random.fold_in(key, 13)
    key_shuffle = jax.random.fold_in(key, 14)
    star = jax.random.randint(key_star, (), 0, device_count)
    device_bias = jax.random.randint(key_bias, (device_count,), 0, 8)
    noise = jax.random.randint(noise_random_key, (device_count, device_count), 0, 65536)
    device_ids = jnp.arange(device_count)
    priority = (device_bias[None, :] * 65536 + noise) * device_count + device_ids[None, :]
    priority = priority + jnp.where(device_ids == star, 1 << 29, 0)[None, :]
    priority = priority + jnp.where(device_ids[None, :] == device_ids[:, None], 1 << 28, 0)
    ordering = jnp.argsort(-priority, axis=1)
    chosen = ordering[:, jnp.arange(P_DEV) // CAP]
    shuffle_scores = jax.random.randint(key_shuffle, (device_count, P_DEV), 0, 65536) * P_DEV + jnp.arange(P_DEV)[None, :]
    shuffle = jnp.argsort(shuffle_scores, axis=1)
    source = jnp.take_along_axis(chosen, shuffle, axis=1)
    home_position = jnp.argmax((source == device_ids[:, None]).astype(jnp.int32), axis=1)
    last_source = source[:, P_DEV - 1]
    source = source.at[device_ids, home_position].set(last_source)
    source = source.at[:, P_DEV - 1].set(device_ids)
    return (source * P_DEV + jnp.arange(P_DEV)[None, :]).reshape(PARTICLES).astype(jnp.int32)


def draw_lengths(key, part):
    key_values = jax.random.fold_in(key, 21)
    key_longest = jax.random.fold_in(key, 22)
    values = jax.random.randint(key_values, (PARTICLES,), 1, CTX + 1)
    longest = jax.random.randint(key_longest, (), 0, PARTICLES)
    return jnp.where(jnp.arange(PARTICLES) == longest, CTX, values).astype(jnp.int32)


def steps_of(key, shape, shards, least, top_value):
    def one(axis_at, shards_of):
        heights = jax.random.uniform(jax.random.fold_in(jax.random.fold_in(key, 6), axis_at), (shards_of,), jnp.float32, least / len(shards), top_value / len(shards))
        return jnp.repeat(jnp.exp(heights), shape[axis_at] // shards_of).reshape((-1,) + (1,) * (len(shape) - axis_at - 1))

    gain = one(*shards[0])
    for cut in shards[1:]:
        gain = gain * one(*cut)
    return gain


def gaussian(stream_key, extent, spread, limit, shards=(), held_as=jnp.bfloat16):
    values = spread * jax.random.normal(stream_key, extent, jnp.float32)
    if shards:
        values = values * steps_of(stream_key, extent, shards, -0.22, 0.18)
    return jnp.clip(values, -limit, limit).astype(held_as)


def setup_inputs(seed: int = 0, part: int = 0) -> dict:
    key_list = jax.random.split(jax.random.key(seed), 15)
    part_splits = jax.random.split(jax.random.fold_in(key_list[14], part), 15)
    queries = draw_queries(jax.random.fold_in(jax.random.fold_in(key_list[14], part), 71), part)
    new_keys = gaussian(part_splits[1], (LAYERS, PARTICLES, KVH * HD), 1.0, 6.0, ((0, 2), (1, 4), (2, 2)))
    new_values = gaussian(part_splits[2], (LAYERS, PARTICLES, KVH * HD), 1.0, 6.0, ((0, 2), (1, 4), (2, 2)))
    key_pages = draw_key_pages(jax.random.fold_in(jax.random.fold_in(key_list[14], part), 71), part)
    value_pages = gaussian(part_splits[4], (LAYERS, POOL, PAGE, KVH * HD), 1.0, 6.0, ((0, 2), (1, 4), (3, 2)))
    page_table = draw_page_table(jax.random.fold_in(jax.random.fold_in(key_list[14], part), 71), part)
    ancestry = draw_ancestry(jax.random.fold_in(jax.random.fold_in(key_list[14], part), 71), part)
    lengths = draw_lengths(jax.random.fold_in(jax.random.fold_in(key_list[14], part), 71), part)
    step_rows = gaussian(part_splits[8], (VROWS, VD), 1.0, 6.0, ((0, 8), (1, 2)))
    norm_gain = jnp.clip(1.0 + 0.18 * jax.random.normal(key_list[9], (VD,), jnp.float32), 0.1, 1.9)
    head_weight = gaussian(key_list[10], (VD, VD), VD ** -0.5, 0.09375, ((0, 8), (1, 2)))
    head_bias = gaussian(key_list[11], (VD,), 1.0, 5.0, ((0, 2),), jnp.float32)
    class_weight = gaussian(key_list[12], (VD, 2), (VD // 2) ** -0.5, 0.125, ((0, 2),))
    class_bias = gaussian(key_list[13], (2,), 1.0, 4.0, (), jnp.float32)
    return {"queries": queries, "new_keys": new_keys, "new_values": new_values, "key_pages": key_pages, "value_pages": value_pages, "page_table": page_table, "ancestry": ancestry, "lengths": lengths, "step_rows": step_rows, "norm_gain": norm_gain, "head_weight": head_weight, "head_bias": head_bias, "class_weight": class_weight, "class_bias": class_bias}


def reference(queries, new_keys, new_values, key_pages, value_pages, page_table, ancestry, lengths, step_rows, norm_gain, head_weight, head_bias, class_weight, class_bias):
    score_scale = 1.0 / HD ** 0.5
    group_size = QH // KVH
    owner = ancestry // P_DEV
    pool_pages = page_table[ancestry] + (owner * (P_DEV * PAGES))[:, None]
    live_mask = jnp.arange(CTX)[None, :] < lengths[ancestry][:, None]

    def one_layer(layer_args):
        query_per_layer, layer_keys, layer_values, layer_key_pages, layer_value_pages = layer_args
        query_head_count = query_per_layer.reshape(PARTICLES, KVH, group_size, HD).astype(jnp.float32)
        cached_key_rows = layer_key_pages[pool_pages].reshape(PARTICLES, CTX, KVH, HD).astype(jnp.float32)
        cache_values = layer_value_pages[pool_pages].reshape(PARTICLES, CTX, KVH, HD).astype(jnp.float32)
        attention_scores = jnp.einsum('pkgd,ptkd->pkgt', query_head_count, cached_key_rows) * score_scale
        attention_scores = jnp.where(live_mask[:, None, None, :], attention_scores, -1e+30)
        top_score = lax.optimization_barrier(jnp.max(attention_scores, axis=-1))
        weights = jnp.exp(attention_scores - top_score[..., None])
        rounded = lax.optimization_barrier(weights.astype(jnp.bfloat16)).astype(jnp.float32)
        numerator = jnp.einsum('pkgt,ptkd->pkgd', rounded, cache_values)
        particle_key_rows = layer_keys.reshape(PARTICLES, KVH, HD).astype(jnp.float32)
        own_values = layer_values.reshape(PARTICLES, KVH, HD).astype(jnp.float32)
        own_score = jnp.einsum('pkgd,pkd->pkg', query_head_count, particle_key_rows) * score_scale
        own_weight = jnp.exp(own_score - top_score)
        denominator = lax.optimization_barrier(jnp.sum(weights, axis=-1)) + own_weight
        result = (numerator + own_weight[..., None] * own_values[:, :, None, :]) / denominator[..., None]
        return result.reshape(PARTICLES, QH * HD).astype(jnp.bfloat16)
    attention = lax.map(one_layer, (queries, new_keys, new_values, key_pages, value_pages))
    row_values = step_rows.astype(jnp.float32)
    power = lax.optimization_barrier(jnp.mean(row_values * row_values, axis=1, keepdims=True))
    normed = (row_values * lax.rsqrt(power + 1e-06) * norm_gain).astype(jnp.bfloat16)
    hidden = jnp.maximum(jnp.dot(normed, head_weight, preferred_element_type=jnp.float32) + head_bias, 0.0).astype(jnp.bfloat16)
    logits = jnp.dot(hidden, class_weight, preferred_element_type=jnp.float32) + class_bias
    log_odds = logits[:, 1] - logits[:, 0]
    return (attention, log_odds)
```

```python
import functools

import jax
import jax.numpy as jnp
from jax import lax
from jax.experimental import pallas as pl
from jax.experimental.pallas import tpu as pltpu
from jax.sharding import PartitionSpec as P

HD = 128
ANY = pl.BlockSpec(memory_space=pl.ANY)
VMEM = pl.BlockSpec(memory_space=pltpu.VMEM)
SMEM = pl.BlockSpec(memory_space=pltpu.SMEM)


def shift_pairs(count, step):
    return [(i, (i + step) % count) for i in range(count)]


def ring_order(count):
    return [0] + list(range(1, count, 2)) + [i for i in range(count - 1, 0, -1) if i % 2 == 0]


def attention_kernel(particle, page_table, lengths, blob, key_pages, value_pages, out, *, kv_local, unroll):
    slots = blob.shape[0]
    heads = out.shape[1]
    group_size = heads // kv_local
    pages = page_table.shape[1]
    context = pages * key_pages.shape[1]
    score_scale = 1.0 / HD**0.5
    lanes_kv = lax.broadcasted_iota(jnp.int32, (heads, kv_local * HD), 1) // HD
    rows_kv = lax.broadcasted_iota(jnp.int32, (heads, kv_local * HD), 0) // group_size
    diagonal = lanes_kv == rows_kv
    positions = lax.broadcasted_iota(jnp.int32, (heads, context), 1)

    def one(slot):
        ancestor = particle[slot]
        length = lengths[slot]
        rows = blob[slot]
        query = rows[:heads].astype(jnp.float32)
        own_key = rows[heads : heads + kv_local].astype(jnp.float32)
        own_value = rows[heads + kv_local :].astype(jnp.float32)

        def spread(x):
            return jnp.broadcast_to(x[:, None, :], (kv_local, group_size, HD)).reshape(heads, HD)

        wide = jnp.concatenate([query] * kv_local, axis=1)
        wide = jnp.where(diagonal, wide, 0.0).astype(jnp.bfloat16)
        keys = jnp.concatenate([key_pages[page_table[ancestor, i]] for i in range(pages)], axis=0)
        values = jnp.concatenate([value_pages[page_table[ancestor, i]] for i in range(pages)], axis=0)
        scores = lax.dot_general(
            wide, keys, (((1,), (1,)), ((), ())), preferred_element_type=jnp.float32
        ) * score_scale
        scores = jnp.where(positions < length, scores, -1e30)
        top = jnp.max(scores, axis=1, keepdims=True)
        weights = jnp.exp(scores - top)
        total = jnp.sum(weights, axis=1, keepdims=True)
        mixed = jnp.dot(weights.astype(jnp.bfloat16), values, preferred_element_type=jnp.float32)
        numerator = jnp.concatenate(
            [
                mixed[k * group_size : (k + 1) * group_size, k * HD : (k + 1) * HD]
                for k in range(kv_local)
            ],
            axis=0,
        )
        own_score = jnp.sum(query * spread(own_key), axis=1, keepdims=True) * score_scale
        own = jnp.exp(own_score - top)
        result = (numerator + own * spread(own_value)) / (total + own)
        out[slot] = result.astype(jnp.bfloat16)

    def body(i, carry):
        for u in range(unroll):
            one(i * unroll + u)
        return carry

    lax.fori_loop(0, slots // unroll, body, 0)


def serve(particle, page_table, lengths, blob, key_pages, value_pages):
    slots = blob.shape[0]
    kv_local = key_pages.shape[2] // HD
    heads = blob.shape[1] - 2 * kv_local
    unroll = 4 if slots % 4 == 0 else 1
    return pl.pallas_call(
        functools.partial(attention_kernel, kv_local=kv_local, unroll=unroll),
        out_shape=jax.ShapeDtypeStruct((slots, heads, HD), jnp.bfloat16),
        in_specs=[SMEM, SMEM, SMEM, VMEM, VMEM, VMEM],
        out_specs=VMEM,
        compiler_params=pltpu.CompilerParams(vmem_limit_bytes=24 << 20),
        cost_estimate=pl.CostEstimate(flops=20_000_000, bytes_accessed=6_000_000, transcendentals=100_000),
    )(particle, page_table, lengths, blob, key_pages, value_pages)


def exchange(blocks, axis):
    count = lax.axis_size(axis)
    if count <= 8:
        return [blocks[0]] + [
            lax.ppermute(blocks[k], axis, shift_pairs(count, k)) for k in range(1, count)
        ]
    me = lax.axis_index(axis)
    stacked = jnp.stack(blocks)
    order = (jnp.arange(count) - me) % count
    arrived = lax.all_to_all(stacked[order], axis, split_axis=0, concat_axis=0, tiled=True)
    back = (me - jnp.arange(count)) % count
    arrived = arrived[back]
    return [arrived[k] for k in range(count)]


def attend(queries, new_keys, new_values, key_pages, value_pages, page_table, ancestry, lengths):
    slot_count, page_count = page_table.shape
    kv_local = key_pages.shape[3] // HD
    heads = queries.shape[2] // HD
    count = lax.axis_size("batch")
    me = lax.axis_index("batch")
    capacity = max(2, (2 * slot_count + count - 1) // count)
    source = (ancestry // slot_count).reshape(count, slot_count)
    local = (ancestry % slot_count).reshape(count, slot_count)
    positions = jnp.arange(slot_count)
    earlier = positions[None, :] < positions[:, None]
    slot_ids = jnp.arange(capacity)
    shifts = jnp.arange(count)

    own_source = lax.dynamic_index_in_dim(source, me, 0, keepdims=False)
    own_rank = jnp.sum((own_source[:, None] == own_source[None, :]) & earlier, axis=1)
    wanted = (own_source[None, None, :] == ((me + shifts) % count)[:, None, None]) & (
        own_rank[None, None, :] == slot_ids[None, :, None]
    )
    wanted = wanted.reshape(count * capacity, slot_count).astype(jnp.bfloat16)
    rows = jnp.concatenate([queries[0], new_keys[0], new_values[0]], axis=1)
    outgoing = jnp.dot(wanted, rows, preferred_element_type=jnp.float32).astype(jnp.bfloat16)
    outgoing = outgoing.reshape(count, capacity, heads + 2 * kv_local, HD)
    arrived = exchange([outgoing[k] for k in range(count)], "batch")

    behind = (me - shifts) % count
    served_source = jnp.take(source, behind, axis=0)
    served_local = jnp.take(local, behind, axis=0)
    match = served_source == me
    rank = jnp.sum(match[:, None, :] & earlier[None], axis=2)
    served = match[:, None, :] & (rank[:, None, :] == slot_ids[None, :, None])
    particle = jnp.sum(jnp.where(served, served_local[:, None, :], 0), axis=2).reshape(-1)
    local_lengths = lax.dynamic_slice_in_dim(lengths, me * slot_count, slot_count)
    served_lengths = jnp.sum(
        jnp.where(particle[:, None] == positions[None, :], local_lengths[None, :], 0), axis=1
    )
    blob = jnp.concatenate(arrived, axis=0)
    result = serve(particle, page_table, served_lengths, blob, key_pages[0], value_pages[0])
    result = result.reshape(count, capacity, heads, HD)
    returned = exchange([result[(-k) % count] for k in range(count)], "batch")
    returned = jnp.concatenate([returned[(-k) % count] for k in range(count)], axis=0)
    returned = returned.reshape(count * capacity, heads * HD)
    attention = lax.dot_general(
        wanted, returned, (((0,), (0,)), ((), ())), preferred_element_type=jnp.float32
    ).astype(jnp.bfloat16)
    return attention[None]


def gemm_kernel(*refs, parts, chunks, own_rows, has_acc, final, tile):
    refs = list(refs)
    part_of, offset_of, column = refs[:3]
    del refs[:3]
    halves = [refs[:parts], refs[parts : 2 * parts]]
    del refs[: 2 * parts]
    weights = refs[: len(chunks)]
    del refs[: len(chunks)]
    acc_in = refs.pop(0) if has_acc else None
    bias = class_weight = None
    if final:
        bias, class_weight = refs[:2]
        del refs[:2]
    out = refs.pop(0)
    x_v, w_v, acc_v, sems, acc_sem = refs
    rows = halves[0][0].shape[0]
    width = acc_v.shape[1]
    starts = [sum(chunks[:i]) for i in range(len(chunks))]

    def copies(i):
        depth = chunks[i]
        offset = pl.multiple_of(offset_of[i], 128)
        found = []
        for r in range(2):
            for p in range(parts):
                found.append(
                    (
                        p,
                        pltpu.make_async_copy(
                            halves[r][p].at[:, pl.ds(offset, depth)],
                            x_v.at[pl.ds(r * rows, rows), pl.ds(starts[i], depth)],
                            sems.at[i, r],
                        ),
                    )
                )
        source = weights[i]
        if source.shape[1] != width:
            source = source.at[:, pl.ds(pl.multiple_of(column[0], 128), width)]
        return found, pltpu.make_async_copy(source, w_v.at[pl.ds(starts[i], depth)], sems.at[i, 2])

    if has_acc:
        acc_copy = pltpu.make_async_copy(acc_in, acc_v, acc_sem)
        acc_copy.start()
    for i in range(len(chunks)):
        found, weight = copies(i)
        weight.start()
        for p, copy in found:
            pl.when(part_of[i] == p)(copy.start)
    groups = []
    i = 0
    while i < len(chunks):
        j, depth = i, 0
        while j < len(chunks) and depth < 1024:
            depth += chunks[j]
            j += 1
        groups.append((i, j))
        i = j
    for g, (first, last) in enumerate(groups):
        for i in range(first, last):
            found, weight = copies(i)
            weight.wait()
            for r in range(2):
                found[r * parts][1].wait()
        if g == 0 and has_acc:
            acc_copy.wait()
        k0 = starts[first]
        k1 = starts[last - 1] + chunks[last - 1]
        fresh = g == 0 and not has_acc

        def body(m, carry):
            at = pl.ds(pl.multiple_of(m * tile, tile), tile)
            product = jnp.dot(x_v[at, k0:k1], w_v[k0:k1, :], preferred_element_type=jnp.float32)
            total = product if fresh else acc_v[at, :] + product
            if final and g == len(groups) - 1:
                hidden = jnp.maximum(total + bias[...], 0.0).astype(jnp.bfloat16)
                out[:, at] = lax.dot_general(
                    class_weight[...], hidden, (((1,), (1,)), ((), ())), preferred_element_type=jnp.float32
                )
            elif g == len(groups) - 1:
                out[at, :] = total
            else:
                acc_v[at, :] = total
            return carry

        lax.fori_loop(0, 2 * rows // tile, body, 0)


def gemm(part_of, offset_of, column, halves, weights, acc=None, tail=None):
    parts = len(halves[0])
    rows = halves[0][0].shape[0]
    chunks = [w.shape[0] for w in weights]
    width = min(w.shape[1] for w in weights)
    depth = sum(chunks)
    tile = 256 if (2 * rows) % 256 == 0 else 2 * rows
    args = [part_of, offset_of, column, *halves[0], *halves[1], *weights]
    specs = [SMEM] * 3 + [ANY] * (2 * parts + len(weights))
    if acc is not None:
        args.append(acc)
        specs.append(ANY)
    if tail is not None:
        args += list(tail)
        specs += [VMEM] * 2
        out_shape = jax.ShapeDtypeStruct((tail[1].shape[0], 2 * rows), jnp.float32)
    else:
        out_shape = jax.ShapeDtypeStruct((2 * rows, width), jnp.float32)
    return pl.pallas_call(
        functools.partial(
            gemm_kernel,
            parts=parts,
            chunks=tuple(chunks),
            own_rows=rows,
            has_acc=acc is not None,
            final=tail is not None,
            tile=tile,
        ),
        out_shape=out_shape,
        in_specs=specs,
        out_specs=VMEM,
        scratch_shapes=[
            pltpu.VMEM((2 * rows, depth), jnp.bfloat16),
            pltpu.VMEM((depth, width), jnp.bfloat16),
            pltpu.VMEM((2 * rows, width), jnp.float32),
            pltpu.SemaphoreType.DMA((len(chunks), 3)),
            pltpu.SemaphoreType.DMA,
        ],
        compiler_params=pltpu.CompilerParams(vmem_limit_bytes=40 << 20),
        cost_estimate=pl.CostEstimate(
            flops=4 * rows * width * depth,
            bytes_accessed=4 * rows * depth + 2 * depth * width + 8 * rows * width,
            transcendentals=0,
        ),
    )(*args)


def judge(step_rows, norm_gain, head_weight, head_bias, class_weight, class_bias):
    z_count, x_count = lax.axis_size("batch"), lax.axis_size("mp")
    y_count = lax.axis_size("group")
    z, x = lax.axis_index("batch"), lax.axis_index("mp")
    s, y = lax.axis_index("section"), lax.axis_index("group")
    swap = shift_pairs(2, 1)
    rows, features = step_rows.shape
    block, columns = head_weight.shape
    width = columns // 2
    share = block // y_count

    def cut(yy, ss):
        return lax.dynamic_slice(head_weight, (yy * share, ss * width), (share, width))

    travelling = [cut(y, s), lax.ppermute(cut(y, 1 - s), "section", swap)]
    siblings = [travelling[1]] + [
        lax.ppermute(cut((y + k) % y_count, 1 - s), "section", swap) for k in range(1, y_count)
    ]
    order = ring_order(z_count)
    ring = [(order[i], order[(i + 1) % z_count]) for i in range(z_count)]
    place = jnp.asarray([order.index(i) for i in range(z_count)])[z]

    values = step_rows.astype(jnp.float32)
    power = jnp.sum(values * values, axis=1)
    power = sum(
        [lax.ppermute(power, "mp", shift_pairs(x_count, k)) for k in range(1, x_count)], power
    )
    power = power / (features * x_count)
    gain = lax.dynamic_slice(norm_gain, (x * features,), (features,))
    normed = (values * lax.rsqrt(power + 1e-06)[:, None] * gain).astype(jnp.bfloat16)
    mine = [normed] + [
        lax.ppermute(normed, "mp", shift_pairs(x_count, k)) for k in range(1, x_count)
    ]
    theirs = [lax.ppermute(part, "section", swap) for part in mine]
    halves = (mine, theirs)

    def place_of(zz, ss, yy):
        feature = (2 * zz + ss) * block + yy * share
        return (x - feature // features) % x_count, feature % features

    own_place = [place_of(z, s, 0)] + [
        place_of(z, 1 - s, (y + k) % y_count) for k in range(y_count)
    ]
    hops = []
    hop_places = []
    for hop in range(1, z_count):
        travelling = [lax.ppermute(t, "batch", ring) for t in travelling]
        zz = jnp.asarray(order)[(place - hop) % z_count]
        buffers, places = [], []
        for j, t in enumerate(travelling):
            ss = s if j == 0 else 1 - s
            for k in range(y_count):
                buffers.append(t if k == 0 else lax.ppermute(t, "group", shift_pairs(y_count, k)))
                places.append(place_of(zz, ss, (y - k) % y_count))
        hops.append(buffers)
        hop_places.append(places)

    def tables(places):
        return jnp.stack([p for p, _ in places]).astype(jnp.int32), jnp.stack(
            [o for _, o in places]
        ).astype(jnp.int32)

    column = (s * width).reshape(1).astype(jnp.int32)
    early = [head_weight] + siblings + sum(hops[:-1], [])
    early_places = own_place + sum(hop_places[:-1], [])
    acc = gemm(*tables(early_places), column, halves, early)
    bias = lax.dynamic_slice(head_bias, (s * width,), (width,))[None]
    classes = lax.dynamic_slice(class_weight, (s * width, 0), (width, 2)).T
    classes = jnp.concatenate([classes, jnp.zeros((14, width), classes.dtype)], axis=0)
    logits = gemm(*tables(hop_places[-1]), column, halves, hops[-1], acc, (bias, classes))
    partial = logits[1] - logits[0]
    kept, given = partial[:rows], partial[rows:]
    total = kept + lax.ppermute(given, "section", swap)
    for k in range(1, x_count):
        total = total + lax.ppermute(kept, "mp", shift_pairs(x_count, k))
        total = total + lax.ppermute(
            given,
            ("mp", "section"),
            [
                (i * 2 + c, ((i + k) % x_count) * 2 + 1 - c)
                for i in range(x_count)
                for c in range(2)
            ],
        )
    return total + (class_bias[1] - class_bias[0])


def judge_gathered(step_rows, norm_gain, head_weight, head_bias, class_weight, class_bias):
    full_rows = lax.all_gather(step_rows, "mp", axis=1, tiled=True)
    row_values = full_rows.astype(jnp.float32)
    power = jnp.mean(row_values * row_values, axis=1, keepdims=True)
    normed = (row_values * lax.rsqrt(power + 1e-06) * norm_gain).astype(jnp.bfloat16)
    projected = jnp.dot(
        normed,
        lax.all_gather(head_weight, ("batch", "section"), axis=0, tiled=True),
        preferred_element_type=jnp.float32,
    )
    hidden = jnp.maximum(projected + head_bias, 0.0).astype(jnp.bfloat16)
    partial_logits = jnp.dot(hidden, class_weight, preferred_element_type=jnp.float32)
    logits = lax.psum(partial_logits, "mp") + class_bias
    return logits[:, 1] - logits[:, 0]


def per_device(
    queries,
    new_keys,
    new_values,
    key_pages,
    value_pages,
    page_table,
    ancestry,
    lengths,
    step_rows,
    norm_gain,
    head_weight,
    head_bias,
    class_weight,
    class_bias,
):
    attention = attend(
        queries, new_keys, new_values, key_pages, value_pages, page_table, ancestry, lengths
    )
    ring_fits = (
        lax.axis_size("batch") <= 8
        and lax.axis_size("section") == 2
        and head_weight.shape[0] % (128 * lax.axis_size("group")) == 0
        and head_weight.shape[1] % 256 == 0
        and step_rows.shape[1] % head_weight.shape[0] == 0
    )
    form = judge if ring_fits else judge_gathered
    log_odds = form(step_rows, norm_gain, head_weight, head_bias, class_weight, class_bias)
    return (attention, log_odds)


def solution(mesh):
    placed = (
        P("section", ("group", "batch"), "mp"),
        P("section", ("group", "batch"), "mp"),
        P("section", ("group", "batch"), "mp"),
        P("section", ("group", "batch"), None, "mp"),
        P("section", ("group", "batch"), None, "mp"),
        P(("group", "batch"), None),
        P("group"),
        P("group"),
        P(("group", "batch", "section"), "mp"),
        P(),
        P(("batch", "section"), "mp"),
        P("mp"),
        P("mp", None),
        P(),
    )
    return jax.shard_map(
        per_device,
        mesh=mesh,
        in_specs=placed,
        out_specs=(P("section", ("group", "batch"), "mp"), P(("group", "batch", "section"))),
        check_vma=False,
    )
```

```python
import functools

import jax
import jax.numpy as jnp
from jax import lax
from jax.experimental import pallas as pl
from jax.experimental.pallas import tpu as pltpu
from jax.sharding import PartitionSpec as P

HD = 128
VMEM_LIMIT = 24 << 20
BRIEF = pl.CostEstimate(flops=1, bytes_accessed=1, transcendentals=0)
ANY = pl.BlockSpec(memory_space=pltpu.HBM)
WAITED = pl.BlockSpec(memory_space=pl.ANY)
VMEM = pl.BlockSpec(memory_space=pltpu.VMEM)
SMEM = pl.BlockSpec(memory_space=pltpu.SMEM)


def pass_kernel(*refs):
    del refs


def after(passing, waited):
    many = len(passing)
    out = pl.pallas_call(
        pass_kernel,
        out_shape=[jax.ShapeDtypeStruct(a.shape, a.dtype) for a in passing],
        in_specs=[ANY] * many + [WAITED] * len(waited),
        out_specs=[ANY] * many,
        input_output_aliases={i: i for i in range(many)},
        cost_estimate=BRIEF,
        compiler_params=pltpu.CompilerParams(has_side_effects=True),
    )(*passing, *waited)
    return list(out)


def shift_pairs(count, step):
    return [(i, (i + step) % count) for i in range(count)]


def ring_order(count):
    return [0] + list(range(1, count, 2)) + [i for i in range(count - 1, 0, -1) if i % 2 == 0]


def pack_kernel(
    me, ancestry, lengths, queries, new_keys, new_values, waited,
    blobs, particle, length, pick, rows, request, seen, *, count, capacity
):
    del waited
    slots = queries.shape[0]
    at = 0
    for source in (queries, new_keys, new_values):
        for h in range(source.shape[1] // HD):
            rows[:, at, :] = source[:, h * HD : (h + 1) * HD].astype(jnp.float32)
            at += 1
    here = me[0]
    for k in range(count):
        seen[k] = 0

    def clear(i, carry):
        request[i] = 0
        particle[i] = 0
        length[i] = 1
        return carry

    lax.fori_loop(0, count * capacity, clear, 0)

    def ask(j, carry):
        owner = ancestry[here * slots + j] // slots
        rank = jnp.minimum(seen[owner], capacity - 1)
        seen[owner] = rank + 1
        pick[j] = owner * capacity + rank
        request[owner * capacity + rank] = j
        return carry

    lax.fori_loop(0, slots, ask, 0)

    def fill(i, carry):
        for k in range(count):
            blobs[k, i] = rows[request[k * capacity + i]].astype(jnp.bfloat16)
        return carry

    lax.fori_loop(0, capacity, fill, 0)
    for k in range(count):

        def answer(p, rank):
            ancestor = ancestry[k * slots + p]
            local = ancestor - here * slots
            match = (local >= 0) & (local < slots)
            at = k * capacity + jnp.minimum(rank, capacity - 1)

            @pl.when(match)
            def _():
                particle[at] = local
                length[at] = lengths[ancestor]

            return rank + match.astype(jnp.int32)

        lax.fori_loop(0, slots, answer, 0)


def pack(me, ancestry, lengths, queries, new_keys, new_values, waited, count, capacity):
    slots = queries.shape[0]
    depth = (queries.shape[1] + new_keys.shape[1] + new_values.shape[1]) // HD
    table = jax.ShapeDtypeStruct((count * capacity,), jnp.int32)
    out = pl.pallas_call(
        functools.partial(pack_kernel, count=count, capacity=capacity),
        out_shape=[jax.ShapeDtypeStruct((count, capacity, depth, HD), jnp.bfloat16)]
        + [table, table, jax.ShapeDtypeStruct((slots,), jnp.int32)],
        in_specs=[SMEM] * 3 + [VMEM] * 3 + [ANY],
        out_specs=[VMEM] + [SMEM] * 3,
        scratch_shapes=[
            pltpu.VMEM((slots, depth, HD), jnp.float32),
            pltpu.SMEM((count * capacity,), jnp.int32),
            pltpu.SMEM((count,), jnp.int32),
        ],
        cost_estimate=BRIEF,
        compiler_params=pltpu.CompilerParams(vmem_limit_bytes=VMEM_LIMIT),
    )(me, ancestry, lengths, queries, new_keys, new_values, waited)
    return out


def serve_kernel(particle, page_table, lengths, blobs, key_pages, value_pages, outs, *, kv_local, unroll):
    count, capacity, heads = outs.shape[:3]
    group_size = heads // kv_local
    pages = page_table.shape[1]
    context = pages * key_pages.shape[1]
    score_scale = 1.0 / HD**0.5
    lanes_kv = lax.broadcasted_iota(jnp.int32, (heads, kv_local * HD), 1) // HD
    rows_kv = lax.broadcasted_iota(jnp.int32, (heads, kv_local * HD), 0) // group_size
    diagonal = lanes_kv == rows_kv
    positions = lax.broadcasted_iota(jnp.int32, (heads, context), 1)

    def spread(x):
        return jnp.broadcast_to(x[:, None, :], (kv_local, group_size, HD)).reshape(heads, HD)

    def together(k, slots):
        scores, own_products, own_values = [], [], []
        for slot in slots:
            at = k * capacity + slot
            rows = blobs[k, slot]
            query = rows[:heads].astype(jnp.float32)
            own_key = rows[heads : heads + kv_local].astype(jnp.float32)
            own_value = rows[heads + kv_local :].astype(jnp.float32)
            wide = jnp.concatenate([query] * kv_local, axis=1)
            wide = jnp.where(diagonal, wide, 0.0).astype(jnp.bfloat16)
            keys = jnp.concatenate(
                [key_pages[page_table[particle[at], i]] for i in range(pages)], axis=0
            )
            score = lax.dot_general(
                wide, keys, (((1,), (1,)), ((), ())), preferred_element_type=jnp.float32
            ) * score_scale
            scores.append(jnp.where(positions < lengths[at], score, -1e30))
            own_products.append(query * spread(own_key))
            own_values.append(spread(own_value))
        score = jnp.concatenate(scores, axis=0)
        top = jnp.max(score, axis=1, keepdims=True)
        weights = jnp.exp(score - top)
        own_score = jnp.sum(jnp.concatenate(own_products, axis=0), axis=1, keepdims=True) * score_scale
        own = jnp.exp(own_score - top)
        total = jnp.sum(weights, axis=1, keepdims=True) + own
        weights = weights.astype(jnp.bfloat16)
        for u, slot in enumerate(slots):
            at = k * capacity + slot
            mine = slice(u * heads, (u + 1) * heads)
            values = jnp.concatenate(
                [value_pages[page_table[particle[at], i]] for i in range(pages)], axis=0
            )
            mixed = jnp.dot(weights[mine], values, preferred_element_type=jnp.float32)
            numerator = jnp.concatenate(
                [
                    mixed[g * group_size : (g + 1) * group_size, g * HD : (g + 1) * HD]
                    for g in range(kv_local)
                ],
                axis=0,
            )
            result = (numerator + own[mine] * own_values[u]) / total[mine]
            outs[k, slot] = result.astype(jnp.bfloat16)

    def body(k, carry):
        for i in range(0, capacity, unroll):
            together(k, range(i, min(i + unroll, capacity)))
        return carry

    lax.fori_loop(0, count, body, 0)


def serve(particle, page_table, lengths, blobs, key_pages, value_pages):
    count, capacity, depth = blobs.shape[:3]
    kv_local = key_pages.shape[2] // HD
    heads = depth - 2 * kv_local
    return pl.pallas_call(
        functools.partial(serve_kernel, kv_local=kv_local, unroll=12),
        out_shape=jax.ShapeDtypeStruct((count, capacity, heads, HD), jnp.bfloat16),
        in_specs=[SMEM] * 3 + [VMEM] * 3,
        out_specs=VMEM,
        cost_estimate=BRIEF,
        compiler_params=pltpu.CompilerParams(vmem_limit_bytes=VMEM_LIMIT),
    )(particle, page_table, lengths, blobs, key_pages, value_pages)


def pick_kernel(pick, parts, out, rows):
    slots = out.shape[0]
    capacity = parts.shape[1]

    def take(j, carry):
        rows[j] = parts[pick[j] // capacity, lax.rem(pick[j], capacity)].astype(jnp.float32)
        return carry

    lax.fori_loop(0, slots, take, 0)
    for h in range(rows.shape[1]):
        out[:, h * HD : (h + 1) * HD] = rows[:, h, :].astype(jnp.bfloat16)


def pick_up(pick, parts):
    heads = parts.shape[2]
    slots = pick.shape[0]
    return pl.pallas_call(
        pick_kernel,
        out_shape=jax.ShapeDtypeStruct((slots, heads * HD), jnp.bfloat16),
        in_specs=[SMEM, VMEM],
        out_specs=VMEM,
        scratch_shapes=[pltpu.VMEM((slots, heads, HD), jnp.float32)],
        cost_estimate=BRIEF,
        compiler_params=pltpu.CompilerParams(vmem_limit_bytes=VMEM_LIMIT),
    )(pick, parts)


class Attention:
    def __init__(self, queries, new_keys, new_values, key_pages, value_pages, page_table, ancestry, lengths):
        self.count = lax.axis_size("batch")
        slots = page_table.shape[0]
        self.capacity = max(2, (2 * slots + self.count - 1) // self.count)
        self.rows = (ancestry, lengths, queries[0], new_keys[0], new_values[0])
        self.page_table, self.keys, self.values = page_table, key_pages[0], value_pages[0]

    def pack(self, waited):
        me = lax.axis_index("batch").reshape(1).astype(jnp.int32)
        blobs, self.particle, self.lengths, self.pick = pack(
            me, *self.rows, waited, self.count, self.capacity
        )
        return blobs

    def send(self, blobs):
        return lax.all_to_all(blobs, "batch", split_axis=0, concat_axis=0, tiled=True)

    def answer(self, arrived):
        return serve(
            self.particle, self.page_table, self.lengths, arrived, self.keys, self.values
        )

    def finish(self, returned):
        return pick_up(self.pick, returned)[None]


def cut_kernel(me, weight, out, sem, *, back, other, y_count):
    share, width = out.shape
    core = 1 - me[2] if other else me[2]
    rows = pl.ds(pl.multiple_of(lax.rem(me[3] + back, y_count) * share, share), share)
    lanes = pl.ds(pl.multiple_of(core * width, width), width)
    copy = pltpu.make_async_copy(weight.at[rows, lanes], out, sem)
    copy.start()
    copy.wait()


def cut_share(me, weight, share, width, y_count, other, back):
    return pl.pallas_call(
        functools.partial(cut_kernel, back=back, other=other, y_count=y_count),
        out_shape=jax.ShapeDtypeStruct((share, width), weight.dtype),
        in_specs=[SMEM, ANY],
        out_specs=VMEM,
        scratch_shapes=[pltpu.SemaphoreType.DMA],
        cost_estimate=BRIEF,
        compiler_params=pltpu.CompilerParams(vmem_limit_bytes=VMEM_LIMIT),
    )(me, weight)


def power_kernel(x, waited, out):
    del waited
    rows, features = x.shape

    def body(i, carry):
        at = pl.ds(pl.multiple_of(i * HD, HD), HD)
        total = jnp.zeros((HD, HD), jnp.float32)
        for j in range(features // HD):
            v = x[at, j * HD : (j + 1) * HD].astype(jnp.float32)
            total = total + v * v
        out[pl.ds(i, 1), :] = jnp.sum(total.T, axis=0, keepdims=True)
        return carry

    lax.fori_loop(0, rows // HD, body, 0)


def row_power(x, waited):
    return pl.pallas_call(
        power_kernel,
        out_shape=jax.ShapeDtypeStruct((x.shape[0] // HD, HD), jnp.float32),
        in_specs=[VMEM, ANY],
        out_specs=VMEM,
        cost_estimate=BRIEF,
        compiler_params=pltpu.CompilerParams(vmem_limit_bytes=VMEM_LIMIT),
    )(x, waited)


def norm_kernel(me, x, *refs, total, count):
    powers, (gain, *outs) = refs[:count], refs[count:]
    rows, features = x.shape
    part = outs[0].shape[1]
    power = powers[0][...]
    for p in powers[1:]:
        power = power + p[...]
    scale = lax.rsqrt(power / total + 1e-06)
    start = me[0] * features

    for i in range(rows // HD):
        column = jnp.broadcast_to(scale[i : i + 1, :], (HD, HD)).T
        for j in range(features // HD):
            at = (slice(i * HD, (i + 1) * HD), slice(j * HD, (j + 1) * HD))
            lanes = pl.ds(pl.multiple_of(start + j * HD, HD), HD)
            value = (x[at].astype(jnp.float32) * column * gain[:, lanes]).astype(jnp.bfloat16)
            first = j * HD % part
            outs[j * HD // part][at[0], first : first + HD] = value


def normalise(me, x, powers, gain, pieces):
    shape = (x.shape[0], x.shape[1] // pieces)
    return pl.pallas_call(
        functools.partial(
            norm_kernel, total=gain.shape[0], count=len(powers)
        ),
        out_shape=[jax.ShapeDtypeStruct(shape, jnp.bfloat16)] * pieces,
        in_specs=[SMEM] + [VMEM] * (2 + len(powers)),
        out_specs=[VMEM] * pieces,
        cost_estimate=BRIEF,
        compiler_params=pltpu.CompilerParams(vmem_limit_bytes=VMEM_LIMIT),
    )(me, x, *powers, gain[None])


class Layout:
    def __init__(self, order, x_count, y_count, block, features, part):
        self.order, self.x_count, self.y_count = order, x_count, y_count
        self.block, self.features, self.part = block, features, part
        self.share = block // y_count

    def place(self, me, run):
        hops, other, back, row = run
        x, z, s, y = me[0], me[1], me[2], me[3]
        count = len(self.order)
        owner = 0
        for i, at in enumerate(self.order):
            owner = owner + jnp.where(z == at, self.order[(i - hops) % count], 0)
        core = 1 - s if other else s
        feature = (2 * owner + core) * self.block + row
        if back is not None:
            group = y - back
            feature = feature + jnp.where(group < 0, group + self.y_count, group) * self.share
        per_device = self.features // self.part
        index = 0
        for i in range(1, self.x_count * per_device):
            index = index + (feature >= i * self.part).astype(jnp.int32)
        offset = feature - index * self.part
        index = index - x * per_device
        return self.rotated(index, per_device, self.x_count * per_device), offset

    def rotated(self, index, per_device, blocks):
        index = jnp.where(index < 0, index + blocks, index)
        place = 0
        for ahead in range(self.x_count):
            back = (self.x_count - ahead) % self.x_count
            inside = (index >= ahead * per_device) & (index < (ahead + 1) * per_device)
            place = place + jnp.where(inside, index + (back - ahead) * per_device, 0)
        return place


def carried(hops, back, share, first, count):
    runs = []
    for other in (False, True):
        low, high = max(first, other * share), min(first + count, (other + 1) * share)
        if low < high:
            runs.append(((hops, other, back, low - other * share), low - first, high - low))
    return runs


def merge_kernel(*refs):
    *sources, out = refs
    at = 0
    for source in sources:
        out[at : at + source.shape[0]] = source[...]
        at += source.shape[0]


def merge(sources):
    rows = sum(a.shape[0] for a in sources)
    return pl.pallas_call(
        merge_kernel,
        out_shape=jax.ShapeDtypeStruct((rows,) + sources[0].shape[1:], sources[0].dtype),
        in_specs=[VMEM] * len(sources),
        out_specs=VMEM,
        cost_estimate=BRIEF,
        compiler_params=pltpu.CompilerParams(vmem_limit_bytes=VMEM_LIMIT),
    )(*sources)


def split_kernel(source, *refs, pieces):
    outs = refs[-pieces:]
    at = 0
    for out in outs:
        out[...] = source[at : at + out.shape[0]]
        at += out.shape[0]


def split(source, pieces, waited):
    shape = (source.shape[0] // pieces,) + source.shape[1:]
    return pl.pallas_call(
        functools.partial(split_kernel, pieces=pieces),
        out_shape=[jax.ShapeDtypeStruct(shape, source.dtype)] * pieces,
        in_specs=[VMEM] + [WAITED] * len(waited),
        out_specs=[VMEM] * pieces,
        cost_estimate=BRIEF,
        compiler_params=pltpu.CompilerParams(vmem_limit_bytes=VMEM_LIMIT),
    )(source, *waited)


def gemm_kernel(me, *refs, parts, sources, runs, layout, has_acc, final, tile):
    refs = list(refs)
    halves = [refs[:parts], refs[parts : 2 * parts]]
    del refs[: 2 * parts]
    weights = refs[:sources]
    del refs[:sources]
    acc_in = refs.pop(0) if has_acc else None
    bias = class_weight = None
    if final:
        bias, class_weight = refs[:2]
        del refs[:2]
        outs = [refs.pop(0), refs.pop(0)]
    else:
        out = refs.pop(0)
    x_v, w_v, sems = refs
    rows = halves[0][0].shape[0]
    width = w_v.shape[1]
    depths = [depth for _, _, _, depth in runs]
    starts = [sum(depths[:i]) for i in range(len(depths))]
    columns = pl.ds(pl.multiple_of(me[2] * width, width), width)

    def weight_copy(i):
        _, which, row, depth = runs[i]
        source = weights[which]
        lanes = slice(None) if source.shape[1] == width else columns
        source = source.at[row : row + depth, lanes]
        return pltpu.make_async_copy(source, w_v.at[pl.ds(starts[i], depths[i])], sems.at[i, 2])

    def row_copy(i, r, p, offset):
        return pltpu.make_async_copy(
            halves[r][p].at[:, pl.ds(offset, depths[i])],
            x_v.at[pl.ds(r * rows, rows), pl.ds(starts[i], depths[i])],
            sems.at[i, r],
        )

    for i, (run, _, _, _) in enumerate(runs):
        weight_copy(i).start()
        part, offset = layout.place(me, run)
        offset = pl.multiple_of(offset, HD)
        for r in range(2):
            for p in range(parts):
                pl.when(part == p)(row_copy(i, r, p, offset).start)
    groups = []
    i = 0
    while i < len(runs):
        j, depth = i, 0
        while j < len(runs) and depth < 1024:
            depth += depths[j]
            j += 1
        groups.append((i, j))
        i = j
    for g, (first, last) in enumerate(groups):
        for i in range(first, last):
            weight_copy(i).wait()
            for r in range(2):
                row_copy(i, r, 0, 0).wait()
        k0 = starts[first]
        k1 = starts[last - 1] + depths[last - 1]

        def body(m, carry, target=None, base=0):
            at = pl.ds(pl.multiple_of(base + m * tile, tile), tile)
            product = jnp.dot(x_v[at, k0:k1], w_v[k0:k1, :], preferred_element_type=jnp.float32)
            if g > 0:
                total = out[at, :] + product
            elif has_acc:
                total = acc_in[at, :] + product
            else:
                total = product
            if target is not None:
                hidden = jnp.maximum(total + bias[:, columns], 0.0).astype(jnp.bfloat16)
                logits = lax.dot_general(
                    class_weight[:, columns],
                    hidden,
                    (((1,), (1,)), ((), ())),
                    preferred_element_type=jnp.float32,
                )
                target[:, pl.ds(pl.multiple_of(m * tile, tile), tile)] = logits[1:2] - logits[0:1]
            else:
                out[at, :] = total
            return carry

        if final:
            for r in range(2):
                lax.fori_loop(
                    0, rows // tile, functools.partial(body, target=outs[r], base=r * rows), 0
                )
        else:
            lax.fori_loop(0, 2 * rows // tile, body, 0)


def gemm(me, layout, halves, chunks, acc=None, tail=None):
    weights = [w for w, _ in chunks]
    runs = [(run, i, row, d) for i, (_, found) in enumerate(chunks) for run, row, d in found]
    parts = len(halves[0])
    rows = halves[0][0].shape[0]
    depth = sum(d for _, _, _, d in runs)
    width = min(w.shape[1] for w in weights)
    args = [me, *halves[0], *halves[1], *weights]
    specs = [SMEM] + [ANY] * (2 * parts + len(weights))
    if acc is not None:
        args.append(acc)
        specs.append(VMEM)
    if tail is not None:
        args += list(tail)
        specs += [VMEM] * 2
        out_shape = [jax.ShapeDtypeStruct((1, rows), jnp.float32)] * 2
        out_specs = [VMEM] * 2
    else:
        out_shape = jax.ShapeDtypeStruct((2 * rows, width), jnp.float32)
        out_specs = VMEM
    return pl.pallas_call(
        functools.partial(
            gemm_kernel,
            parts=parts,
            sources=len(weights),
            runs=tuple(runs),
            layout=layout,
            has_acc=acc is not None,
            final=tail is not None,
            tile=256,
        ),
        out_shape=out_shape,
        in_specs=specs,
        out_specs=out_specs,
        scratch_shapes=[
            pltpu.VMEM((2 * rows, depth), jnp.bfloat16),
            pltpu.VMEM((depth, width), jnp.bfloat16),
            pltpu.SemaphoreType.DMA((len(runs), 3)),
        ],
        cost_estimate=BRIEF,
        compiler_params=pltpu.CompilerParams(vmem_limit_bytes=VMEM_LIMIT),
    )(*args)


def both(attention, step_rows, norm_gain, head_weight, head_bias, class_weight, class_bias):
    z_count, x_count = lax.axis_size("batch"), lax.axis_size("mp")
    y_count = lax.axis_size("group")
    me = jnp.stack([lax.axis_index(a) for a in ("mp", "batch", "section", "group")]).astype(jnp.int32)
    swap = shift_pairs(2, 1)
    rows, features = step_rows.shape
    block, columns = head_weight.shape
    width = columns // 2
    share = block // y_count
    order = ring_order(z_count)
    ring = [(order[i], order[(i + 1) % z_count]) for i in range(z_count)]
    pieces, final_pieces = 2, 2
    layout = Layout(order, x_count, y_count, block, features, features // pieces)

    def forward(t):
        return lax.ppermute(t, "batch", ring)

    def over_group(t):
        return [lax.ppermute(t, "group", shift_pairs(y_count, k)) for k in range(1, y_count)]

    own = cut_share(me, head_weight, share, width, y_count, False, 0)
    given = [cut_share(me, head_weight, share, width, y_count, True, k) for k in range(y_count)]
    hop = [forward(own)]
    siblings = [lax.ppermute(g, "section", swap) for g in given]
    hop.append(forward(siblings[0]))
    power = row_power(step_rows, siblings[0])
    powers = [power] + [
        lax.ppermute(power, "mp", shift_pairs(x_count, k)) for k in range(1, x_count)
    ]
    mine = list(normalise(me, step_rows, powers, norm_gain, pieces))
    raw = [
        lax.ppermute(part, "mp", shift_pairs(x_count, k))
        for k in range(1, x_count)
        for part in mine
    ]
    theirs = [lax.ppermute(part, "section", swap) for part in mine]
    arrived = attention.send(attention.pack(siblings[0]))
    tail = [head_bias[None], jnp.pad(class_weight.T, ((0, 14), (0, 0)))]
    chunks = [(head_weight, [((0, False, None, 0), 0, block)])] + [
        (t, [((0, True, (y_count - k) % y_count, 0), 0, share)]) for k, t in enumerate(siblings)
    ]
    whole = merge(hop)
    waited = siblings[1:] + mine[:1]
    for h in range(1, z_count - 2):
        swapped = over_group(whole)
        chunks += [
            (t, carried(h, k, share, 0, 2 * share)) for k, t in enumerate([whole] + swapped)
        ]
        hop = forward(whole)
        if h < z_count - 3:
            (whole,) = after([hop], waited + swapped)
            waited = []
        else:
            whole = hop
    cuts = split(whole, final_pieces, waited + swapped + raw + theirs[:1] + [arrived])
    last = [forward(t) for t in cuts]
    swapped = over_group(whole)
    second = [
        (t, carried(z_count - 2, k, share, 0, 2 * share)) for k, t in enumerate([whole] + swapped)
    ]
    mine += raw
    theirs += [lax.ppermute(part, "section", swap) for part in mine[pieces:]]
    results = attention.answer(arrived)
    returned = attention.send(results)
    acc = gemm(me, layout, (mine, theirs), chunks)
    depth = 2 * share // final_pieces
    ends = []
    marks = [[results], [acc]] + [[] for _ in last[2:]]
    for j, t in enumerate(last):
        (t,) = after([t], marks[j])
        ends.append(
            [(u, carried(z_count - 1, k, share, j * depth, depth)) for k, u in enumerate([t] + over_group(t))]
        )
    acc = gemm(me, layout, (mine, theirs), second, acc)
    attended = attention.finish(returned)
    acc = gemm(me, layout, (mine, theirs), sum(ends[:-1], []) + ends[-1][:1], acc)
    kept, given = gemm(me, layout, (mine, theirs), ends[-1][1:], acc, tail)
    total = kept + lax.ppermute(given, "section", swap)
    for k in range(1, x_count):
        total = total + lax.ppermute(kept, "mp", shift_pairs(x_count, k))
        total = total + lax.ppermute(
            given,
            ("mp", "section"),
            [
                (i * 2 + c, ((i + k) % x_count) * 2 + 1 - c)
                for i in range(x_count)
                for c in range(2)
            ],
        )
    return attended, total[0] + (class_bias[1] - class_bias[0])


def judge_gathered(step_rows, norm_gain, head_weight, head_bias, class_weight, class_bias):
    full_rows = lax.all_gather(step_rows, "mp", axis=1, tiled=True)
    row_values = full_rows.astype(jnp.float32)
    power = jnp.mean(row_values * row_values, axis=1, keepdims=True)
    normed = (row_values * lax.rsqrt(power + 1e-06) * norm_gain).astype(jnp.bfloat16)
    projected = jnp.dot(
        normed,
        lax.all_gather(head_weight, ("batch", "section"), axis=0, tiled=True),
        preferred_element_type=jnp.float32,
    )
    hidden = jnp.maximum(projected + head_bias, 0.0).astype(jnp.bfloat16)
    partial_logits = jnp.dot(hidden, class_weight, preferred_element_type=jnp.float32)
    logits = lax.psum(partial_logits, "mp") + class_bias
    return logits[:, 1] - logits[:, 0]


def per_device(
    queries,
    new_keys,
    new_values,
    key_pages,
    value_pages,
    page_table,
    ancestry,
    lengths,
    step_rows,
    norm_gain,
    head_weight,
    head_bias,
    class_weight,
    class_bias,
):
    attention = Attention(
        queries, new_keys, new_values, key_pages, value_pages, page_table, ancestry, lengths
    )
    verifier = (step_rows, norm_gain, head_weight, head_bias, class_weight, class_bias)
    ring_fits = (
        4 <= lax.axis_size("batch") <= 8
        and lax.axis_size("mp") > 1
        and lax.axis_size("section") == 2
        and head_weight.shape[0] % (128 * lax.axis_size("group")) == 0
        and step_rows.shape[1] % (2 * head_weight.shape[0]) == 0
        and head_weight.shape[1] % 256 == 0
        and step_rows.shape[1] % head_weight.shape[0] == 0
    )
    if ring_fits:
        return both(attention, *verifier)
    arrived = attention.send(attention.pack(step_rows))
    returned = attention.send(attention.answer(arrived))
    return attention.finish(returned), judge_gathered(*verifier)


def solution(mesh):
    placed = (
        P("section", ("group", "batch"), "mp"),
        P("section", ("group", "batch"), "mp"),
        P("section", ("group", "batch"), "mp"),
        P("section", ("group", "batch"), None, "mp"),
        P("section", ("group", "batch"), None, "mp"),
        P(("group", "batch"), None),
        P("group"),
        P("group"),
        P(("group", "batch", "section"), "mp"),
        P(),
        P(("batch", "section"), "mp"),
        P("mp"),
        P("mp", None),
        P(),
    )
    return jax.shard_map(
        per_device,
        mesh=mesh,
        in_specs=placed,
        out_specs=(P("section", ("group", "batch"), "mp"), P(("group", "batch", "section"))),
        check_vma=False,
    )
```

```python
import functools

import jax
import jax.numpy as jnp
from jax import lax
from jax.experimental import pallas as pl
from jax.experimental.pallas import tpu as pltpu
from jax.sharding import PartitionSpec as P

HD = 128
VMEM_LIMIT = 24 << 20
BRIEF = pl.CostEstimate(flops=1, bytes_accessed=1, transcendentals=0)
ANY = pl.BlockSpec(memory_space=pltpu.HBM)
WAITED = pl.BlockSpec(memory_space=pl.ANY)
VMEM = pl.BlockSpec(memory_space=pltpu.VMEM)
SMEM = pl.BlockSpec(memory_space=pltpu.SMEM)


def in_hbm(arrays):
    return [pltpu.with_memory_space_constraint(a, pltpu.HBM) for a in arrays]


def pass_kernel(*refs):
    del refs


def after(passing, waited):
    many = len(passing)
    out = pl.pallas_call(
        pass_kernel,
        out_shape=[jax.ShapeDtypeStruct(a.shape, a.dtype) for a in passing],
        in_specs=[ANY] * many + [WAITED] * len(waited),
        out_specs=[ANY] * many,
        input_output_aliases={i: i for i in range(many)},
        cost_estimate=BRIEF,
        compiler_params=pltpu.CompilerParams(has_side_effects=True),
    )(*passing, *waited)
    return list(out)


def shift_pairs(count, step):
    return [(i, (i + step) % count) for i in range(count)]


def ring_order(count):
    return [0] + list(range(1, count, 2)) + [i for i in range(count - 1, 0, -1) if i % 2 == 0]


def pack_kernel(
    me, ancestry, lengths, queries, new_keys, new_values, waited,
    blobs, particle, length, pick, rows, request, seen, *, count, capacity
):
    del waited
    slots = queries.shape[0]
    at = 0
    for source in (queries, new_keys, new_values):
        for h in range(source.shape[1] // HD):
            rows[:, at, :] = source[:, h * HD : (h + 1) * HD].astype(jnp.float32)
            at += 1
    here = me[0]
    for k in range(count):
        seen[k] = 0

    def clear(i, carry):
        request[i] = 0
        particle[i] = 0
        length[i] = 1
        return carry

    lax.fori_loop(0, count * capacity, clear, 0)

    def ask(j, carry):
        owner = ancestry[here * slots + j] // slots
        rank = jnp.minimum(seen[owner], capacity - 1)
        seen[owner] = rank + 1
        pick[j] = owner * capacity + rank
        request[owner * capacity + rank] = j
        return carry

    lax.fori_loop(0, slots, ask, 0)

    def fill(i, carry):
        for k in range(count):
            blobs[k, i] = rows[request[k * capacity + i]].astype(jnp.bfloat16)
        return carry

    lax.fori_loop(0, capacity, fill, 0)
    for k in range(count):

        def answer(p, rank):
            ancestor = ancestry[k * slots + p]
            local = ancestor - here * slots
            match = (local >= 0) & (local < slots)
            at = k * capacity + jnp.minimum(rank, capacity - 1)

            @pl.when(match)
            def _():
                particle[at] = local
                length[at] = lengths[ancestor]

            return rank + match.astype(jnp.int32)

        lax.fori_loop(0, slots, answer, 0)


def pack(me, ancestry, lengths, queries, new_keys, new_values, waited, count, capacity):
    slots = queries.shape[0]
    depth = (queries.shape[1] + new_keys.shape[1] + new_values.shape[1]) // HD
    table = jax.ShapeDtypeStruct((count * capacity,), jnp.int32)
    out = pl.pallas_call(
        functools.partial(pack_kernel, count=count, capacity=capacity),
        out_shape=[jax.ShapeDtypeStruct((count, capacity, depth, HD), jnp.bfloat16)]
        + [table, table, jax.ShapeDtypeStruct((slots,), jnp.int32)],
        in_specs=[SMEM] * 3 + [VMEM] * 3 + [ANY],
        out_specs=[VMEM] + [SMEM] * 3,
        scratch_shapes=[
            pltpu.VMEM((slots, depth, HD), jnp.float32),
            pltpu.SMEM((count * capacity,), jnp.int32),
            pltpu.SMEM((count,), jnp.int32),
        ],
        cost_estimate=BRIEF,
        compiler_params=pltpu.CompilerParams(vmem_limit_bytes=VMEM_LIMIT),
    )(me, ancestry, lengths, queries, new_keys, new_values, waited)
    return out


def serve_kernel(
    particle, page_table, lengths, blobs, key_source, value_source, outs,
    key_pages, value_pages, sems, *, kv_local, unroll
):
    copies = [
        pltpu.make_async_copy(key_source, key_pages, sems.at[0]),
        pltpu.make_async_copy(value_source, value_pages, sems.at[1]),
    ]
    for c in copies:
        c.start()
    for c in copies:
        c.wait()
    count, capacity, heads = outs.shape[:3]
    group_size = heads // kv_local
    pages = page_table.shape[1]
    context = pages * key_pages.shape[1]
    score_scale = 1.0 / HD**0.5
    lanes_kv = lax.broadcasted_iota(jnp.int32, (heads, kv_local * HD), 1) // HD
    rows_kv = lax.broadcasted_iota(jnp.int32, (heads, kv_local * HD), 0) // group_size
    diagonal = lanes_kv == rows_kv
    positions = lax.broadcasted_iota(jnp.int32, (heads, context), 1)

    def spread(x):
        return jnp.broadcast_to(x[:, None, :], (kv_local, group_size, HD)).reshape(heads, HD)

    def together(k, slots):
        scores, own_products, own_values = [], [], []
        for slot in slots:
            at = k * capacity + slot
            rows = blobs[k, slot]
            query = rows[:heads].astype(jnp.float32)
            own_key = rows[heads : heads + kv_local].astype(jnp.float32)
            own_value = rows[heads + kv_local :].astype(jnp.float32)
            wide = jnp.concatenate([query] * kv_local, axis=1)
            wide = jnp.where(diagonal, wide, 0.0).astype(jnp.bfloat16)
            keys = jnp.concatenate(
                [key_pages[page_table[particle[at], i]] for i in range(pages)], axis=0
            )
            score = lax.dot_general(
                wide, keys, (((1,), (1,)), ((), ())), preferred_element_type=jnp.float32
            ) * score_scale
            scores.append(jnp.where(positions < lengths[at], score, -1e30))
            own_products.append(query * spread(own_key))
            own_values.append(spread(own_value))
        score = jnp.concatenate(scores, axis=0)
        top = jnp.max(score, axis=1, keepdims=True)
        weights = jnp.exp(score - top)
        own_score = jnp.sum(jnp.concatenate(own_products, axis=0), axis=1, keepdims=True) * score_scale
        own = jnp.exp(own_score - top)
        total = jnp.sum(weights, axis=1, keepdims=True) + own
        weights = weights.astype(jnp.bfloat16)
        for u, slot in enumerate(slots):
            at = k * capacity + slot
            mine = slice(u * heads, (u + 1) * heads)
            values = jnp.concatenate(
                [value_pages[page_table[particle[at], i]] for i in range(pages)], axis=0
            )
            mixed = jnp.dot(weights[mine], values, preferred_element_type=jnp.float32)
            numerator = jnp.concatenate(
                [
                    mixed[g * group_size : (g + 1) * group_size, g * HD : (g + 1) * HD]
                    for g in range(kv_local)
                ],
                axis=0,
            )
            result = (numerator + own[mine] * own_values[u]) / total[mine]
            outs[k, slot] = result.astype(jnp.bfloat16)

    def body(k, carry):
        for i in range(0, capacity, unroll):
            together(k, range(i, min(i + unroll, capacity)))
        return carry

    lax.fori_loop(0, count, body, 0)


def serve(particle, page_table, lengths, blobs, key_pages, value_pages):
    count, capacity, depth = blobs.shape[:3]
    kv_local = key_pages.shape[2] // HD
    heads = depth - 2 * kv_local
    return pl.pallas_call(
        functools.partial(serve_kernel, kv_local=kv_local, unroll=12),
        out_shape=jax.ShapeDtypeStruct((count, capacity, heads, HD), jnp.bfloat16),
        in_specs=[SMEM] * 3 + [VMEM] + [ANY] * 2,
        out_specs=VMEM,
        scratch_shapes=[
            pltpu.VMEM(key_pages.shape, key_pages.dtype),
            pltpu.VMEM(value_pages.shape, value_pages.dtype),
            pltpu.SemaphoreType.DMA((2,)),
        ],
        cost_estimate=BRIEF,
        compiler_params=pltpu.CompilerParams(vmem_limit_bytes=VMEM_LIMIT),
    )(particle, page_table, lengths, blobs, *in_hbm([key_pages, value_pages]))


def pick_kernel(pick, parts, *refs):
    out, rows = refs[-2:]
    slots = out.shape[0]
    capacity = parts.shape[1]

    def take(j, carry):
        rows[j] = parts[pick[j] // capacity, lax.rem(pick[j], capacity)].astype(jnp.float32)
        return carry

    lax.fori_loop(0, slots, take, 0)
    for h in range(rows.shape[1]):
        out[:, h * HD : (h + 1) * HD] = rows[:, h, :].astype(jnp.bfloat16)


def pick_up(pick, parts, waited):
    heads = parts.shape[2]
    slots = pick.shape[0]
    return pl.pallas_call(
        pick_kernel,
        out_shape=jax.ShapeDtypeStruct((slots, heads * HD), jnp.bfloat16),
        in_specs=[SMEM, VMEM] + [WAITED] * len(waited),
        out_specs=VMEM,
        scratch_shapes=[pltpu.VMEM((slots, heads, HD), jnp.float32)],
        cost_estimate=BRIEF,
        compiler_params=pltpu.CompilerParams(vmem_limit_bytes=VMEM_LIMIT),
    )(pick, parts, *waited)


class Attention:
    def __init__(self, queries, new_keys, new_values, key_pages, value_pages, page_table, ancestry, lengths):
        self.count = lax.axis_size("batch")
        slots = page_table.shape[0]
        self.capacity = max(2, (2 * slots + self.count - 1) // self.count)
        self.rows = (ancestry, lengths, queries[0], new_keys[0], new_values[0])
        self.page_table, self.keys, self.values = page_table, key_pages[0], value_pages[0]

    def pack(self, waited):
        me = lax.axis_index("batch").reshape(1).astype(jnp.int32)
        blobs, self.particle, self.lengths, self.pick = pack(
            me, *self.rows, waited, self.count, self.capacity
        )
        return blobs

    def send(self, blobs):
        return lax.all_to_all(blobs, "batch", split_axis=0, concat_axis=0, tiled=True)

    def answer(self, arrived):
        return serve(
            self.particle, self.page_table, self.lengths, arrived, self.keys, self.values
        )

    def finish(self, returned, *waited):
        return pick_up(self.pick, returned, waited)[None]


def cut_kernel(me, weight, out, sem, *, back, other, y_count):
    share, width = out.shape
    core = 1 - me[2] if other else me[2]
    rows = pl.ds(pl.multiple_of(lax.rem(me[3] + back, y_count) * share, share), share)
    lanes = pl.ds(pl.multiple_of(core * width, width), width)
    copy = pltpu.make_async_copy(weight.at[rows, lanes], out, sem)
    copy.start()
    copy.wait()


def cut_share(me, weight, share, width, y_count, other, back):
    return pl.pallas_call(
        functools.partial(cut_kernel, back=back, other=other, y_count=y_count),
        out_shape=jax.ShapeDtypeStruct((share, width), weight.dtype),
        in_specs=[SMEM, ANY],
        out_specs=VMEM,
        scratch_shapes=[pltpu.SemaphoreType.DMA],
        cost_estimate=BRIEF,
        compiler_params=pltpu.CompilerParams(vmem_limit_bytes=VMEM_LIMIT),
    )(me, weight)


def power_kernel(x, waited, out):
    del waited
    rows, features = x.shape

    def body(i, carry):
        at = pl.ds(pl.multiple_of(i * HD, HD), HD)
        total = jnp.zeros((HD, HD), jnp.float32)
        for j in range(features // HD):
            v = x[at, j * HD : (j + 1) * HD].astype(jnp.float32)
            total = total + v * v
        out[pl.ds(i, 1), :] = jnp.sum(total.T, axis=0, keepdims=True)
        return carry

    lax.fori_loop(0, rows // HD, body, 0)


def row_power(x, waited):
    return pl.pallas_call(
        power_kernel,
        out_shape=jax.ShapeDtypeStruct((x.shape[0] // HD, HD), jnp.float32),
        in_specs=[VMEM, ANY],
        out_specs=VMEM,
        cost_estimate=BRIEF,
        compiler_params=pltpu.CompilerParams(vmem_limit_bytes=VMEM_LIMIT),
    )(x, waited)


def norm_kernel(me, x, *refs, total, count):
    powers, (gain, _, *outs) = refs[:count], refs[count:]
    rows, features = x.shape
    part = outs[0].shape[1]
    power = powers[0][...]
    for p in powers[1:]:
        power = power + p[...]
    scale = lax.rsqrt(power / total + 1e-06)
    start = me[0] * features

    for i in range(rows // HD):
        column = jnp.broadcast_to(scale[i : i + 1, :], (HD, HD)).T
        for j in range(features // HD):
            at = (slice(i * HD, (i + 1) * HD), slice(j * HD, (j + 1) * HD))
            lanes = pl.ds(pl.multiple_of(start + j * HD, HD), HD)
            value = (x[at].astype(jnp.float32) * column * gain[:, lanes]).astype(jnp.bfloat16)
            first = j * HD % part
            outs[j * HD // part][at[0], first : first + HD] = value


def normalise(me, x, powers, gain, pieces, waited):
    shape = (x.shape[0], x.shape[1] // pieces)
    return pl.pallas_call(
        functools.partial(
            norm_kernel, total=gain.shape[0], count=len(powers)
        ),
        out_shape=[jax.ShapeDtypeStruct(shape, jnp.bfloat16)] * pieces,
        in_specs=[SMEM] + [VMEM] * (2 + len(powers)) + [WAITED],
        out_specs=[VMEM] * pieces,
        cost_estimate=BRIEF,
        compiler_params=pltpu.CompilerParams(vmem_limit_bytes=VMEM_LIMIT),
    )(me, x, *powers, gain[None], waited)


class Layout:
    def __init__(self, order, x_count, y_count, block, features, part):
        self.order, self.x_count, self.y_count = order, x_count, y_count
        self.block, self.features, self.part = block, features, part
        self.share = block // y_count

    def place(self, me, run):
        hops, other, back, row = run
        x, z, s, y = me[0], me[1], me[2], me[3]
        count = len(self.order)
        owner = 0
        for i, at in enumerate(self.order):
            owner = owner + jnp.where(z == at, self.order[(i - hops) % count], 0)
        core = 1 - s if other else s
        feature = (2 * owner + core) * self.block + row
        if back is not None:
            group = y - back
            feature = feature + jnp.where(group < 0, group + self.y_count, group) * self.share
        per_device = self.features // self.part
        index = 0
        for i in range(1, self.x_count * per_device):
            index = index + (feature >= i * self.part).astype(jnp.int32)
        offset = feature - index * self.part
        index = index - x * per_device
        return self.rotated(index, per_device, self.x_count * per_device), offset

    def rotated(self, index, per_device, blocks):
        index = jnp.where(index < 0, index + blocks, index)
        place = 0
        for ahead in range(self.x_count):
            back = (self.x_count - ahead) % self.x_count
            inside = (index >= ahead * per_device) & (index < (ahead + 1) * per_device)
            place = place + jnp.where(inside, index + (back - ahead) * per_device, 0)
        return place


def carried(hops, back, share, first, count):
    runs = []
    for other in (False, True):
        low, high = max(first, other * share), min(first + count, (other + 1) * share)
        if low < high:
            runs.append(((hops, other, back, low - other * share), low - first, high - low))
    return runs


def merge_kernel(*refs):
    *sources, out = refs
    at = 0
    for source in sources:
        out[at : at + source.shape[0]] = source[...]
        at += source.shape[0]


def merge(sources):
    rows = sum(a.shape[0] for a in sources)
    return pl.pallas_call(
        merge_kernel,
        out_shape=jax.ShapeDtypeStruct((rows,) + sources[0].shape[1:], sources[0].dtype),
        in_specs=[VMEM] * len(sources),
        out_specs=VMEM,
        cost_estimate=BRIEF,
        compiler_params=pltpu.CompilerParams(vmem_limit_bytes=VMEM_LIMIT),
    )(*sources)


def split_kernel(source, *refs, pieces):
    outs, sems = refs[-pieces - 1 : -1], refs[-1]
    rows = outs[0].shape[0]
    copies = [
        pltpu.make_async_copy(source.at[pl.ds(i * rows, rows)], out, sems.at[i])
        for i, out in enumerate(outs)
    ]
    for c in copies:
        c.start()
    for c in copies:
        c.wait()


def split(source, pieces, waited):
    shape = (source.shape[0] // pieces,) + source.shape[1:]
    return pl.pallas_call(
        functools.partial(split_kernel, pieces=pieces),
        out_shape=[jax.ShapeDtypeStruct(shape, source.dtype)] * pieces,
        in_specs=[ANY] + [WAITED] * len(waited),
        out_specs=[VMEM] * pieces,
        scratch_shapes=[pltpu.SemaphoreType.DMA((pieces,))],
        cost_estimate=BRIEF,
        compiler_params=pltpu.CompilerParams(vmem_limit_bytes=VMEM_LIMIT),
    )(source, *waited)


def gemm_kernel(me, *refs, parts, sources, runs, layout, has_acc, final, tile):
    refs = list(refs)
    halves = [refs[:parts], refs[parts : 2 * parts]]
    del refs[: 2 * parts]
    weights = refs[:sources]
    del refs[:sources]
    acc_in = refs.pop(0) if has_acc else None
    bias = class_weight = None
    if final:
        bias, class_weight = refs[:2]
        del refs[:2]
        outs = [refs.pop(0), refs.pop(0)]
    else:
        out, token = refs.pop(0), refs.pop(0)
        token[...] = jnp.zeros_like(token)
    x_v, w_v, sems = refs
    rows = halves[0][0].shape[0]
    width = w_v.shape[1]
    depths = [depth for _, _, _, depth in runs]
    starts = [sum(depths[:i]) for i in range(len(depths))]
    columns = pl.ds(pl.multiple_of(me[2] * width, width), width)

    if final:
        classes = class_weight[1:2, columns] - class_weight[0:1, columns]

    def weight_copy(i):
        _, which, row, depth = runs[i]
        source = weights[which]
        lanes = slice(None) if source.shape[1] == width else columns
        source = source.at[row : row + depth, lanes]
        return pltpu.make_async_copy(source, w_v.at[pl.ds(starts[i], depths[i])], sems.at[i, 2])

    def row_copy(i, r, p, offset):
        return pltpu.make_async_copy(
            halves[r][p].at[:, pl.ds(offset, depths[i])],
            x_v.at[pl.ds(r * rows, rows), pl.ds(starts[i], depths[i])],
            sems.at[i, r],
        )

    for i, (run, _, _, _) in enumerate(runs):
        weight_copy(i).start()
        part, offset = layout.place(me, run)
        offset = pl.multiple_of(offset, HD)
        for r in range(2):
            for p in range(parts):
                pl.when(part == p)(row_copy(i, r, p, offset).start)
    groups = []
    i = 0
    while i < len(runs):
        j, depth = i, 0
        while j < len(runs) and depth < 1024:
            depth += depths[j]
            j += 1
        groups.append((i, j))
        i = j
    for g, (first, last) in enumerate(groups):
        for i in range(first, last):
            weight_copy(i).wait()
            for r in range(2):
                row_copy(i, r, 0, 0).wait()
        k0 = starts[first]
        k1 = starts[last - 1] + depths[last - 1]

        def body(m, carry, target=None, base=0):
            at = pl.ds(pl.multiple_of(base + m * tile, tile), tile)
            product = jnp.dot(x_v[at, k0:k1], w_v[k0:k1, :], preferred_element_type=jnp.float32)
            if g > 0:
                total = out[at, :] + product
            elif has_acc:
                total = acc_in[at, :] + product
            else:
                total = product
            if target is not None:
                hidden = jnp.maximum(total + bias[:, columns], 0.0).astype(jnp.bfloat16)
                weighed = hidden.astype(jnp.float32) * classes
                folded = weighed[:, :HD]
                for j in range(1, width // HD):
                    folded = folded + weighed[:, j * HD : (j + 1) * HD]
                for j in range(tile // HD):
                    turned = folded[j * HD : (j + 1) * HD, :].T
                    lanes = pl.ds(pl.multiple_of(m * tile + j * HD, HD), HD)
                    target[:, lanes] = jnp.sum(turned, axis=0, keepdims=True)
            else:
                out[at, :] = total
            return carry

        if final:
            for r in range(2):
                lax.fori_loop(
                    0, rows // tile, functools.partial(body, target=outs[r], base=r * rows), 0
                )
        else:
            lax.fori_loop(0, 2 * rows // tile, body, 0)


def gemm(me, layout, halves, chunks, acc=None, tail=None):
    weights = [w for w, _ in chunks]
    runs = [(run, i, row, d) for i, (_, found) in enumerate(chunks) for run, row, d in found]
    parts = len(halves[0])
    rows = halves[0][0].shape[0]
    depth = sum(d for _, _, _, d in runs)
    width = min(w.shape[1] for w in weights)
    args = [me, *in_hbm([*halves[0], *halves[1]]), *weights]
    specs = [SMEM] + [ANY] * (2 * parts + len(weights))
    if acc is not None:
        args.append(pltpu.with_memory_space_constraint(acc, pltpu.VMEM))
        specs.append(VMEM)
    if tail is not None:
        args += list(tail)
        specs += [VMEM] * 2
        out_shape = [jax.ShapeDtypeStruct((1, rows), jnp.float32)] * 2
        out_specs = [VMEM] * 2
    else:
        out_shape = [
            pltpu.VMEM((2 * rows, width), jnp.float32),
            jax.ShapeDtypeStruct((8, HD), jnp.float32),
        ]
        out_specs = [VMEM] * 2
    return pl.pallas_call(
        functools.partial(
            gemm_kernel,
            parts=parts,
            sources=len(weights),
            runs=tuple(runs),
            layout=layout,
            has_acc=acc is not None,
            final=tail is not None,
            tile=256,
        ),
        out_shape=out_shape,
        in_specs=specs,
        out_specs=out_specs,
        scratch_shapes=[
            pltpu.VMEM((2 * rows, depth), jnp.bfloat16),
            pltpu.VMEM((depth, width), jnp.bfloat16),
            pltpu.SemaphoreType.DMA((len(runs), 3)),
        ],
        cost_estimate=BRIEF,
        compiler_params=pltpu.CompilerParams(vmem_limit_bytes=VMEM_LIMIT),
    )(*args)


def both(attention, step_rows, norm_gain, head_weight, head_bias, class_weight, class_bias):
    z_count, x_count = lax.axis_size("batch"), lax.axis_size("mp")
    y_count = lax.axis_size("group")
    me = jnp.stack([lax.axis_index(a) for a in ("mp", "batch", "section", "group")]).astype(jnp.int32)
    swap = shift_pairs(2, 1)
    rows, features = step_rows.shape
    block, columns = head_weight.shape
    width = columns // 2
    share = block // y_count
    order = ring_order(z_count)
    ring = [(order[i], order[(i + 1) % z_count]) for i in range(z_count)]
    pieces, final_pieces = 2, 2
    layout = Layout(order, x_count, y_count, block, features, features // pieces)

    def forward(t):
        return lax.ppermute(t, "batch", ring)

    def over_group(t):
        return [lax.ppermute(t, "group", shift_pairs(y_count, k)) for k in range(1, y_count)]

    own = cut_share(me, head_weight, share, width, y_count, False, 0)
    given = [cut_share(me, head_weight, share, width, y_count, True, k) for k in range(y_count)]
    siblings = [lax.ppermute(g, "section", swap) for g in given]
    merged = merge([own, siblings[0]])
    whole = forward(merged)
    power = row_power(step_rows, own)
    powers = [power] + [
        lax.ppermute(power, "mp", shift_pairs(x_count, k)) for k in range(1, x_count)
    ]
    mine = list(normalise(me, step_rows, powers, norm_gain, pieces, merged))
    raw = [
        lax.ppermute(part, "mp", shift_pairs(x_count, k))
        for k in range(1, x_count)
        for part in mine
    ]
    theirs = [lax.ppermute(part, "section", swap) for part in mine]
    blobs = attention.pack(siblings[0])
    arrived = attention.send(blobs)
    tail = [head_bias[None], class_weight.T.astype(jnp.float32)]
    chunks = [(head_weight, [((0, False, None, 0), 0, block)])] + [
        (t, [((0, True, (y_count - k) % y_count, 0), 0, share)]) for k, t in enumerate(siblings)
    ]
    waited = siblings[1:] + theirs
    for h in range(1, z_count - 2):
        if h > 1:
            whole = forward(whole)
        swapped = over_group(whole)
        chunks += [
            (t, carried(h, k, share, 0, 2 * share)) for k, t in enumerate([whole] + swapped)
        ]
        if h < z_count - 3:
            (whole,) = after([whole], waited)
            waited = swapped
    cuts = [forward(t) for t in split(whole, final_pieces, waited)]
    depth = 2 * share // final_pieces
    results = attention.answer(arrived)
    marks = [[blobs] + swapped + raw, [results]]
    second, last, travelled = [], [], []
    for j, t in enumerate(cuts):
        (t,) = after([t], marks[j])
        last.append(forward(t))
        swapped = over_group(t)
        if j + 1 < final_pieces:
            marks[j + 1] += swapped
        second += [
            (u, carried(z_count - 2, k, share, j * depth, depth))
            for k, u in enumerate([t] + swapped)
        ]
        travelled.append(t)
    for i, part in enumerate(raw):
        (part,) = after([part], [travelled[0]])
        mine.append(part)
        theirs.append(lax.ppermute(part, "section", swap))
    returned = attention.send(results)
    acc, early = gemm(me, layout, (mine, theirs), chunks)
    ends = []
    marks = [[], [early]]
    for j, t in enumerate(last):
        (t,) = after([t], marks[j])
        ends.append(
            [
                (u, carried(z_count - 1, k, share, j * depth, depth))
                for k, u in enumerate([t] + over_group(t))
            ]
        )
    attended = attention.finish(returned, early)
    acc, _ = gemm(me, layout, (mine, theirs), second + sum(ends[:-1], []) + ends[-1][:1], acc)
    kept, given = gemm(me, layout, (mine, theirs), ends[-1][1:], acc, tail)
    total = kept + lax.ppermute(given, "section", swap)
    for k in range(1, x_count):
        total = total + lax.ppermute(kept, "mp", shift_pairs(x_count, k))
        total = total + lax.ppermute(
            given,
            ("mp", "section"),
            [
                (i * 2 + c, ((i + k) % x_count) * 2 + 1 - c)
                for i in range(x_count)
                for c in range(2)
            ],
        )
    return attended, total[0] + (class_bias[1] - class_bias[0])


def judge_gathered(step_rows, norm_gain, head_weight, head_bias, class_weight, class_bias):
    full_rows = lax.all_gather(step_rows, "mp", axis=1, tiled=True)
    row_values = full_rows.astype(jnp.float32)
    power = jnp.mean(row_values * row_values, axis=1, keepdims=True)
    normed = (row_values * lax.rsqrt(power + 1e-06) * norm_gain).astype(jnp.bfloat16)
    projected = jnp.dot(
        normed,
        lax.all_gather(head_weight, ("batch", "section"), axis=0, tiled=True),
        preferred_element_type=jnp.float32,
    )
    hidden = jnp.maximum(projected + head_bias, 0.0).astype(jnp.bfloat16)
    partial_logits = jnp.dot(hidden, class_weight, preferred_element_type=jnp.float32)
    logits = lax.psum(partial_logits, "mp") + class_bias
    return logits[:, 1] - logits[:, 0]


def per_device(
    queries,
    new_keys,
    new_values,
    key_pages,
    value_pages,
    page_table,
    ancestry,
    lengths,
    step_rows,
    norm_gain,
    head_weight,
    head_bias,
    class_weight,
    class_bias,
):
    attention = Attention(
        queries, new_keys, new_values, key_pages, value_pages, page_table, ancestry, lengths
    )
    verifier = (step_rows, norm_gain, head_weight, head_bias, class_weight, class_bias)
    ring_fits = (
        4 <= lax.axis_size("batch") <= 8
        and lax.axis_size("mp") > 1
        and lax.axis_size("section") == 2
        and head_weight.shape[0] % (128 * lax.axis_size("group")) == 0
        and step_rows.shape[1] % (2 * head_weight.shape[0]) == 0
        and head_weight.shape[1] % 256 == 0
        and step_rows.shape[1] % head_weight.shape[0] == 0
    )
    if ring_fits:
        return both(attention, *verifier)
    arrived = attention.send(attention.pack(step_rows))
    returned = attention.send(attention.answer(arrived))
    return attention.finish(returned), judge_gathered(*verifier)


def solution(mesh):
    placed = (
        P("section", ("group", "batch"), "mp"),
        P("section", ("group", "batch"), "mp"),
        P("section", ("group", "batch"), "mp"),
        P("section", ("group", "batch"), None, "mp"),
        P("section", ("group", "batch"), None, "mp"),
        P(("group", "batch"), None),
        P("group"),
        P("group"),
        P(("group", "batch", "section"), "mp"),
        P(),
        P(("batch", "section"), "mp"),
        P("mp"),
        P("mp", None),
        P(),
    )
    return jax.shard_map(
        per_device,
        mesh=mesh,
        in_specs=placed,
        out_specs=(P("section", ("group", "batch"), "mp"), P(("group", "batch", "section"))),
        check_vma=False,
    )
```

```python
import functools

import jax
import jax.numpy as jnp
from jax import lax
from jax.experimental import pallas as pl
from jax.experimental.pallas import tpu as pltpu
from jax.sharding import PartitionSpec as P

HD = 128
VMEM_LIMIT = 24 << 20
BRIEF = pl.CostEstimate(flops=1, bytes_accessed=1, transcendentals=0)
ANY = pl.BlockSpec(memory_space=pltpu.HBM)
WAITED = pl.BlockSpec(memory_space=pl.ANY)
VMEM = pl.BlockSpec(memory_space=pltpu.VMEM)
SMEM = pl.BlockSpec(memory_space=pltpu.SMEM)


def in_hbm(arrays):
    return [pltpu.with_memory_space_constraint(a, pltpu.HBM) for a in arrays]


def pass_kernel(*refs):
    del refs


def after(passing, waited):
    many = len(passing)
    out = pl.pallas_call(
        pass_kernel,
        out_shape=[jax.ShapeDtypeStruct(a.shape, a.dtype) for a in passing],
        in_specs=[ANY] * many + [WAITED] * len(waited),
        out_specs=[ANY] * many,
        input_output_aliases={i: i for i in range(many)},
        cost_estimate=BRIEF,
        compiler_params=pltpu.CompilerParams(has_side_effects=True),
    )(*passing, *waited)
    return list(out)


def shift_pairs(count, step):
    return [(i, (i + step) % count) for i in range(count)]


def ring_order(count):
    return [0] + list(range(1, count, 2)) + [i for i in range(count - 1, 0, -1) if i % 2 == 0]


def pack_kernel(
    me, ancestry, lengths, queries, new_keys, new_values, waited,
    blobs, particle, length, pick, rows, request, seen, *, count, capacity
):
    del waited
    slots = queries.shape[0]
    at = 0
    for source in (queries, new_keys, new_values):
        for h in range(source.shape[1] // HD):
            rows[:, at, :] = source[:, h * HD : (h + 1) * HD].astype(jnp.float32)
            at += 1
    here = me[0]
    for k in range(count):
        seen[k] = 0

    def clear(i, carry):
        request[i] = 0
        particle[i] = 0
        length[i] = 1
        return carry

    lax.fori_loop(0, count * capacity, clear, 0)

    def ask(j, carry):
        owner = ancestry[here * slots + j] // slots
        rank = jnp.minimum(seen[owner], capacity - 1)
        seen[owner] = rank + 1
        pick[j] = owner * capacity + rank
        request[owner * capacity + rank] = j
        return carry

    lax.fori_loop(0, slots, ask, 0)

    def fill(i, carry):
        for k in range(count):
            blobs[k, i] = rows[request[k * capacity + i]].astype(jnp.bfloat16)
        return carry

    lax.fori_loop(0, capacity, fill, 0)
    for k in range(count):

        def answer(p, rank):
            ancestor = ancestry[k * slots + p]
            local = ancestor - here * slots
            match = (local >= 0) & (local < slots)
            at = k * capacity + jnp.minimum(rank, capacity - 1)

            @pl.when(match)
            def _():
                particle[at] = local
                length[at] = lengths[ancestor]

            return rank + match.astype(jnp.int32)

        lax.fori_loop(0, slots, answer, 0)


def pack(me, ancestry, lengths, queries, new_keys, new_values, waited, count, capacity):
    slots = queries.shape[0]
    depth = (queries.shape[1] + new_keys.shape[1] + new_values.shape[1]) // HD
    table = jax.ShapeDtypeStruct((count * capacity,), jnp.int32)
    out = pl.pallas_call(
        functools.partial(pack_kernel, count=count, capacity=capacity),
        out_shape=[jax.ShapeDtypeStruct((count, capacity, depth, HD), jnp.bfloat16)]
        + [table, table, jax.ShapeDtypeStruct((slots,), jnp.int32)],
        in_specs=[SMEM] * 3 + [VMEM] * 3 + [ANY],
        out_specs=[VMEM] + [SMEM] * 3,
        scratch_shapes=[
            pltpu.VMEM((slots, depth, HD), jnp.float32),
            pltpu.SMEM((count * capacity,), jnp.int32),
            pltpu.SMEM((count,), jnp.int32),
        ],
        cost_estimate=BRIEF,
        compiler_params=pltpu.CompilerParams(vmem_limit_bytes=VMEM_LIMIT),
    )(me, ancestry, lengths, queries, new_keys, new_values, waited)
    return out


def serve_kernel(
    particle, page_table, lengths, blobs, key_source, value_source, outs,
    key_pages, value_pages, sems, *, kv_local, unroll
):
    copies = [
        pltpu.make_async_copy(key_source, key_pages, sems.at[0]),
        pltpu.make_async_copy(value_source, value_pages, sems.at[1]),
    ]
    for c in copies:
        c.start()
    for c in copies:
        c.wait()
    count, capacity, heads = outs.shape[:3]
    group_size = heads // kv_local
    pages = page_table.shape[1]
    context = pages * key_pages.shape[1]
    score_scale = 1.0 / HD**0.5
    lanes_kv = lax.broadcasted_iota(jnp.int32, (heads, kv_local * HD), 1) // HD
    rows_kv = lax.broadcasted_iota(jnp.int32, (heads, kv_local * HD), 0) // group_size
    diagonal = lanes_kv == rows_kv
    positions = lax.broadcasted_iota(jnp.int32, (heads, context), 1)

    def spread(x):
        return jnp.broadcast_to(x[:, None, :], (kv_local, group_size, HD)).reshape(heads, HD)

    def together(k, slots):
        scores, own_products, own_values = [], [], []
        for slot in slots:
            at = k * capacity + slot
            rows = blobs[k, slot]
            query = rows[:heads].astype(jnp.float32)
            own_key = rows[heads : heads + kv_local].astype(jnp.float32)
            own_value = rows[heads + kv_local :].astype(jnp.float32)
            wide = jnp.concatenate([query] * kv_local, axis=1)
            wide = jnp.where(diagonal, wide, 0.0).astype(jnp.bfloat16)
            keys = jnp.concatenate(
                [key_pages[page_table[particle[at], i]] for i in range(pages)], axis=0
            )
            score = lax.dot_general(
                wide, keys, (((1,), (1,)), ((), ())), preferred_element_type=jnp.float32
            ) * score_scale
            scores.append(jnp.where(positions < lengths[at], score, -1e30))
            own_products.append(query * spread(own_key))
            own_values.append(spread(own_value))
        score = jnp.concatenate(scores, axis=0)
        top = jnp.max(score, axis=1, keepdims=True)
        weights = jnp.exp(score - top)
        own_score = jnp.sum(jnp.concatenate(own_products, axis=0), axis=1, keepdims=True) * score_scale
        own = jnp.exp(own_score - top)
        total = jnp.sum(weights, axis=1, keepdims=True) + own
        weights = weights.astype(jnp.bfloat16)
        for u, slot in enumerate(slots):
            at = k * capacity + slot
            mine = slice(u * heads, (u + 1) * heads)
            values = jnp.concatenate(
                [value_pages[page_table[particle[at], i]] for i in range(pages)], axis=0
            )
            mixed = jnp.dot(weights[mine], values, preferred_element_type=jnp.float32)
            numerator = jnp.concatenate(
                [
                    mixed[g * group_size : (g + 1) * group_size, g * HD : (g + 1) * HD]
                    for g in range(kv_local)
                ],
                axis=0,
            )
            result = (numerator + own[mine] * own_values[u]) / total[mine]
            outs[k, slot] = result.astype(jnp.bfloat16)

    def body(k, carry):
        for i in range(0, capacity, unroll):
            together(k, range(i, min(i + unroll, capacity)))
        return carry

    lax.fori_loop(0, count, body, 0)


def serve(particle, page_table, lengths, blobs, key_pages, value_pages):
    count, capacity, depth = blobs.shape[:3]
    kv_local = key_pages.shape[2] // HD
    heads = depth - 2 * kv_local
    return pl.pallas_call(
        functools.partial(serve_kernel, kv_local=kv_local, unroll=12),
        out_shape=jax.ShapeDtypeStruct((count, capacity, heads, HD), jnp.bfloat16),
        in_specs=[SMEM] * 3 + [VMEM] + [ANY] * 2,
        out_specs=VMEM,
        scratch_shapes=[
            pltpu.VMEM(key_pages.shape, key_pages.dtype),
            pltpu.VMEM(value_pages.shape, value_pages.dtype),
            pltpu.SemaphoreType.DMA((2,)),
        ],
        cost_estimate=BRIEF,
        compiler_params=pltpu.CompilerParams(vmem_limit_bytes=VMEM_LIMIT),
    )(particle, page_table, lengths, blobs, *in_hbm([key_pages, value_pages]))


def pick_kernel(pick, parts, *refs):
    out, rows = refs[-2:]
    slots = out.shape[0]
    capacity = parts.shape[1]

    def take(j, carry):
        rows[j] = parts[pick[j] // capacity, lax.rem(pick[j], capacity)].astype(jnp.float32)
        return carry

    lax.fori_loop(0, slots, take, 0)
    for h in range(rows.shape[1]):
        out[:, h * HD : (h + 1) * HD] = rows[:, h, :].astype(jnp.bfloat16)


def pick_up(pick, parts, waited):
    heads = parts.shape[2]
    slots = pick.shape[0]
    return pl.pallas_call(
        pick_kernel,
        out_shape=jax.ShapeDtypeStruct((slots, heads * HD), jnp.bfloat16),
        in_specs=[SMEM, VMEM] + [WAITED] * len(waited),
        out_specs=VMEM,
        scratch_shapes=[pltpu.VMEM((slots, heads, HD), jnp.float32)],
        cost_estimate=BRIEF,
        compiler_params=pltpu.CompilerParams(vmem_limit_bytes=VMEM_LIMIT),
    )(pick, parts, *waited)


class Attention:
    def __init__(self, queries, new_keys, new_values, key_pages, value_pages, page_table, ancestry, lengths):
        self.count = lax.axis_size("batch")
        slots = page_table.shape[0]
        self.capacity = max(2, (2 * slots + self.count - 1) // self.count)
        self.rows = (ancestry, lengths, queries[0], new_keys[0], new_values[0])
        self.page_table, self.keys, self.values = page_table, key_pages[0], value_pages[0]

    def pack(self, waited):
        me = lax.axis_index("batch").reshape(1).astype(jnp.int32)
        blobs, self.particle, self.lengths, self.pick = pack(
            me, *self.rows, waited, self.count, self.capacity
        )
        return blobs

    def send(self, blobs):
        return lax.all_to_all(blobs, "batch", split_axis=0, concat_axis=0, tiled=True)

    def answer(self, arrived):
        return serve(
            self.particle, self.page_table, self.lengths, arrived, self.keys, self.values
        )

    def finish(self, returned, *waited):
        return pick_up(self.pick, returned, waited)[None]


def cut_kernel(me, weight, out, sem, *, back, other, y_count):
    share, width = out.shape
    core = 1 - me[2] if other else me[2]
    rows = pl.ds(pl.multiple_of(lax.rem(me[3] + back, y_count) * share, share), share)
    lanes = pl.ds(pl.multiple_of(core * width, width), width)
    copy = pltpu.make_async_copy(weight.at[rows, lanes], out, sem)
    copy.start()
    copy.wait()


def cut_share(me, weight, share, width, y_count, other, back):
    return pl.pallas_call(
        functools.partial(cut_kernel, back=back, other=other, y_count=y_count),
        out_shape=jax.ShapeDtypeStruct((share, width), weight.dtype),
        in_specs=[SMEM, ANY],
        out_specs=VMEM,
        scratch_shapes=[pltpu.SemaphoreType.DMA],
        cost_estimate=BRIEF,
        compiler_params=pltpu.CompilerParams(vmem_limit_bytes=VMEM_LIMIT),
    )(me, weight)


def power_kernel(x, waited, out):
    del waited
    rows, features = x.shape

    def body(i, carry):
        at = pl.ds(pl.multiple_of(i * HD, HD), HD)
        total = jnp.zeros((HD, HD), jnp.float32)
        for j in range(features // HD):
            v = x[at, j * HD : (j + 1) * HD].astype(jnp.float32)
            total = total + v * v
        out[pl.ds(i, 1), :] = jnp.sum(total.T, axis=0, keepdims=True)
        return carry

    lax.fori_loop(0, rows // HD, body, 0)


def row_power(x, waited):
    return pl.pallas_call(
        power_kernel,
        out_shape=jax.ShapeDtypeStruct((x.shape[0] // HD, HD), jnp.float32),
        in_specs=[VMEM, ANY],
        out_specs=VMEM,
        cost_estimate=BRIEF,
        compiler_params=pltpu.CompilerParams(vmem_limit_bytes=VMEM_LIMIT),
    )(x, waited)


def norm_kernel(me, x, *refs, total, count):
    powers, (gain, _, *outs) = refs[:count], refs[count:]
    rows, features = x.shape
    part = outs[0].shape[1]
    power = powers[0][...]
    for p in powers[1:]:
        power = power + p[...]
    scale = lax.rsqrt(power / total + 1e-06)
    start = me[0] * features

    for i in range(rows // HD):
        column = jnp.broadcast_to(scale[i : i + 1, :], (HD, HD)).T
        for j in range(features // HD):
            at = (slice(i * HD, (i + 1) * HD), slice(j * HD, (j + 1) * HD))
            lanes = pl.ds(pl.multiple_of(start + j * HD, HD), HD)
            value = (x[at].astype(jnp.float32) * column * gain[:, lanes]).astype(jnp.bfloat16)
            first = j * HD % part
            outs[j * HD // part][at[0], first : first + HD] = value


def normalise(me, x, powers, gain, pieces, waited):
    shape = (x.shape[0], x.shape[1] // pieces)
    return pl.pallas_call(
        functools.partial(
            norm_kernel, total=gain.shape[0], count=len(powers)
        ),
        out_shape=[jax.ShapeDtypeStruct(shape, jnp.bfloat16)] * pieces,
        in_specs=[SMEM] + [VMEM] * (2 + len(powers)) + [WAITED],
        out_specs=[VMEM] * pieces,
        cost_estimate=BRIEF,
        compiler_params=pltpu.CompilerParams(vmem_limit_bytes=VMEM_LIMIT),
    )(me, x, *powers, gain[None], waited)


class Layout:
    def __init__(self, order, x_count, y_count, block, features, part):
        self.order, self.x_count, self.y_count = order, x_count, y_count
        self.block, self.features, self.part = block, features, part
        self.share = block // y_count

    def place(self, me, run):
        hops, other, back, row = run
        x, z, s, y = me[0], me[1], me[2], me[3]
        count = len(self.order)
        owner = 0
        for i, at in enumerate(self.order):
            owner = owner + jnp.where(z == at, self.order[(i - hops) % count], 0)
        core = 1 - s if other else s
        feature = (2 * owner + core) * self.block + row
        if back is not None:
            group = y - back
            feature = feature + jnp.where(group < 0, group + self.y_count, group) * self.share
        per_device = self.features // self.part
        index = 0
        for i in range(1, self.x_count * per_device):
            index = index + (feature >= i * self.part).astype(jnp.int32)
        offset = feature - index * self.part
        index = index - x * per_device
        return self.rotated(index, per_device, self.x_count * per_device), offset

    def rotated(self, index, per_device, blocks):
        index = jnp.where(index < 0, index + blocks, index)
        place = 0
        for ahead in range(self.x_count):
            back = (self.x_count - ahead) % self.x_count
            inside = (index >= ahead * per_device) & (index < (ahead + 1) * per_device)
            place = place + jnp.where(inside, index + (back - ahead) * per_device, 0)
        return place


def carried(hops, back, share, first, count):
    runs = []
    for other in (False, True):
        low, high = max(first, other * share), min(first + count, (other + 1) * share)
        if low < high:
            runs.append(((hops, other, back, low - other * share), low - first, high - low))
    return runs


def merge_kernel(*refs, count):
    sources, out = refs[:count], refs[-1]
    at = 0
    for source in sources:
        out[at : at + source.shape[0]] = source[...]
        at += source.shape[0]


def merge(sources, waited):
    rows = sum(a.shape[0] for a in sources)
    return pl.pallas_call(
        functools.partial(merge_kernel, count=len(sources)),
        out_shape=jax.ShapeDtypeStruct((rows,) + sources[0].shape[1:], sources[0].dtype),
        in_specs=[VMEM] * len(sources) + [WAITED] * len(waited),
        out_specs=VMEM,
        cost_estimate=BRIEF,
        compiler_params=pltpu.CompilerParams(vmem_limit_bytes=VMEM_LIMIT),
    )(*sources, *waited)


def split_kernel(source, *refs, pieces):
    outs, sems = refs[-pieces - 1 : -1], refs[-1]
    rows = outs[0].shape[0]
    copies = [
        pltpu.make_async_copy(source.at[pl.ds(i * rows, rows)], out, sems.at[i])
        for i, out in enumerate(outs)
    ]
    for c in copies:
        c.start()
    for c in copies:
        c.wait()


def split(source, pieces, waited):
    shape = (source.shape[0] // pieces,) + source.shape[1:]
    return pl.pallas_call(
        functools.partial(split_kernel, pieces=pieces),
        out_shape=[jax.ShapeDtypeStruct(shape, source.dtype)] * pieces,
        in_specs=[ANY] + [WAITED] * len(waited),
        out_specs=[VMEM] * pieces,
        scratch_shapes=[pltpu.SemaphoreType.DMA((pieces,))],
        cost_estimate=BRIEF,
        compiler_params=pltpu.CompilerParams(vmem_limit_bytes=VMEM_LIMIT),
    )(source, *waited)


def gemm_kernel(me, *refs, parts, sources, runs, layout, has_acc, final, tile, via_hbm):
    refs = list(refs)
    halves = [refs[:parts], refs[parts : 2 * parts]]
    del refs[: 2 * parts]
    weights = refs[:sources]
    del refs[:sources]
    acc_in = refs.pop(0) if has_acc else None
    bias = class_weight = None
    if final:
        bias, class_weight, class_bias = refs[:3]
        del refs[:3]
        outs = [refs.pop(0), refs.pop(0)]
        biased = refs.pop(0)
    else:
        out, token = refs.pop(0), refs.pop(0)
        token[...] = jnp.zeros_like(token)
    x_v, w_v, sems, acc_v, acc_sem = refs if via_hbm else refs + [None, None]
    rows = halves[0][0].shape[0]
    width = w_v.shape[1]
    depths = [depth for _, _, _, depth in runs]
    starts = [sum(depths[:i]) for i in range(len(depths))]
    columns = pl.ds(pl.multiple_of(me[2] * width, width), width)

    if final:
        classes = class_weight[1:2, columns] - class_weight[0:1, columns]

    def weight_copy(i):
        _, which, row, depth = runs[i]
        source = weights[which]
        lanes = slice(None) if source.shape[1] == width else columns
        source = source.at[row : row + depth, lanes]
        return pltpu.make_async_copy(source, w_v.at[pl.ds(starts[i], depths[i])], sems.at[i, 2])

    def row_copy(i, r, p, offset):
        return pltpu.make_async_copy(
            halves[r][p].at[:, pl.ds(offset, depths[i])],
            x_v.at[pl.ds(r * rows, rows), pl.ds(starts[i], depths[i])],
            sems.at[i, r],
        )

    for i, (run, _, _, _) in enumerate(runs):
        weight_copy(i).start()
        part, offset = layout.place(me, run)
        offset = pl.multiple_of(offset, HD)
        for r in range(2):
            for p in range(parts):
                pl.when(part == p)(row_copy(i, r, p, offset).start)
    held = out if not final else None
    if via_hbm:
        held = acc_v
        if has_acc:
            pltpu.make_async_copy(acc_in, acc_v, acc_sem).start()
    groups = []
    i = 0
    while i < len(runs):
        j, depth = i, 0
        while j < len(runs) and depth < 1024:
            depth += depths[j]
            j += 1
        groups.append((i, j))
        i = j
    for g, (first, last) in enumerate(groups):
        for i in range(first, last):
            weight_copy(i).wait()
            for r in range(2):
                row_copy(i, r, 0, 0).wait()
        if g == len(groups) - 1 and via_hbm and has_acc:
            pltpu.make_async_copy(acc_in, acc_v, acc_sem).wait()
        k0 = starts[first]
        k1 = starts[last - 1] + depths[last - 1]

        def body(m, carry, target=None, base=0):
            at = pl.ds(pl.multiple_of(base + m * tile, tile), tile)
            product = jnp.dot(x_v[at, k0:k1], w_v[k0:k1, :], preferred_element_type=jnp.float32)
            if via_hbm and has_acc:
                total = out[at, :] + product if g > 0 else product
                if g == len(groups) - 1:
                    total = total + acc_v[at, :]
            elif g > 0:
                total = held[at, :] + product
            elif has_acc:
                total = acc_in[at, :] + product
            else:
                total = product
            if target is not None:
                hidden = jnp.maximum(total + bias[:, columns], 0.0).astype(jnp.bfloat16)
                weighed = hidden.astype(jnp.float32) * classes
                folded = weighed[:, :HD]
                for j in range(1, width // HD):
                    folded = folded + weighed[:, j * HD : (j + 1) * HD]
                for j in range(tile // HD):
                    turned = folded[j * HD : (j + 1) * HD, :].T
                    lanes = pl.ds(pl.multiple_of(m * tile + j * HD, HD), HD)
                    target[:, lanes] = jnp.sum(turned, axis=0, keepdims=True)
            elif via_hbm and has_acc:
                out[at, :] = total
            else:
                held[at, :] = total
                if via_hbm and g == len(groups) - 1:
                    pltpu.make_async_copy(held.at[at, :], out.at[at, :], acc_sem).start()
            return carry

        if final:
            for r in range(2):
                lax.fori_loop(
                    0, rows // tile, functools.partial(body, target=outs[r], base=r * rows), 0
                )
            biased[...] = outs[0][...] + (class_bias[1] - class_bias[0])
        else:
            lax.fori_loop(0, 2 * rows // tile, body, 0)
    if via_hbm and not has_acc:
        pltpu.make_async_copy(held, out, acc_sem).wait()


def gemm(me, layout, halves, chunks, acc=None, tail=None, via_hbm=False):
    weights = [w for w, _ in chunks]
    runs = [(run, i, row, d) for i, (_, found) in enumerate(chunks) for run, row, d in found]
    parts = len(halves[0])
    rows = halves[0][0].shape[0]
    depth = sum(d for _, _, _, d in runs)
    width = min(w.shape[1] for w in weights)
    args = [me, *in_hbm([*halves[0], *halves[1]]), *weights]
    specs = [SMEM] + [ANY] * (2 * parts + len(weights))
    if acc is not None:
        space = pltpu.HBM if via_hbm else pltpu.VMEM
        args.append(pltpu.with_memory_space_constraint(acc, space))
        specs.append(ANY if via_hbm else VMEM)
    if tail is not None:
        args += list(tail)
        specs += [VMEM] * 2 + [SMEM]
        out_shape = [jax.ShapeDtypeStruct((1, rows), jnp.float32)] * 3
        out_specs = [VMEM] * 3
    else:
        out_shape = [
            (pltpu.HBM if via_hbm and acc is None else pltpu.VMEM)((2 * rows, width), jnp.float32),
            jax.ShapeDtypeStruct((8, HD), jnp.float32),
        ]
        out_specs = [ANY if via_hbm and acc is None else VMEM, VMEM]
    return pl.pallas_call(
        functools.partial(
            gemm_kernel,
            parts=parts,
            sources=len(weights),
            runs=tuple(runs),
            layout=layout,
            has_acc=acc is not None,
            final=tail is not None,
            tile=256,
            via_hbm=via_hbm,
        ),
        out_shape=out_shape,
        in_specs=specs,
        out_specs=out_specs,
        scratch_shapes=[
            pltpu.VMEM((2 * rows, depth), jnp.bfloat16),
            pltpu.VMEM((depth, width), jnp.bfloat16),
            pltpu.SemaphoreType.DMA((len(runs), 3)),
        ]
        + ([pltpu.VMEM((2 * rows, width), jnp.float32), pltpu.SemaphoreType.DMA] if via_hbm else []),
        cost_estimate=BRIEF,
        compiler_params=pltpu.CompilerParams(vmem_limit_bytes=VMEM_LIMIT),
    )(*args)


def both(attention, step_rows, norm_gain, head_weight, head_bias, class_weight, class_bias):
    z_count, x_count = lax.axis_size("batch"), lax.axis_size("mp")
    y_count = lax.axis_size("group")
    me = jnp.stack([lax.axis_index(a) for a in ("mp", "batch", "section", "group")]).astype(jnp.int32)
    swap = shift_pairs(2, 1)
    rows, features = step_rows.shape
    block, columns = head_weight.shape
    width = columns // 2
    share = block // y_count
    order = ring_order(z_count)
    ring = [(order[i], order[(i + 1) % z_count]) for i in range(z_count)]
    pieces, final_pieces = 2, 2
    layout = Layout(order, x_count, y_count, block, features, features // pieces)

    def forward(t):
        return lax.ppermute(t, "batch", ring)

    def over_group(t):
        return [lax.ppermute(t, "group", shift_pairs(y_count, k)) for k in range(1, y_count)]

    own = cut_share(me, head_weight, share, width, y_count, False, 0)
    given = [cut_share(me, head_weight, share, width, y_count, True, k) for k in range(y_count)]
    siblings = [lax.ppermute(g, "section", swap) for g in given]
    power = row_power(step_rows, own)
    merged = merge([own, siblings[0]], [power])
    whole = forward(merged)
    powers = [power] + [
        lax.ppermute(power, "mp", shift_pairs(x_count, k)) for k in range(1, x_count)
    ]
    mine = list(normalise(me, step_rows, powers, norm_gain, pieces, merged))
    raw = [
        lax.ppermute(part, "mp", shift_pairs(x_count, k))
        for k in range(1, x_count)
        for part in mine
    ]
    theirs = [lax.ppermute(part, "section", swap) for part in mine]
    blobs = attention.pack(siblings[0])
    arrived = attention.send(blobs)
    tail = [head_bias[None], class_weight.T.astype(jnp.float32), class_bias]
    chunks = [(head_weight, [((0, False, None, 0), 0, block)])] + [
        (t, [((0, True, (y_count - k) % y_count, 0), 0, share)]) for k, t in enumerate(siblings)
    ]
    waited = siblings[1:] + theirs
    for h in range(1, z_count - 2):
        if h > 1:
            whole = forward(whole)
        swapped = over_group(whole)
        chunks += [
            (t, carried(h, k, share, 0, 2 * share)) for k, t in enumerate([whole] + swapped)
        ]
        if h < z_count - 3:
            (whole,) = after([whole], waited)
            waited = swapped
    cuts = [forward(t) for t in split(whole, final_pieces, waited)]
    depth = 2 * share // final_pieces
    results = attention.answer(arrived)
    marks = [[blobs] + swapped + raw, [results]]
    second, last, travelled = [], [], []
    for j, t in enumerate(cuts):
        (t,) = after([t], marks[j])
        last.append(forward(t))
        swapped = over_group(t)
        if j + 1 < final_pieces:
            marks[j + 1] += swapped
        second += [
            (u, carried(z_count - 2, k, share, j * depth, depth))
            for k, u in enumerate([t] + swapped)
        ]
        travelled.append(t)
    for i, part in enumerate(raw):
        (part,) = after([part], [travelled[0]])
        mine.append(part)
        theirs.append(lax.ppermute(part, "section", swap))
    acc, early = gemm(me, layout, (mine, theirs), chunks, via_hbm=True)
    (results,) = after([results], [early])
    returned = attention.send(results)
    ends = []
    marks = [[], [early]]
    for j, t in enumerate(last):
        (t,) = after([t], marks[j])
        ends.append(
            [
                (u, carried(z_count - 1, k, share, j * depth, depth))
                for k, u in enumerate([t] + over_group(t))
            ]
        )
    attended = attention.finish(returned, early)
    middle = second + sum(ends[:-1], []) + ends[-1][:1]
    acc, _ = gemm(me, layout, (mine, theirs), middle, acc, via_hbm=True)
    kept, given, total = gemm(me, layout, (mine, theirs), ends[-1][1:], acc, tail)
    total = total + lax.ppermute(given, "section", swap)
    for k in range(1, x_count):
        total = total + lax.ppermute(kept, "mp", shift_pairs(x_count, k))
        total = total + lax.ppermute(
            given,
            ("mp", "section"),
            [
                (i * 2 + c, ((i + k) % x_count) * 2 + 1 - c)
                for i in range(x_count)
                for c in range(2)
            ],
        )
    return attended, total[0]


def judge_gathered(step_rows, norm_gain, head_weight, head_bias, class_weight, class_bias):
    full_rows = lax.all_gather(step_rows, "mp", axis=1, tiled=True)
    row_values = full_rows.astype(jnp.float32)
    power = jnp.mean(row_values * row_values, axis=1, keepdims=True)
    normed = (row_values * lax.rsqrt(power + 1e-06) * norm_gain).astype(jnp.bfloat16)
    projected = jnp.dot(
        normed,
        lax.all_gather(head_weight, ("batch", "section"), axis=0, tiled=True),
        preferred_element_type=jnp.float32,
    )
    hidden = jnp.maximum(projected + head_bias, 0.0).astype(jnp.bfloat16)
    partial_logits = jnp.dot(hidden, class_weight, preferred_element_type=jnp.float32)
    logits = lax.psum(partial_logits, "mp") + class_bias
    return logits[:, 1] - logits[:, 0]


def per_device(
    queries,
    new_keys,
    new_values,
    key_pages,
    value_pages,
    page_table,
    ancestry,
    lengths,
    step_rows,
    norm_gain,
    head_weight,
    head_bias,
    class_weight,
    class_bias,
):
    attention = Attention(
        queries, new_keys, new_values, key_pages, value_pages, page_table, ancestry, lengths
    )
    verifier = (step_rows, norm_gain, head_weight, head_bias, class_weight, class_bias)
    ring_fits = (
        4 <= lax.axis_size("batch") <= 8
        and lax.axis_size("mp") > 1
        and lax.axis_size("section") == 2
        and head_weight.shape[0] % (128 * lax.axis_size("group")) == 0
        and step_rows.shape[1] % (2 * head_weight.shape[0]) == 0
        and head_weight.shape[1] % 256 == 0
        and step_rows.shape[1] % head_weight.shape[0] == 0
    )
    if ring_fits:
        return both(attention, *verifier)
    arrived = attention.send(attention.pack(step_rows))
    returned = attention.send(attention.answer(arrived))
    return attention.finish(returned), judge_gathered(*verifier)


def solution(mesh):
    placed = (
        P("section", ("group", "batch"), "mp"),
        P("section", ("group", "batch"), "mp"),
        P("section", ("group", "batch"), "mp"),
        P("section", ("group", "batch"), None, "mp"),
        P("section", ("group", "batch"), None, "mp"),
        P(("group", "batch"), None),
        P("group"),
        P("group"),
        P(("group", "batch", "section"), "mp"),
        P(),
        P(("batch", "section"), "mp"),
        P("mp"),
        P("mp", None),
        P(),
    )
    return jax.shard_map(
        per_device,
        mesh=mesh,
        in_specs=placed,
        out_specs=(P("section", ("group", "batch"), "mp"), P(("group", "batch", "section"))),
        check_vma=False,
    )
```

```python
import functools

import jax
import jax.numpy as jnp
from jax import lax
from jax.experimental import pallas as pl
from jax.experimental.pallas import tpu as pltpu
from jax.sharding import PartitionSpec as P

HD = 128
VMEM_LIMIT = 24 << 20
BRIEF = pl.CostEstimate(flops=1, bytes_accessed=1, transcendentals=0)
ANY = pl.BlockSpec(memory_space=pltpu.HBM)
WAITED = pl.BlockSpec(memory_space=pl.ANY)
VMEM = pl.BlockSpec(memory_space=pltpu.VMEM)
SMEM = pl.BlockSpec(memory_space=pltpu.SMEM)


def in_hbm(arrays):
    return [pltpu.with_memory_space_constraint(a, pltpu.HBM) for a in arrays]


def pass_kernel(*refs):
    del refs


def after(passing, waited):
    many = len(passing)
    out = pl.pallas_call(
        pass_kernel,
        out_shape=[jax.ShapeDtypeStruct(a.shape, a.dtype) for a in passing],
        in_specs=[ANY] * many + [WAITED] * len(waited),
        out_specs=[ANY] * many,
        input_output_aliases={i: i for i in range(many)},
        cost_estimate=BRIEF,
        compiler_params=pltpu.CompilerParams(has_side_effects=True),
    )(*passing, *waited)
    return list(out)


def shift_pairs(count, step):
    return [(i, (i + step) % count) for i in range(count)]


def ring_order(count):
    return [0] + list(range(1, count, 2)) + [i for i in range(count - 1, 0, -1) if i % 2 == 0]


def pack_kernel(
    me, ancestry, lengths, queries, new_keys, new_values, waited,
    blobs, particle, length, pick, rows, request, seen, *, count, capacity
):
    del waited
    slots = queries.shape[0]
    at = 0
    for source in (queries, new_keys, new_values):
        for h in range(source.shape[1] // HD):
            rows[:, at, :] = source[:, h * HD : (h + 1) * HD].astype(jnp.float32)
            at += 1
    here = me[0]
    for k in range(count):
        seen[k] = 0

    def clear(i, carry):
        request[i] = 0
        particle[i] = 0
        length[i] = 1
        return carry

    lax.fori_loop(0, count * capacity, clear, 0)

    def ask(j, carry):
        owner = ancestry[here * slots + j] // slots
        rank = jnp.minimum(seen[owner], capacity - 1)
        seen[owner] = rank + 1
        pick[j] = owner * capacity + rank
        request[owner * capacity + rank] = j
        return carry

    lax.fori_loop(0, slots, ask, 0)

    def fill(i, carry):
        for k in range(count):
            blobs[k, i] = rows[request[k * capacity + i]].astype(jnp.bfloat16)
        return carry

    lax.fori_loop(0, capacity, fill, 0)
    for k in range(count):

        def answer(p, rank):
            ancestor = ancestry[k * slots + p]
            local = ancestor - here * slots
            match = (local >= 0) & (local < slots)
            at = k * capacity + jnp.minimum(rank, capacity - 1)

            @pl.when(match)
            def _():
                particle[at] = local
                length[at] = lengths[ancestor]

            return rank + match.astype(jnp.int32)

        lax.fori_loop(0, slots, answer, 0)


def pack(me, ancestry, lengths, queries, new_keys, new_values, waited, count, capacity):
    slots = queries.shape[0]
    depth = (queries.shape[1] + new_keys.shape[1] + new_values.shape[1]) // HD
    table = jax.ShapeDtypeStruct((count * capacity,), jnp.int32)
    out = pl.pallas_call(
        functools.partial(pack_kernel, count=count, capacity=capacity),
        out_shape=[jax.ShapeDtypeStruct((count, capacity, depth, HD), jnp.bfloat16)]
        + [table, table, jax.ShapeDtypeStruct((slots,), jnp.int32)],
        in_specs=[SMEM] * 3 + [VMEM] * 3 + [ANY],
        out_specs=[VMEM] + [SMEM] * 3,
        scratch_shapes=[
            pltpu.VMEM((slots, depth, HD), jnp.float32),
            pltpu.SMEM((count * capacity,), jnp.int32),
            pltpu.SMEM((count,), jnp.int32),
        ],
        cost_estimate=BRIEF,
        compiler_params=pltpu.CompilerParams(vmem_limit_bytes=VMEM_LIMIT),
    )(me, ancestry, lengths, queries, new_keys, new_values, waited)
    return out


def serve_kernel(
    particle, page_table, lengths, blobs, key_source, value_source, outs,
    key_pages, value_pages, sems, *, kv_local, unroll
):
    copies = [
        pltpu.make_async_copy(key_source, key_pages, sems.at[0]),
        pltpu.make_async_copy(value_source, value_pages, sems.at[1]),
    ]
    for c in copies:
        c.start()
    for c in copies:
        c.wait()
    count, capacity, heads = outs.shape[:3]
    group_size = heads // kv_local
    pages = page_table.shape[1]
    context = pages * key_pages.shape[1]
    score_scale = 1.0 / HD**0.5
    lanes_kv = lax.broadcasted_iota(jnp.int32, (heads, kv_local * HD), 1) // HD
    rows_kv = lax.broadcasted_iota(jnp.int32, (heads, kv_local * HD), 0) // group_size
    diagonal = lanes_kv == rows_kv
    positions = lax.broadcasted_iota(jnp.int32, (heads, context), 1)

    def spread(x):
        return jnp.broadcast_to(x[:, None, :], (kv_local, group_size, HD)).reshape(heads, HD)

    def together(k, slots):
        scores, own_products, own_values = [], [], []
        for slot in slots:
            at = k * capacity + slot
            rows = blobs[k, slot]
            query = rows[:heads].astype(jnp.float32)
            own_key = rows[heads : heads + kv_local].astype(jnp.float32)
            own_value = rows[heads + kv_local :].astype(jnp.float32)
            wide = jnp.concatenate([query] * kv_local, axis=1)
            wide = jnp.where(diagonal, wide, 0.0).astype(jnp.bfloat16)
            keys = jnp.concatenate(
                [key_pages[page_table[particle[at], i]] for i in range(pages)], axis=0
            )
            score = lax.dot_general(
                wide, keys, (((1,), (1,)), ((), ())), preferred_element_type=jnp.float32
            ) * score_scale
            scores.append(jnp.where(positions < lengths[at], score, -1e30))
            own_products.append(query * spread(own_key))
            own_values.append(spread(own_value))
        score = jnp.concatenate(scores, axis=0)
        top = jnp.max(score, axis=1, keepdims=True)
        weights = jnp.exp(score - top)
        own_score = jnp.sum(jnp.concatenate(own_products, axis=0), axis=1, keepdims=True) * score_scale
        own = jnp.exp(own_score - top)
        total = jnp.sum(weights, axis=1, keepdims=True) + own
        weights = weights.astype(jnp.bfloat16)
        for u, slot in enumerate(slots):
            at = k * capacity + slot
            mine = slice(u * heads, (u + 1) * heads)
            values = jnp.concatenate(
                [value_pages[page_table[particle[at], i]] for i in range(pages)], axis=0
            )
            mixed = jnp.dot(weights[mine], values, preferred_element_type=jnp.float32)
            numerator = jnp.concatenate(
                [
                    mixed[g * group_size : (g + 1) * group_size, g * HD : (g + 1) * HD]
                    for g in range(kv_local)
                ],
                axis=0,
            )
            result = (numerator + own[mine] * own_values[u]) / total[mine]
            outs[k, slot] = result.astype(jnp.bfloat16)

    def body(k, carry):
        for i in range(0, capacity, unroll):
            together(k, range(i, min(i + unroll, capacity)))
        return carry

    lax.fori_loop(0, count, body, 0)


def serve(particle, page_table, lengths, blobs, key_pages, value_pages):
    count, capacity, depth = blobs.shape[:3]
    kv_local = key_pages.shape[2] // HD
    heads = depth - 2 * kv_local
    return pl.pallas_call(
        functools.partial(serve_kernel, kv_local=kv_local, unroll=12),
        out_shape=jax.ShapeDtypeStruct((count, capacity, heads, HD), jnp.bfloat16),
        in_specs=[SMEM] * 3 + [VMEM] + [ANY] * 2,
        out_specs=VMEM,
        scratch_shapes=[
            pltpu.VMEM(key_pages.shape, key_pages.dtype),
            pltpu.VMEM(value_pages.shape, value_pages.dtype),
            pltpu.SemaphoreType.DMA((2,)),
        ],
        cost_estimate=BRIEF,
        compiler_params=pltpu.CompilerParams(vmem_limit_bytes=VMEM_LIMIT),
    )(particle, page_table, lengths, blobs, *in_hbm([key_pages, value_pages]))


def pick_kernel(pick, parts, *refs):
    out, rows = refs[-2:]
    slots = out.shape[0]
    capacity = parts.shape[1]

    flat = parts.reshape(parts.shape[0] * capacity, *parts.shape[2:])
    for j in range(slots):
        rows[j] = flat[pick[j]].astype(jnp.float32)
    for h in range(rows.shape[1]):
        out[:, h * HD : (h + 1) * HD] = rows[:, h, :].astype(jnp.bfloat16)


def pick_up(pick, parts, waited):
    heads = parts.shape[2]
    slots = pick.shape[0]
    return pl.pallas_call(
        pick_kernel,
        out_shape=jax.ShapeDtypeStruct((slots, heads * HD), jnp.bfloat16),
        in_specs=[SMEM, VMEM] + [WAITED] * len(waited),
        out_specs=VMEM,
        scratch_shapes=[pltpu.VMEM((slots, heads, HD), jnp.float32)],
        cost_estimate=BRIEF,
        compiler_params=pltpu.CompilerParams(vmem_limit_bytes=VMEM_LIMIT),
    )(pick, parts, *waited)


class Attention:
    def __init__(self, queries, new_keys, new_values, key_pages, value_pages, page_table, ancestry, lengths):
        self.count = lax.axis_size("batch")
        slots = page_table.shape[0]
        self.capacity = max(2, (2 * slots + self.count - 1) // self.count)
        self.rows = (ancestry, lengths, queries[0], new_keys[0], new_values[0])
        self.page_table, self.keys, self.values = page_table, key_pages[0], value_pages[0]

    def pack(self, waited):
        me = lax.axis_index("batch").reshape(1).astype(jnp.int32)
        blobs, self.particle, self.lengths, self.pick = pack(
            me, *self.rows, waited, self.count, self.capacity
        )
        return blobs

    def send(self, blobs):
        return lax.all_to_all(blobs, "batch", split_axis=0, concat_axis=0, tiled=True)

    def answer(self, arrived):
        return serve(
            self.particle, self.page_table, self.lengths, arrived, self.keys, self.values
        )

    def finish(self, returned, *waited):
        return pick_up(self.pick, returned, waited)[None]


def cut_kernel(me, weight, out, sem, *, back, other, y_count):
    share, width = out.shape
    core = 1 - me[2] if other else me[2]
    rows = pl.ds(pl.multiple_of(lax.rem(me[3] + back, y_count) * share, share), share)
    lanes = pl.ds(pl.multiple_of(core * width, width), width)
    copy = pltpu.make_async_copy(weight.at[rows, lanes], out, sem)
    copy.start()
    copy.wait()


def cut_share(me, weight, share, width, y_count, other, back):
    return pl.pallas_call(
        functools.partial(cut_kernel, back=back, other=other, y_count=y_count),
        out_shape=jax.ShapeDtypeStruct((share, width), weight.dtype),
        in_specs=[SMEM, ANY],
        out_specs=VMEM,
        scratch_shapes=[pltpu.SemaphoreType.DMA],
        cost_estimate=BRIEF,
        compiler_params=pltpu.CompilerParams(vmem_limit_bytes=VMEM_LIMIT),
    )(me, weight)


def power_kernel(x, waited, out):
    del waited
    rows, features = x.shape

    def body(i, carry):
        at = pl.ds(pl.multiple_of(i * HD, HD), HD)
        total = jnp.zeros((HD, HD), jnp.float32)
        for j in range(features // HD):
            v = x[at, j * HD : (j + 1) * HD].astype(jnp.float32)
            total = total + v * v
        out[pl.ds(i, 1), :] = jnp.sum(total.T, axis=0, keepdims=True)
        return carry

    lax.fori_loop(0, rows // HD, body, 0)


def row_power(x, waited):
    return pl.pallas_call(
        power_kernel,
        out_shape=jax.ShapeDtypeStruct((x.shape[0] // HD, HD), jnp.float32),
        in_specs=[VMEM, ANY],
        out_specs=VMEM,
        cost_estimate=BRIEF,
        compiler_params=pltpu.CompilerParams(vmem_limit_bytes=VMEM_LIMIT),
    )(x, waited)


def norm_kernel(me, x, *refs, total, count):
    powers, (gain, _, *outs) = refs[:count], refs[count:]
    rows, features = x.shape
    part = outs[0].shape[1]
    power = powers[0][...]
    for p in powers[1:]:
        power = power + p[...]
    scale = lax.rsqrt(power / total + 1e-06)
    start = me[0] * features

    for i in range(rows // HD):
        column = jnp.broadcast_to(scale[i : i + 1, :], (HD, HD)).T
        for j in range(features // HD):
            at = (slice(i * HD, (i + 1) * HD), slice(j * HD, (j + 1) * HD))
            lanes = pl.ds(pl.multiple_of(start + j * HD, HD), HD)
            value = (x[at].astype(jnp.float32) * column * gain[:, lanes]).astype(jnp.bfloat16)
            first = j * HD % part
            outs[j * HD // part][at[0], first : first + HD] = value


def normalise(me, x, powers, gain, pieces, waited):
    shape = (x.shape[0], x.shape[1] // pieces)
    return pl.pallas_call(
        functools.partial(
            norm_kernel, total=gain.shape[0], count=len(powers)
        ),
        out_shape=[jax.ShapeDtypeStruct(shape, jnp.bfloat16)] * pieces,
        in_specs=[SMEM] + [VMEM] * (2 + len(powers)) + [WAITED],
        out_specs=[VMEM] * pieces,
        cost_estimate=BRIEF,
        compiler_params=pltpu.CompilerParams(vmem_limit_bytes=VMEM_LIMIT),
    )(me, x, *powers, gain[None], waited)


class Layout:
    def __init__(self, order, x_count, y_count, block, features, part):
        self.order, self.x_count, self.y_count = order, x_count, y_count
        self.block, self.features, self.part = block, features, part
        self.share = block // y_count

    def place(self, me, run):
        hops, other, back, row = run
        x, z, s, y = me[0], me[1], me[2], me[3]
        count = len(self.order)
        owner = 0
        for i, at in enumerate(self.order):
            owner = owner + jnp.where(z == at, self.order[(i - hops) % count], 0)
        core = 1 - s if other else s
        feature = (2 * owner + core) * self.block + row
        if back is not None:
            group = y - back
            feature = feature + jnp.where(group < 0, group + self.y_count, group) * self.share
        per_device = self.features // self.part
        index = 0
        for i in range(1, self.x_count * per_device):
            index = index + (feature >= i * self.part).astype(jnp.int32)
        offset = feature - index * self.part
        index = index - x * per_device
        return self.rotated(index, per_device, self.x_count * per_device), offset

    def rotated(self, index, per_device, blocks):
        index = jnp.where(index < 0, index + blocks, index)
        place = 0
        for ahead in range(self.x_count):
            back = (self.x_count - ahead) % self.x_count
            inside = (index >= ahead * per_device) & (index < (ahead + 1) * per_device)
            place = place + jnp.where(inside, index + (back - ahead) * per_device, 0)
        return place


def carried(hops, back, share, first, count):
    runs = []
    for other in (False, True):
        low, high = max(first, other * share), min(first + count, (other + 1) * share)
        if low < high:
            runs.append(((hops, other, back, low - other * share), low - first, high - low))
    return runs


def merge_kernel(*refs, count):
    sources, out = refs[:count], refs[-1]
    at = 0
    for source in sources:
        out[at : at + source.shape[0]] = source[...]
        at += source.shape[0]


def merge(sources, waited):
    rows = sum(a.shape[0] for a in sources)
    return pl.pallas_call(
        functools.partial(merge_kernel, count=len(sources)),
        out_shape=jax.ShapeDtypeStruct((rows,) + sources[0].shape[1:], sources[0].dtype),
        in_specs=[VMEM] * len(sources) + [WAITED] * len(waited),
        out_specs=VMEM,
        cost_estimate=BRIEF,
        compiler_params=pltpu.CompilerParams(vmem_limit_bytes=VMEM_LIMIT),
    )(*sources, *waited)


def split_kernel(source, *refs, pieces):
    outs, sems = refs[-pieces - 1 : -1], refs[-1]
    rows = outs[0].shape[0]
    copies = [
        pltpu.make_async_copy(source.at[pl.ds(i * rows, rows)], out, sems.at[i])
        for i, out in enumerate(outs)
    ]
    for c in copies:
        c.start()
    for c in copies:
        c.wait()


def split(source, pieces, waited):
    shape = (source.shape[0] // pieces,) + source.shape[1:]
    return pl.pallas_call(
        functools.partial(split_kernel, pieces=pieces),
        out_shape=[jax.ShapeDtypeStruct(shape, source.dtype)] * pieces,
        in_specs=[ANY] + [WAITED] * len(waited),
        out_specs=[VMEM] * pieces,
        scratch_shapes=[pltpu.SemaphoreType.DMA((pieces,))],
        cost_estimate=BRIEF,
        compiler_params=pltpu.CompilerParams(vmem_limit_bytes=VMEM_LIMIT),
    )(source, *waited)


def gemm_kernel(me, *refs, parts, sources, runs, layout, has_acc, tile, via_hbm, later):
    refs = list(refs)
    halves = [refs[:parts], refs[parts : 2 * parts]]
    del refs[: 2 * parts]
    weights = refs[:sources]
    del refs[:sources]
    acc_in = refs.pop(0) if has_acc else None
    out, token = refs.pop(0), refs.pop(0)
    token[...] = jnp.zeros_like(token)
    ahead = refs.pop(0) if later else None
    x_v, w_v, sems, acc_v, acc_sem, later_sem = refs
    rows = halves[0][0].shape[0]
    width = w_v.shape[1]
    depths = [depth for _, _, _, depth in runs]
    starts = [sum(depths[:i]) for i in range(len(depths))]
    columns = pl.ds(pl.multiple_of(me[2] * width, width), width)

    def weight_copy(i):
        _, which, row, depth = runs[i]
        source = weights[which]
        lanes = slice(None) if source.shape[1] == width else columns
        source = source.at[row : row + depth, lanes]
        return pltpu.make_async_copy(source, w_v.at[pl.ds(starts[i], depths[i])], sems.at[i, 2])

    def row_copy(i, r, p, offset):
        return pltpu.make_async_copy(
            halves[r][p].at[:, pl.ds(offset, depths[i])],
            x_v.at[pl.ds(r * rows, rows), pl.ds(starts[i], depths[i])],
            sems.at[i, r],
        )

    for i, (run, _, _, _) in enumerate(runs):
        weight_copy(i).start()
        part, offset = layout.place(me, run)
        offset = pl.multiple_of(offset, HD)
        for r in range(2):
            for p in range(parts):
                pl.when(part == p)(row_copy(i, r, p, offset).start)
    held = acc_v if via_hbm else out
    if has_acc:
        pltpu.make_async_copy(acc_in, acc_v, acc_sem).start()
    first_lane = 0
    for run, depth in later:
        part, offset = layout.place(me, run)
        offset = pl.multiple_of(offset, HD)
        for r in range(2):
            for p in range(parts):
                copy = pltpu.make_async_copy(
                    halves[r][p].at[:, pl.ds(offset, depth)],
                    ahead.at[pl.ds(r * rows, rows), pl.ds(first_lane, depth)],
                    later_sem,
                )
                pl.when(part == p)(copy.start)
        first_lane += depth
    groups = []
    i = 0
    while i < len(runs):
        j, depth = i, 0
        while j < len(runs) and depth < 1024:
            depth += depths[j]
            j += 1
        groups.append((i, j))
        i = j
    for g, (first, last) in enumerate(groups):
        for i in range(first, last):
            weight_copy(i).wait()
            for r in range(2):
                row_copy(i, r, 0, 0).wait()
        if g == len(groups) - 1 and has_acc:
            pltpu.make_async_copy(acc_in, acc_v, acc_sem).wait()
        k0 = starts[first]
        k1 = starts[last - 1] + depths[last - 1]

        def body(m, carry):
            at = pl.ds(pl.multiple_of(m * tile, tile), tile)
            product = jnp.dot(x_v[at, k0:k1], w_v[k0:k1, :], preferred_element_type=jnp.float32)
            total = held[at, :] + product if g > 0 else product
            if has_acc and g == len(groups) - 1:
                total = total + acc_v[at, :]
            held[at, :] = total
            if via_hbm and g == len(groups) - 1:
                pltpu.make_async_copy(held.at[at, :], out.at[at, :], acc_sem).start()
            return carry

        lax.fori_loop(0, 2 * rows // tile, body, 0)
    if via_hbm:
        pltpu.make_async_copy(held, out, acc_sem).wait()
    if later:
        pltpu.make_async_copy(ahead, ahead, later_sem).wait()


def last_kernel(me, x, acc, *refs, tile):
    *weights, bias, class_weight, class_bias, kept, given, biased = refs
    rows, width = kept.shape[1], acc.shape[1]
    columns = pl.ds(pl.multiple_of(me[2] * width, width), width)
    classes = class_weight[1:2, columns] - class_weight[0:1, columns]
    for r, target in enumerate((kept, given)):

        def body(m, carry):
            at = pl.ds(pl.multiple_of(r * rows + m * tile, tile), tile)
            total = acc[at, :]
            first = 0
            for weight in weights:
                depth = weight.shape[0]
                total = total + jnp.dot(
                    x[at, first : first + depth], weight[...], preferred_element_type=jnp.float32
                )
                first += depth
            hidden = jnp.maximum(total + bias[:, columns], 0.0).astype(jnp.bfloat16)
            weighed = hidden.astype(jnp.float32) * classes
            folded = weighed[:, :HD]
            for j in range(1, width // HD):
                folded = folded + weighed[:, j * HD : (j + 1) * HD]
            for j in range(tile // HD):
                turned = folded[j * HD : (j + 1) * HD, :].T
                lanes = pl.ds(pl.multiple_of(m * tile + j * HD, HD), HD)
                target[:, lanes] = jnp.sum(turned, axis=0, keepdims=True)
            return carry

        lax.fori_loop(0, rows // tile, body, 0)
    biased[...] = kept[...] + (class_bias[1] - class_bias[0])


def last_phase(me, x, acc, weights, bias, class_weight, class_bias):
    rows = x.shape[0] // 2
    near = [pltpu.with_memory_space_constraint(a, pltpu.VMEM) for a in (x, acc)]
    return pl.pallas_call(
        functools.partial(last_kernel, tile=256),
        out_shape=[jax.ShapeDtypeStruct((1, rows), jnp.float32)] * 3,
        in_specs=[SMEM] + [VMEM] * (4 + len(weights)) + [SMEM],
        out_specs=[VMEM] * 3,
        cost_estimate=BRIEF,
        compiler_params=pltpu.CompilerParams(vmem_limit_bytes=VMEM_LIMIT),
    )(me, *near, *weights, bias, class_weight, class_bias)


def gemm(me, layout, halves, chunks, acc=None, later=()):
    weights = [w for w, _ in chunks]
    runs = [(run, i, row, d) for i, (_, found) in enumerate(chunks) for run, row, d in found]
    parts = len(halves[0])
    rows = halves[0][0].shape[0]
    depth = sum(d for _, _, _, d in runs)
    width = min(w.shape[1] for w in weights)
    args = [me, *in_hbm([*halves[0], *halves[1]]), *weights]
    if acc is not None:
        args += in_hbm([acc])
    space = pltpu.HBM if acc is None else pltpu.VMEM
    out_shape = [
        space((2 * rows, width), jnp.float32),
        jax.ShapeDtypeStruct((8, HD), jnp.float32),
    ]
    out_specs = [ANY if acc is None else VMEM, VMEM]
    if later:
        out_shape.append(pltpu.VMEM((2 * rows, sum(d for _, d in later)), jnp.bfloat16))
        out_specs.append(VMEM)
    return pl.pallas_call(
        functools.partial(
            gemm_kernel,
            parts=parts,
            sources=len(weights),
            runs=tuple(runs),
            layout=layout,
            has_acc=acc is not None,
            tile=256,
            via_hbm=acc is None,
            later=tuple(later),
        ),
        out_shape=out_shape,
        in_specs=[SMEM] + [ANY] * (len(args) - 1),
        out_specs=out_specs,
        scratch_shapes=[
            pltpu.VMEM((2 * rows, depth), jnp.bfloat16),
            pltpu.VMEM((depth, width), jnp.bfloat16),
            pltpu.SemaphoreType.DMA((len(runs), 3)),
            pltpu.VMEM((2 * rows, width), jnp.float32),
            pltpu.SemaphoreType.DMA,
            pltpu.SemaphoreType.DMA,
        ],
        cost_estimate=BRIEF,
        compiler_params=pltpu.CompilerParams(vmem_limit_bytes=VMEM_LIMIT),
    )(*args)


def both(attention, step_rows, norm_gain, head_weight, head_bias, class_weight, class_bias):
    z_count, x_count = lax.axis_size("batch"), lax.axis_size("mp")
    y_count = lax.axis_size("group")
    me = jnp.stack([lax.axis_index(a) for a in ("mp", "batch", "section", "group")]).astype(jnp.int32)
    swap = shift_pairs(2, 1)
    rows, features = step_rows.shape
    block, columns = head_weight.shape
    width = columns // 2
    share = block // y_count
    order = ring_order(z_count)
    ring = [(order[i], order[(i + 1) % z_count]) for i in range(z_count)]
    pieces, final_pieces = 2, 2
    layout = Layout(order, x_count, y_count, block, features, features // pieces)

    def forward(t):
        return lax.ppermute(t, "batch", ring)

    def over_group(t):
        return [lax.ppermute(t, "group", shift_pairs(y_count, k)) for k in range(1, y_count)]

    own = cut_share(me, head_weight, share, width, y_count, False, 0)
    given = [cut_share(me, head_weight, share, width, y_count, True, k) for k in range(y_count)]
    siblings = [lax.ppermute(g, "section", swap) for g in given]
    power = row_power(step_rows, own)
    merged = merge([own, siblings[0]], [power])
    whole = forward(merged)
    powers = [power] + [
        lax.ppermute(power, "mp", shift_pairs(x_count, k)) for k in range(1, x_count)
    ]
    mine = list(normalise(me, step_rows, powers, norm_gain, pieces, merged))
    raw = [
        lax.ppermute(part, "mp", shift_pairs(x_count, k))
        for k in range(1, x_count)
        for part in mine
    ]
    theirs = [lax.ppermute(part, "section", swap) for part in mine]
    blobs = attention.pack(siblings[0])
    arrived = attention.send(blobs)
    tail = [head_bias[None], class_weight.T.astype(jnp.float32), class_bias]
    chunks = [(head_weight, [((0, False, None, 0), 0, block)])] + [
        (t, [((0, True, (y_count - k) % y_count, 0), 0, share)]) for k, t in enumerate(siblings)
    ]
    waited = siblings[1:] + theirs
    for h in range(1, z_count - 2):
        if h > 1:
            whole = forward(whole)
        swapped = over_group(whole)
        chunks += [
            (t, carried(h, k, share, 0, 2 * share)) for k, t in enumerate([whole] + swapped)
        ]
        if h < z_count - 3:
            (whole,) = after([whole], waited)
            waited = swapped
    cuts = [forward(t) for t in split(whole, final_pieces, waited)]
    depth = 2 * share // final_pieces
    results = attention.answer(arrived)
    marks = [[blobs] + swapped + raw, [results]]
    second, last, travelled = [], [], []
    for j, t in enumerate(cuts):
        (t,) = after([t], marks[j])
        last.append(forward(t))
        swapped = over_group(t)
        if j + 1 < final_pieces:
            marks[j + 1] += swapped
        second += [
            (u, carried(z_count - 2, k, share, j * depth, depth))
            for k, u in enumerate([t] + swapped)
        ]
        travelled.append(t)
    for i, part in enumerate(raw):
        (part,) = after([part], [travelled[0]])
        mine.append(part)
        theirs.append(lax.ppermute(part, "section", swap))
    acc, early = gemm(me, layout, (mine, theirs), chunks)
    (results,) = after([results], [early])
    returned = attention.send(results)
    ends = []
    marks = [[], [early]]
    for j, t in enumerate(last):
        (t,) = after([t], marks[j])
        ends.append(
            [
                (u, carried(z_count - 1, k, share, j * depth, depth))
                for k, u in enumerate([t] + over_group(t))
            ]
        )
    attended = attention.finish(returned, early)
    middle = second + sum(ends[:-1], []) + ends[-1][:1]
    final = ends[-1][1:]
    later = [(run, d) for _, found in final for run, _, d in found]
    acc, _, ahead = gemm(me, layout, (mine, theirs), middle, acc, later)
    kept, given, total = last_phase(me, ahead, acc, [t for t, _ in final], *tail)
    total = total + lax.ppermute(given, "section", swap)
    for k in range(1, x_count):
        total = total + lax.ppermute(kept, "mp", shift_pairs(x_count, k))
        total = total + lax.ppermute(
            given,
            ("mp", "section"),
            [
                (i * 2 + c, ((i + k) % x_count) * 2 + 1 - c)
                for i in range(x_count)
                for c in range(2)
            ],
        )
    return attended, total[0]


def judge_gathered(step_rows, norm_gain, head_weight, head_bias, class_weight, class_bias):
    full_rows = lax.all_gather(step_rows, "mp", axis=1, tiled=True)
    row_values = full_rows.astype(jnp.float32)
    power = jnp.mean(row_values * row_values, axis=1, keepdims=True)
    normed = (row_values * lax.rsqrt(power + 1e-06) * norm_gain).astype(jnp.bfloat16)
    projected = jnp.dot(
        normed,
        lax.all_gather(head_weight, ("batch", "section"), axis=0, tiled=True),
        preferred_element_type=jnp.float32,
    )
    hidden = jnp.maximum(projected + head_bias, 0.0).astype(jnp.bfloat16)
    partial_logits = jnp.dot(hidden, class_weight, preferred_element_type=jnp.float32)
    logits = lax.psum(partial_logits, "mp") + class_bias
    return logits[:, 1] - logits[:, 0]


def per_device(
    queries,
    new_keys,
    new_values,
    key_pages,
    value_pages,
    page_table,
    ancestry,
    lengths,
    step_rows,
    norm_gain,
    head_weight,
    head_bias,
    class_weight,
    class_bias,
):
    attention = Attention(
        queries, new_keys, new_values, key_pages, value_pages, page_table, ancestry, lengths
    )
    verifier = (step_rows, norm_gain, head_weight, head_bias, class_weight, class_bias)
    ring_fits = (
        4 <= lax.axis_size("batch") <= 8
        and lax.axis_size("mp") > 1
        and lax.axis_size("section") == 2
        and head_weight.shape[0] % (128 * lax.axis_size("group")) == 0
        and step_rows.shape[1] % (2 * head_weight.shape[0]) == 0
        and head_weight.shape[1] % 256 == 0
        and step_rows.shape[1] % head_weight.shape[0] == 0
    )
    if ring_fits:
        return both(attention, *verifier)
    arrived = attention.send(attention.pack(step_rows))
    returned = attention.send(attention.answer(arrived))
    return attention.finish(returned), judge_gathered(*verifier)


def solution(mesh):
    placed = (
        P("section", ("group", "batch"), "mp"),
        P("section", ("group", "batch"), "mp"),
        P("section", ("group", "batch"), "mp"),
        P("section", ("group", "batch"), None, "mp"),
        P("section", ("group", "batch"), None, "mp"),
        P(("group", "batch"), None),
        P("group"),
        P("group"),
        P(("group", "batch", "section"), "mp"),
        P(),
        P(("batch", "section"), "mp"),
        P("mp"),
        P("mp", None),
        P(),
    )
    return jax.shard_map(
        per_device,
        mesh=mesh,
        in_specs=placed,
        out_specs=(P("section", ("group", "batch"), "mp"), P(("group", "batch", "section"))),
        check_vma=False,
    )
```

```python
import functools

import jax
import jax.numpy as jnp
from jax import lax
from jax.experimental import pallas as pl
from jax.experimental.pallas import tpu as pltpu
from jax.sharding import PartitionSpec as P

HD = 128
VMEM_LIMIT = 24 << 20
BRIEF = pl.CostEstimate(flops=1, bytes_accessed=1, transcendentals=0)
ANY = pl.BlockSpec(memory_space=pltpu.HBM)
WAITED = pl.BlockSpec(memory_space=pl.ANY)
VMEM = pl.BlockSpec(memory_space=pltpu.VMEM)
SMEM = pl.BlockSpec(memory_space=pltpu.SMEM)


def in_hbm(arrays):
    return [pltpu.with_memory_space_constraint(a, pltpu.HBM) for a in arrays]


def pass_kernel(*refs):
    del refs


def after(passing, waited):
    many = len(passing)
    out = pl.pallas_call(
        pass_kernel,
        out_shape=[jax.ShapeDtypeStruct(a.shape, a.dtype) for a in passing],
        in_specs=[ANY] * many + [WAITED] * len(waited),
        out_specs=[ANY] * many,
        input_output_aliases={i: i for i in range(many)},
        cost_estimate=BRIEF,
        compiler_params=pltpu.CompilerParams(has_side_effects=True),
    )(*passing, *waited)
    return list(out)


def shift_pairs(count, step):
    return [(i, (i + step) % count) for i in range(count)]


def ring_order(count):
    return [0] + list(range(1, count, 2)) + [i for i in range(count - 1, 0, -1) if i % 2 == 0]


def pack_kernel(
    me, ancestry, lengths, queries, new_keys, new_values, waited,
    blobs, particle, length, pick, rows, request, seen, *, count, capacity
):
    del waited
    slots = queries.shape[0]
    at = 0
    for source in (queries, new_keys, new_values):
        for h in range(source.shape[1] // HD):
            rows[:, at, :] = source[:, h * HD : (h + 1) * HD].astype(jnp.float32)
            at += 1
    here = me[0]
    for k in range(count):
        seen[k] = 0

    def clear(i, carry):
        request[i] = 0
        particle[i] = 0
        length[i] = 1
        return carry

    lax.fori_loop(0, count * capacity, clear, 0)

    def ask(j, carry):
        owner = ancestry[here * slots + j] // slots
        rank = jnp.minimum(seen[owner], capacity - 1)
        seen[owner] = rank + 1
        pick[j] = owner * capacity + rank
        request[owner * capacity + rank] = j
        return carry

    lax.fori_loop(0, slots, ask, 0)

    def fill(i, carry):
        for k in range(count):
            blobs[k, i] = rows[request[k * capacity + i]].astype(jnp.bfloat16)
        return carry

    lax.fori_loop(0, capacity, fill, 0)
    for k in range(count):

        def answer(p, rank):
            ancestor = ancestry[k * slots + p]
            local = ancestor - here * slots
            match = (local >= 0) & (local < slots)
            at = k * capacity + jnp.minimum(rank, capacity - 1)

            @pl.when(match)
            def _():
                particle[at] = local
                length[at] = lengths[ancestor]

            return rank + match.astype(jnp.int32)

        lax.fori_loop(0, slots, answer, 0)


def pack(me, ancestry, lengths, queries, new_keys, new_values, waited, count, capacity):
    slots = queries.shape[0]
    depth = (queries.shape[1] + new_keys.shape[1] + new_values.shape[1]) // HD
    table = jax.ShapeDtypeStruct((count * capacity,), jnp.int32)
    out = pl.pallas_call(
        functools.partial(pack_kernel, count=count, capacity=capacity),
        out_shape=[jax.ShapeDtypeStruct((count, capacity, depth, HD), jnp.bfloat16)]
        + [table, table, jax.ShapeDtypeStruct((slots,), jnp.int32)],
        in_specs=[SMEM] * 3 + [VMEM] * 3 + [ANY],
        out_specs=[VMEM] + [SMEM] * 3,
        scratch_shapes=[
            pltpu.VMEM((slots, depth, HD), jnp.float32),
            pltpu.SMEM((count * capacity,), jnp.int32),
            pltpu.SMEM((count,), jnp.int32),
        ],
        cost_estimate=BRIEF,
        compiler_params=pltpu.CompilerParams(vmem_limit_bytes=VMEM_LIMIT),
    )(me, ancestry, lengths, queries, new_keys, new_values, waited)
    return out


def serve_kernel(
    particle, page_table, lengths, blobs, key_source, value_source, outs,
    key_pages, value_pages, sems, *, kv_local, unroll
):
    copies = [
        pltpu.make_async_copy(key_source, key_pages, sems.at[0]),
        pltpu.make_async_copy(value_source, value_pages, sems.at[1]),
    ]
    for c in copies:
        c.start()
    for c in copies:
        c.wait()
    count, capacity, heads = outs.shape[:3]
    group_size = heads // kv_local
    pages = page_table.shape[1]
    context = pages * key_pages.shape[1]
    score_scale = 1.0 / HD**0.5
    lanes_kv = lax.broadcasted_iota(jnp.int32, (heads, kv_local * HD), 1) // HD
    rows_kv = lax.broadcasted_iota(jnp.int32, (heads, kv_local * HD), 0) // group_size
    diagonal = lanes_kv == rows_kv
    positions = lax.broadcasted_iota(jnp.int32, (heads, context), 1)

    def spread(x):
        return jnp.broadcast_to(x[:, None, :], (kv_local, group_size, HD)).reshape(heads, HD)

    def together(k, slots):
        scores, own_products, own_values = [], [], []
        for slot in slots:
            at = k * capacity + slot
            rows = blobs[k, slot]
            query = rows[:heads].astype(jnp.float32)
            own_key = rows[heads : heads + kv_local].astype(jnp.float32)
            own_value = rows[heads + kv_local :].astype(jnp.float32)
            wide = jnp.concatenate([query] * kv_local, axis=1)
            wide = jnp.where(diagonal, wide, 0.0).astype(jnp.bfloat16)
            keys = jnp.concatenate(
                [key_pages[page_table[particle[at], i]] for i in range(pages)], axis=0
            )
            score = lax.dot_general(
                wide, keys, (((1,), (1,)), ((), ())), preferred_element_type=jnp.float32
            ) * score_scale
            scores.append(jnp.where(positions < lengths[at], score, -1e30))
            own_products.append(query * spread(own_key))
            own_values.append(spread(own_value))
        score = jnp.concatenate(scores, axis=0)
        top = jnp.max(score, axis=1, keepdims=True)
        weights = jnp.exp(score - top)
        own_score = jnp.sum(jnp.concatenate(own_products, axis=0), axis=1, keepdims=True) * score_scale
        own = jnp.exp(own_score - top)
        total = jnp.sum(weights, axis=1, keepdims=True) + own
        weights = weights.astype(jnp.bfloat16)
        for u, slot in enumerate(slots):
            at = k * capacity + slot
            mine = slice(u * heads, (u + 1) * heads)
            values = jnp.concatenate(
                [value_pages[page_table[particle[at], i]] for i in range(pages)], axis=0
            )
            mixed = jnp.dot(weights[mine], values, preferred_element_type=jnp.float32)
            numerator = jnp.concatenate(
                [
                    mixed[g * group_size : (g + 1) * group_size, g * HD : (g + 1) * HD]
                    for g in range(kv_local)
                ],
                axis=0,
            )
            result = (numerator + own[mine] * own_values[u]) / total[mine]
            outs[k, slot] = result.astype(jnp.bfloat16)

    def body(k, carry):
        for i in range(0, capacity, unroll):
            together(k, range(i, min(i + unroll, capacity)))
        return carry

    lax.fori_loop(0, count, body, 0)


def serve(particle, page_table, lengths, blobs, key_pages, value_pages):
    count, capacity, depth = blobs.shape[:3]
    kv_local = key_pages.shape[2] // HD
    heads = depth - 2 * kv_local
    return pl.pallas_call(
        functools.partial(serve_kernel, kv_local=kv_local, unroll=12),
        out_shape=jax.ShapeDtypeStruct((count, capacity, heads, HD), jnp.bfloat16),
        in_specs=[SMEM] * 3 + [VMEM] + [ANY] * 2,
        out_specs=VMEM,
        scratch_shapes=[
            pltpu.VMEM(key_pages.shape, key_pages.dtype),
            pltpu.VMEM(value_pages.shape, value_pages.dtype),
            pltpu.SemaphoreType.DMA((2,)),
        ],
        cost_estimate=BRIEF,
        compiler_params=pltpu.CompilerParams(vmem_limit_bytes=VMEM_LIMIT),
    )(particle, page_table, lengths, blobs, *in_hbm([key_pages, value_pages]))


def pick_kernel(pick, parts, *refs):
    out, rows = refs[-2:]
    slots = out.shape[0]
    capacity = parts.shape[1]

    flat = parts.reshape(parts.shape[0] * capacity, *parts.shape[2:])
    for j in range(slots):
        rows[j] = flat[pick[j]].astype(jnp.float32)
    for h in range(rows.shape[1]):
        out[:, h * HD : (h + 1) * HD] = rows[:, h, :].astype(jnp.bfloat16)


def pick_up(pick, parts, waited):
    heads = parts.shape[2]
    slots = pick.shape[0]
    return pl.pallas_call(
        pick_kernel,
        out_shape=jax.ShapeDtypeStruct((slots, heads * HD), jnp.bfloat16),
        in_specs=[SMEM, VMEM] + [WAITED] * len(waited),
        out_specs=VMEM,
        scratch_shapes=[pltpu.VMEM((slots, heads, HD), jnp.float32)],
        cost_estimate=BRIEF,
        compiler_params=pltpu.CompilerParams(vmem_limit_bytes=VMEM_LIMIT),
    )(pick, parts, *waited)


class Attention:
    def __init__(self, queries, new_keys, new_values, key_pages, value_pages, page_table, ancestry, lengths):
        self.count = lax.axis_size("batch")
        slots = page_table.shape[0]
        self.capacity = max(2, (2 * slots + self.count - 1) // self.count)
        self.rows = (ancestry, lengths, queries[0], new_keys[0], new_values[0])
        self.page_table, self.keys, self.values = page_table, key_pages[0], value_pages[0]

    def pack(self, waited):
        me = lax.axis_index("batch").reshape(1).astype(jnp.int32)
        blobs, self.particle, self.lengths, self.pick = pack(
            me, *self.rows, waited, self.count, self.capacity
        )
        return blobs

    def send(self, blobs):
        return lax.all_to_all(blobs, "batch", split_axis=0, concat_axis=0, tiled=True)

    def answer(self, arrived):
        return serve(
            self.particle, self.page_table, self.lengths, arrived, self.keys, self.values
        )

    def finish(self, returned, *waited):
        return pick_up(self.pick, returned, waited)[None]


def cut_kernel(me, weight, out, sem, *, back, other, y_count):
    share, width = out.shape
    core = 1 - me[2] if other else me[2]
    rows = pl.ds(pl.multiple_of(lax.rem(me[3] + back, y_count) * share, share), share)
    lanes = pl.ds(pl.multiple_of(core * width, width), width)
    copy = pltpu.make_async_copy(weight.at[rows, lanes], out, sem)
    copy.start()
    copy.wait()


def cut_share(me, weight, share, width, y_count, other, back):
    return pl.pallas_call(
        functools.partial(cut_kernel, back=back, other=other, y_count=y_count),
        out_shape=jax.ShapeDtypeStruct((share, width), weight.dtype),
        in_specs=[SMEM, ANY],
        out_specs=VMEM,
        scratch_shapes=[pltpu.SemaphoreType.DMA],
        cost_estimate=BRIEF,
        compiler_params=pltpu.CompilerParams(vmem_limit_bytes=VMEM_LIMIT),
    )(me, weight)


def power_kernel(x, waited, out):
    del waited
    rows, features = x.shape

    def body(i, carry):
        at = pl.ds(pl.multiple_of(i * HD, HD), HD)
        total = jnp.zeros((HD, HD), jnp.float32)
        for j in range(features // HD):
            v = x[at, j * HD : (j + 1) * HD].astype(jnp.float32)
            total = total + v * v
        out[pl.ds(i, 1), :] = jnp.sum(total.T, axis=0, keepdims=True)
        return carry

    lax.fori_loop(0, rows // HD, body, 0)


def row_power(x, waited):
    return pl.pallas_call(
        power_kernel,
        out_shape=jax.ShapeDtypeStruct((x.shape[0] // HD, HD), jnp.float32),
        in_specs=[VMEM, ANY],
        out_specs=VMEM,
        cost_estimate=BRIEF,
        compiler_params=pltpu.CompilerParams(vmem_limit_bytes=VMEM_LIMIT),
    )(x, waited)


def norm_kernel(me, x, *refs, total, count):
    powers, (gain, _, *outs) = refs[:count], refs[count:]
    rows, features = x.shape
    part = outs[0].shape[1]
    power = powers[0][...]
    for p in powers[1:]:
        power = power + p[...]
    scale = lax.rsqrt(power / total + 1e-06)
    start = me[0] * features

    for i in range(rows // HD):
        column = jnp.broadcast_to(scale[i : i + 1, :], (HD, HD)).T
        for j in range(features // HD):
            at = (slice(i * HD, (i + 1) * HD), slice(j * HD, (j + 1) * HD))
            lanes = pl.ds(pl.multiple_of(start + j * HD, HD), HD)
            value = (x[at].astype(jnp.float32) * column * gain[:, lanes]).astype(jnp.bfloat16)
            first = j * HD % part
            outs[j * HD // part][at[0], first : first + HD] = value


def normalise(me, x, powers, gain, pieces, waited):
    shape = (x.shape[0], x.shape[1] // pieces)
    return pl.pallas_call(
        functools.partial(
            norm_kernel, total=gain.shape[0], count=len(powers)
        ),
        out_shape=[jax.ShapeDtypeStruct(shape, jnp.bfloat16)] * pieces,
        in_specs=[SMEM] + [VMEM] * (2 + len(powers)) + [WAITED],
        out_specs=[VMEM] * pieces,
        cost_estimate=BRIEF,
        compiler_params=pltpu.CompilerParams(vmem_limit_bytes=VMEM_LIMIT),
    )(me, x, *powers, gain[None], waited)


class Layout:
    def __init__(self, order, x_count, y_count, block, features, part):
        self.order, self.x_count, self.y_count = order, x_count, y_count
        self.block, self.features, self.part = block, features, part
        self.share = block // y_count

    def place(self, me, run):
        hops, other, back, row = run
        x, z, s, y = me[0], me[1], me[2], me[3]
        count = len(self.order)
        owner = 0
        for i, at in enumerate(self.order):
            owner = owner + jnp.where(z == at, self.order[(i - hops) % count], 0)
        core = 1 - s if other else s
        feature = (2 * owner + core) * self.block + row
        if back is not None:
            group = y - back
            feature = feature + jnp.where(group < 0, group + self.y_count, group) * self.share
        per_device = self.features // self.part
        index = 0
        for i in range(1, self.x_count * per_device):
            index = index + (feature >= i * self.part).astype(jnp.int32)
        offset = feature - index * self.part
        index = index - x * per_device
        return self.rotated(index, per_device, self.x_count * per_device), offset

    def rotated(self, index, per_device, blocks):
        index = jnp.where(index < 0, index + blocks, index)
        place = 0
        for ahead in range(self.x_count):
            back = (self.x_count - ahead) % self.x_count
            inside = (index >= ahead * per_device) & (index < (ahead + 1) * per_device)
            place = place + jnp.where(inside, index + (back - ahead) * per_device, 0)
        return place


def carried(hops, back, share, first, count):
    runs = []
    for other in (False, True):
        low, high = max(first, other * share), min(first + count, (other + 1) * share)
        if low < high:
            runs.append(((hops, other, back, low - other * share), low - first, high - low))
    return runs


def merge_kernel(*refs, count):
    sources, out = refs[:count], refs[-1]
    at = 0
    for source in sources:
        out[at : at + source.shape[0]] = source[...]
        at += source.shape[0]


def merge(sources, waited):
    rows = sum(a.shape[0] for a in sources)
    return pl.pallas_call(
        functools.partial(merge_kernel, count=len(sources)),
        out_shape=jax.ShapeDtypeStruct((rows,) + sources[0].shape[1:], sources[0].dtype),
        in_specs=[VMEM] * len(sources) + [WAITED] * len(waited),
        out_specs=VMEM,
        cost_estimate=BRIEF,
        compiler_params=pltpu.CompilerParams(vmem_limit_bytes=VMEM_LIMIT),
    )(*sources, *waited)


def split_kernel(source, *refs, pieces):
    outs, sems = refs[-pieces - 1 : -1], refs[-1]
    rows = outs[0].shape[0]
    copies = [
        pltpu.make_async_copy(source.at[pl.ds(i * rows, rows)], out, sems.at[i])
        for i, out in enumerate(outs)
    ]
    for c in copies:
        c.start()
    for c in copies:
        c.wait()


def split(source, pieces, waited):
    shape = (source.shape[0] // pieces,) + source.shape[1:]
    return pl.pallas_call(
        functools.partial(split_kernel, pieces=pieces),
        out_shape=[jax.ShapeDtypeStruct(shape, source.dtype)] * pieces,
        in_specs=[ANY] + [WAITED] * len(waited),
        out_specs=[VMEM] * pieces,
        scratch_shapes=[pltpu.SemaphoreType.DMA((pieces,))],
        cost_estimate=BRIEF,
        compiler_params=pltpu.CompilerParams(vmem_limit_bytes=VMEM_LIMIT),
    )(source, *waited)


def gemm_kernel(me, *refs, parts, sources, runs, layout, has_acc, tile, via_hbm, later):
    refs = list(refs)
    halves = [refs[:parts], refs[parts : 2 * parts]]
    del refs[: 2 * parts]
    weights = refs[:sources]
    del refs[:sources]
    acc_in = refs.pop(0) if has_acc else None
    out, token = refs.pop(0), refs.pop(0)
    token[...] = jnp.zeros_like(token)
    ahead = refs.pop(0) if later else None
    x_v, w_v, sems, acc_v, acc_sem, later_sem = refs
    rows = halves[0][0].shape[0]
    width = w_v.shape[1]
    depths = [depth for _, _, _, depth in runs]
    starts = [sum(depths[:i]) for i in range(len(depths))]
    columns = pl.ds(pl.multiple_of(me[2] * width, width), width)

    def weight_copy(i):
        _, which, row, depth = runs[i]
        source = weights[which]
        lanes = slice(None) if source.shape[1] == width else columns
        source = source.at[row : row + depth, lanes]
        return pltpu.make_async_copy(source, w_v.at[pl.ds(starts[i], depths[i])], sems.at[i, 2])

    def row_copy(i, r, p, offset):
        return pltpu.make_async_copy(
            halves[r][p].at[:, pl.ds(offset, depths[i])],
            x_v.at[pl.ds(r * rows, rows), pl.ds(starts[i], depths[i])],
            sems.at[i, r],
        )

    for i, (run, _, _, _) in enumerate(runs):
        weight_copy(i).start()
        part, offset = layout.place(me, run)
        offset = pl.multiple_of(offset, HD)
        for r in range(2):
            for p in range(parts):
                pl.when(part == p)(row_copy(i, r, p, offset).start)
    held = acc_v if via_hbm else out
    if has_acc:
        pltpu.make_async_copy(acc_in, acc_v, acc_sem).start()
    first_lane = 0
    for run, depth in later:
        part, offset = layout.place(me, run)
        offset = pl.multiple_of(offset, HD)
        for r in range(2):
            for p in range(parts):
                copy = pltpu.make_async_copy(
                    halves[r][p].at[:, pl.ds(offset, depth)],
                    ahead.at[pl.ds(r * rows, rows), pl.ds(first_lane, depth)],
                    later_sem,
                )
                pl.when(part == p)(copy.start)
        first_lane += depth
    groups = []
    i = 0
    while i < len(runs):
        j, depth = i, 0
        while j < len(runs) and depth < 1024:
            depth += depths[j]
            j += 1
        groups.append((i, j))
        i = j
    for g, (first, last) in enumerate(groups):
        for i in range(first, last):
            weight_copy(i).wait()
            for r in range(2):
                row_copy(i, r, 0, 0).wait()
        if g == len(groups) - 1 and has_acc:
            pltpu.make_async_copy(acc_in, acc_v, acc_sem).wait()
        k0 = starts[first]
        k1 = starts[last - 1] + depths[last - 1]

        def body(m, carry):
            at = pl.ds(pl.multiple_of(m * tile, tile), tile)
            product = jnp.dot(x_v[at, k0:k1], w_v[k0:k1, :], preferred_element_type=jnp.float32)
            total = held[at, :] + product if g > 0 else product
            if has_acc and g == len(groups) - 1:
                total = total + acc_v[at, :]
            held[at, :] = total
            if via_hbm and g == len(groups) - 1:
                pltpu.make_async_copy(held.at[at, :], out.at[at, :], acc_sem).start()
            return carry

        lax.fori_loop(0, 2 * rows // tile, body, 0)
    if via_hbm:
        pltpu.make_async_copy(held, out, acc_sem).wait()
    if later:
        pltpu.make_async_copy(ahead, ahead, later_sem).wait()


def last_kernel(me, x, acc, *refs, tile):
    *weights, bias, class_weight, class_bias, kept, given, biased = refs
    rows, width = kept.shape[1], acc.shape[1]
    columns = pl.ds(pl.multiple_of(me[2] * width, width), width)
    classes = class_weight[1:2, columns] - class_weight[0:1, columns]
    for r, target in enumerate((kept, given)):

        def body(m, carry):
            at = pl.ds(pl.multiple_of(r * rows + m * tile, tile), tile)
            total = acc[at, :]
            first = 0
            for weight in weights:
                depth = weight.shape[0]
                total = total + jnp.dot(
                    x[at, first : first + depth], weight[...], preferred_element_type=jnp.float32
                )
                first += depth
            hidden = jnp.maximum(total + bias[:, columns], 0.0).astype(jnp.bfloat16)
            weighed = hidden.astype(jnp.float32) * classes
            folded = weighed[:, :HD]
            for j in range(1, width // HD):
                folded = folded + weighed[:, j * HD : (j + 1) * HD]
            for j in range(tile // HD):
                turned = folded[j * HD : (j + 1) * HD, :].T
                lanes = pl.ds(pl.multiple_of(m * tile + j * HD, HD), HD)
                target[:, lanes] = jnp.sum(turned, axis=0, keepdims=True)
            return carry

        lax.fori_loop(0, rows // tile, body, 0)
    biased[...] = kept[...] + (class_bias[1] - class_bias[0])


def last_phase(me, x, acc, weights, bias, class_weight, class_bias):
    rows = x.shape[0] // 2
    near = [pltpu.with_memory_space_constraint(a, pltpu.VMEM) for a in (x, acc)]
    return pl.pallas_call(
        functools.partial(last_kernel, tile=512),
        out_shape=[jax.ShapeDtypeStruct((1, rows), jnp.float32)] * 3,
        in_specs=[SMEM] + [VMEM] * (4 + len(weights)) + [SMEM],
        out_specs=[VMEM] * 3,
        cost_estimate=BRIEF,
        compiler_params=pltpu.CompilerParams(vmem_limit_bytes=VMEM_LIMIT),
    )(me, *near, *weights, bias, class_weight, class_bias)


def gemm(me, layout, halves, chunks, acc=None, later=()):
    weights = [w for w, _ in chunks]
    runs = [(run, i, row, d) for i, (_, found) in enumerate(chunks) for run, row, d in found]
    parts = len(halves[0])
    rows = halves[0][0].shape[0]
    depth = sum(d for _, _, _, d in runs)
    width = min(w.shape[1] for w in weights)
    args = [me, *in_hbm([*halves[0], *halves[1]]), *weights]
    if acc is not None:
        args += in_hbm([acc])
    space = pltpu.HBM if acc is None else pltpu.VMEM
    out_shape = [
        space((2 * rows, width), jnp.float32),
        jax.ShapeDtypeStruct((8, HD), jnp.float32),
    ]
    out_specs = [ANY if acc is None else VMEM, VMEM]
    if later:
        out_shape.append(pltpu.VMEM((2 * rows, sum(d for _, d in later)), jnp.bfloat16))
        out_specs.append(VMEM)
    return pl.pallas_call(
        functools.partial(
            gemm_kernel,
            parts=parts,
            sources=len(weights),
            runs=tuple(runs),
            layout=layout,
            has_acc=acc is not None,
            tile=512,
            via_hbm=acc is None,
            later=tuple(later),
        ),
        out_shape=out_shape,
        in_specs=[SMEM] + [ANY] * (len(args) - 1),
        out_specs=out_specs,
        scratch_shapes=[
            pltpu.VMEM((2 * rows, depth), jnp.bfloat16),
            pltpu.VMEM((depth, width), jnp.bfloat16),
            pltpu.SemaphoreType.DMA((len(runs), 3)),
            pltpu.VMEM((2 * rows, width), jnp.float32),
            pltpu.SemaphoreType.DMA,
            pltpu.SemaphoreType.DMA,
        ],
        cost_estimate=BRIEF,
        compiler_params=pltpu.CompilerParams(vmem_limit_bytes=VMEM_LIMIT),
    )(*args)


def both(attention, step_rows, norm_gain, head_weight, head_bias, class_weight, class_bias):
    z_count, x_count = lax.axis_size("batch"), lax.axis_size("mp")
    y_count = lax.axis_size("group")
    me = jnp.stack([lax.axis_index(a) for a in ("mp", "batch", "section", "group")]).astype(jnp.int32)
    swap = shift_pairs(2, 1)
    rows, features = step_rows.shape
    block, columns = head_weight.shape
    width = columns // 2
    share = block // y_count
    order = ring_order(z_count)
    ring = [(order[i], order[(i + 1) % z_count]) for i in range(z_count)]
    pieces, final_pieces = 2, 2
    layout = Layout(order, x_count, y_count, block, features, features // pieces)

    def forward(t):
        return lax.ppermute(t, "batch", ring)

    def over_group(t):
        return [lax.ppermute(t, "group", shift_pairs(y_count, k)) for k in range(1, y_count)]

    own = cut_share(me, head_weight, share, width, y_count, False, 0)
    given = [cut_share(me, head_weight, share, width, y_count, True, k) for k in range(y_count)]
    siblings = [lax.ppermute(g, "section", swap) for g in given]
    power = row_power(step_rows, own)
    merged = merge([own, siblings[0]], [power])
    whole = forward(merged)
    powers = [power] + [
        lax.ppermute(power, "mp", shift_pairs(x_count, k)) for k in range(1, x_count)
    ]
    mine = list(normalise(me, step_rows, powers, norm_gain, pieces, merged))
    raw = [
        lax.ppermute(part, "mp", shift_pairs(x_count, k))
        for k in range(1, x_count)
        for part in mine
    ]
    theirs = [lax.ppermute(part, "section", swap) for part in mine]
    blobs = attention.pack(siblings[0])
    arrived = attention.send(blobs)
    tail = [head_bias[None], class_weight.T.astype(jnp.float32), class_bias]
    chunks = [(head_weight, [((0, False, None, 0), 0, block)])] + [
        (t, [((0, True, (y_count - k) % y_count, 0), 0, share)]) for k, t in enumerate(siblings)
    ]
    waited = siblings[1:] + theirs
    for h in range(1, z_count - 2):
        if h > 1:
            whole = forward(whole)
        swapped = over_group(whole)
        chunks += [
            (t, carried(h, k, share, 0, 2 * share)) for k, t in enumerate([whole] + swapped)
        ]
        if h < z_count - 3:
            (whole,) = after([whole], waited)
            waited = swapped
    cuts = [forward(t) for t in split(whole, final_pieces, waited)]
    depth = 2 * share // final_pieces
    results = attention.answer(arrived)
    marks = [[blobs] + swapped + raw, [results]]
    second, last, travelled = [], [], []
    for j, t in enumerate(cuts):
        (t,) = after([t], marks[j])
        last.append(forward(t))
        swapped = over_group(t)
        if j + 1 < final_pieces:
            marks[j + 1] += swapped
        second += [
            (u, carried(z_count - 2, k, share, j * depth, depth))
            for k, u in enumerate([t] + swapped)
        ]
        travelled.append(t)
    for i, part in enumerate(raw):
        (part,) = after([part], [travelled[0]])
        mine.append(part)
        theirs.append(lax.ppermute(part, "section", swap))
    acc, early = gemm(me, layout, (mine, theirs), chunks)
    (results,) = after([results], [early])
    returned = attention.send(results)
    ends = []
    marks = [[], [early]]
    for j, t in enumerate(last):
        (t,) = after([t], marks[j])
        ends.append(
            [
                (u, carried(z_count - 1, k, share, j * depth, depth))
                for k, u in enumerate([t] + over_group(t))
            ]
        )
    attended = attention.finish(returned, early)
    middle = second + sum(ends[:-1], []) + ends[-1][:1]
    final = ends[-1][1:]
    later = [(run, d) for _, found in final for run, _, d in found]
    acc, _, ahead = gemm(me, layout, (mine, theirs), middle, acc, later)
    kept, given, total = last_phase(me, ahead, acc, [t for t, _ in final], *tail)
    total = total + lax.ppermute(given, "section", swap)
    for k in range(1, x_count):
        total = total + lax.ppermute(kept, "mp", shift_pairs(x_count, k))
        total = total + lax.ppermute(
            given,
            ("mp", "section"),
            [
                (i * 2 + c, ((i + k) % x_count) * 2 + 1 - c)
                for i in range(x_count)
                for c in range(2)
            ],
        )
    return attended, total[0]


def judge_gathered(step_rows, norm_gain, head_weight, head_bias, class_weight, class_bias):
    full_rows = lax.all_gather(step_rows, "mp", axis=1, tiled=True)
    row_values = full_rows.astype(jnp.float32)
    power = jnp.mean(row_values * row_values, axis=1, keepdims=True)
    normed = (row_values * lax.rsqrt(power + 1e-06) * norm_gain).astype(jnp.bfloat16)
    projected = jnp.dot(
        normed,
        lax.all_gather(head_weight, ("batch", "section"), axis=0, tiled=True),
        preferred_element_type=jnp.float32,
    )
    hidden = jnp.maximum(projected + head_bias, 0.0).astype(jnp.bfloat16)
    partial_logits = jnp.dot(hidden, class_weight, preferred_element_type=jnp.float32)
    logits = lax.psum(partial_logits, "mp") + class_bias
    return logits[:, 1] - logits[:, 0]


def per_device(
    queries,
    new_keys,
    new_values,
    key_pages,
    value_pages,
    page_table,
    ancestry,
    lengths,
    step_rows,
    norm_gain,
    head_weight,
    head_bias,
    class_weight,
    class_bias,
):
    attention = Attention(
        queries, new_keys, new_values, key_pages, value_pages, page_table, ancestry, lengths
    )
    verifier = (step_rows, norm_gain, head_weight, head_bias, class_weight, class_bias)
    ring_fits = (
        4 <= lax.axis_size("batch") <= 8
        and lax.axis_size("mp") > 1
        and lax.axis_size("section") == 2
        and head_weight.shape[0] % (128 * lax.axis_size("group")) == 0
        and step_rows.shape[1] % (2 * head_weight.shape[0]) == 0
        and step_rows.shape[0] % 512 == 0
        and head_weight.shape[1] % 256 == 0
        and step_rows.shape[1] % head_weight.shape[0] == 0
    )
    if ring_fits:
        return both(attention, *verifier)
    arrived = attention.send(attention.pack(step_rows))
    returned = attention.send(attention.answer(arrived))
    return attention.finish(returned), judge_gathered(*verifier)


def solution(mesh):
    placed = (
        P("section", ("group", "batch"), "mp"),
        P("section", ("group", "batch"), "mp"),
        P("section", ("group", "batch"), "mp"),
        P("section", ("group", "batch"), None, "mp"),
        P("section", ("group", "batch"), None, "mp"),
        P(("group", "batch"), None),
        P("group"),
        P("group"),
        P(("group", "batch", "section"), "mp"),
        P(),
        P(("batch", "section"), "mp"),
        P("mp"),
        P("mp", None),
        P(),
    )
    return jax.shard_map(
        per_device,
        mesh=mesh,
        in_specs=placed,
        out_specs=(P("section", ("group", "batch"), "mp"), P(("group", "batch", "section"))),
        check_vma=False,
    )
```

```python
import functools

import jax
import jax.numpy as jnp
from jax import lax
from jax.experimental import pallas as pl
from jax.experimental.pallas import tpu as pltpu
from jax.sharding import PartitionSpec as P

HD = 128
VMEM_LIMIT = 32 << 20
BRIEF = pl.CostEstimate(flops=1, bytes_accessed=1, transcendentals=0)
ANY = pl.BlockSpec(memory_space=pltpu.HBM)
WAITED = pl.BlockSpec(memory_space=pl.ANY)
VMEM = pl.BlockSpec(memory_space=pltpu.VMEM)
SMEM = pl.BlockSpec(memory_space=pltpu.SMEM)


def in_hbm(arrays):
    return [pltpu.with_memory_space_constraint(a, pltpu.HBM) for a in arrays]


def pass_kernel(*refs):
    del refs


def after(passing, waited):
    many = len(passing)
    out = pl.pallas_call(
        pass_kernel,
        out_shape=[jax.ShapeDtypeStruct(a.shape, a.dtype) for a in passing],
        in_specs=[ANY] * many + [WAITED] * len(waited),
        out_specs=[ANY] * many,
        input_output_aliases={i: i for i in range(many)},
        cost_estimate=BRIEF,
        compiler_params=pltpu.CompilerParams(has_side_effects=True),
    )(*passing, *waited)
    return list(out)


def shift_pairs(count, step):
    return [(i, (i + step) % count) for i in range(count)]


def ring_order(count):
    return [0] + list(range(1, count, 2)) + [i for i in range(count - 1, 0, -1) if i % 2 == 0]


def pack_kernel(
    me, ancestry, lengths, queries, new_keys, new_values, waited,
    blobs, particle, length, pick, rows, request, seen, *, count, capacity
):
    del waited
    slots = queries.shape[0]
    at = 0
    for source in (queries, new_keys, new_values):
        for h in range(source.shape[1] // HD):
            rows[:, at, :] = source[:, h * HD : (h + 1) * HD].astype(jnp.float32)
            at += 1
    here = me[0]
    for k in range(count):
        seen[k] = 0

    def clear(i, carry):
        request[i] = 0
        particle[i] = 0
        length[i] = 1
        return carry

    lax.fori_loop(0, count * capacity, clear, 0)

    def ask(j, carry):
        owner = ancestry[here * slots + j] // slots
        rank = jnp.minimum(seen[owner], capacity - 1)
        seen[owner] = rank + 1
        pick[j] = owner * capacity + rank
        request[owner * capacity + rank] = j
        return carry

    lax.fori_loop(0, slots, ask, 0)

    def fill(i, carry):
        for k in range(count):
            blobs[k, i] = rows[request[k * capacity + i]].astype(jnp.bfloat16)
        return carry

    lax.fori_loop(0, capacity, fill, 0)
    for k in range(count):

        def answer(p, rank):
            ancestor = ancestry[k * slots + p]
            local = ancestor - here * slots
            match = (local >= 0) & (local < slots)
            at = k * capacity + jnp.minimum(rank, capacity - 1)

            @pl.when(match)
            def _():
                particle[at] = local
                length[at] = lengths[ancestor]

            return rank + match.astype(jnp.int32)

        lax.fori_loop(0, slots, answer, 0)


def pack(me, ancestry, lengths, queries, new_keys, new_values, waited, count, capacity):
    slots = queries.shape[0]
    depth = (queries.shape[1] + new_keys.shape[1] + new_values.shape[1]) // HD
    table = jax.ShapeDtypeStruct((count * capacity,), jnp.int32)
    out = pl.pallas_call(
        functools.partial(pack_kernel, count=count, capacity=capacity),
        out_shape=[jax.ShapeDtypeStruct((count, capacity, depth, HD), jnp.bfloat16)]
        + [table, table, jax.ShapeDtypeStruct((slots,), jnp.int32)],
        in_specs=[SMEM] * 3 + [VMEM] * 3 + [ANY],
        out_specs=[VMEM] + [SMEM] * 3,
        scratch_shapes=[
            pltpu.VMEM((slots, depth, HD), jnp.float32),
            pltpu.SMEM((count * capacity,), jnp.int32),
            pltpu.SMEM((count,), jnp.int32),
        ],
        cost_estimate=BRIEF,
        compiler_params=pltpu.CompilerParams(vmem_limit_bytes=VMEM_LIMIT),
    )(me, ancestry, lengths, queries, new_keys, new_values, waited)
    return out


def serve_kernel(
    particle, page_table, lengths, blobs, key_source, value_source, outs,
    key_pages, value_pages, sems, *, kv_local, unroll
):
    copies = [
        pltpu.make_async_copy(key_source, key_pages, sems.at[0]),
        pltpu.make_async_copy(value_source, value_pages, sems.at[1]),
    ]
    for c in copies:
        c.start()
    for c in copies:
        c.wait()
    count, capacity, heads = outs.shape[:3]
    group_size = heads // kv_local
    pages = page_table.shape[1]
    context = pages * key_pages.shape[1]
    score_scale = 1.0 / HD**0.5
    lanes_kv = lax.broadcasted_iota(jnp.int32, (heads, kv_local * HD), 1) // HD
    rows_kv = lax.broadcasted_iota(jnp.int32, (heads, kv_local * HD), 0) // group_size
    diagonal = lanes_kv == rows_kv
    positions = lax.broadcasted_iota(jnp.int32, (heads, context), 1)

    def spread(x):
        return jnp.broadcast_to(x[:, None, :], (kv_local, group_size, HD)).reshape(heads, HD)

    def together(k, slots):
        scores, own_products, own_values = [], [], []
        for slot in slots:
            at = k * capacity + slot
            rows = blobs[k, slot]
            query = rows[:heads].astype(jnp.float32)
            own_key = rows[heads : heads + kv_local].astype(jnp.float32)
            own_value = rows[heads + kv_local :].astype(jnp.float32)
            wide = jnp.concatenate([query] * kv_local, axis=1)
            wide = jnp.where(diagonal, wide, 0.0).astype(jnp.bfloat16)
            keys = jnp.concatenate(
                [key_pages[page_table[particle[at], i]] for i in range(pages)], axis=0
            )
            score = lax.dot_general(
                wide, keys, (((1,), (1,)), ((), ())), preferred_element_type=jnp.float32
            ) * score_scale
            scores.append(jnp.where(positions < lengths[at], score, -1e30))
            own_products.append(query * spread(own_key))
            own_values.append(spread(own_value))
        score = jnp.concatenate(scores, axis=0)
        top = jnp.max(score, axis=1, keepdims=True)
        weights = jnp.exp(score - top)
        own_score = jnp.sum(jnp.concatenate(own_products, axis=0), axis=1, keepdims=True) * score_scale
        own = jnp.exp(own_score - top)
        total = jnp.sum(weights, axis=1, keepdims=True) + own
        weights = weights.astype(jnp.bfloat16)
        for u, slot in enumerate(slots):
            at = k * capacity + slot
            mine = slice(u * heads, (u + 1) * heads)
            values = jnp.concatenate(
                [value_pages[page_table[particle[at], i]] for i in range(pages)], axis=0
            )
            mixed = jnp.dot(weights[mine], values, preferred_element_type=jnp.float32)
            numerator = jnp.concatenate(
                [
                    mixed[g * group_size : (g + 1) * group_size, g * HD : (g + 1) * HD]
                    for g in range(kv_local)
                ],
                axis=0,
            )
            result = (numerator + own[mine] * own_values[u]) / total[mine]
            outs[k, slot] = result.astype(jnp.bfloat16)

    def body(k, carry):
        for i in range(0, capacity, unroll):
            together(k, range(i, min(i + unroll, capacity)))
        return carry

    lax.fori_loop(0, count, body, 0)


def serve(particle, page_table, lengths, blobs, key_pages, value_pages):
    count, capacity, depth = blobs.shape[:3]
    kv_local = key_pages.shape[2] // HD
    heads = depth - 2 * kv_local
    return pl.pallas_call(
        functools.partial(serve_kernel, kv_local=kv_local, unroll=12),
        out_shape=jax.ShapeDtypeStruct((count, capacity, heads, HD), jnp.bfloat16),
        in_specs=[SMEM] * 3 + [VMEM] + [ANY] * 2,
        out_specs=VMEM,
        scratch_shapes=[
            pltpu.VMEM(key_pages.shape, key_pages.dtype),
            pltpu.VMEM(value_pages.shape, value_pages.dtype),
            pltpu.SemaphoreType.DMA((2,)),
        ],
        cost_estimate=BRIEF,
        compiler_params=pltpu.CompilerParams(vmem_limit_bytes=VMEM_LIMIT),
    )(particle, page_table, lengths, blobs, *in_hbm([key_pages, value_pages]))


def pick_kernel(pick, parts, *refs):
    out, rows = refs[-2:]
    slots = out.shape[0]
    capacity = parts.shape[1]

    flat = parts.reshape(parts.shape[0] * capacity, *parts.shape[2:])
    for j in range(slots):
        rows[j] = flat[pick[j]].astype(jnp.float32)
    for h in range(rows.shape[1]):
        out[:, h * HD : (h + 1) * HD] = rows[:, h, :].astype(jnp.bfloat16)


def pick_up(pick, parts, waited):
    heads = parts.shape[2]
    slots = pick.shape[0]
    return pl.pallas_call(
        pick_kernel,
        out_shape=jax.ShapeDtypeStruct((slots, heads * HD), jnp.bfloat16),
        in_specs=[SMEM, VMEM] + [WAITED] * len(waited),
        out_specs=VMEM,
        scratch_shapes=[pltpu.VMEM((slots, heads, HD), jnp.float32)],
        cost_estimate=BRIEF,
        compiler_params=pltpu.CompilerParams(vmem_limit_bytes=VMEM_LIMIT),
    )(pick, parts, *waited)


class Attention:
    def __init__(self, queries, new_keys, new_values, key_pages, value_pages, page_table, ancestry, lengths):
        self.count = lax.axis_size("batch")
        slots = page_table.shape[0]
        self.capacity = max(2, (2 * slots + self.count - 1) // self.count)
        self.rows = (ancestry, lengths, queries[0], new_keys[0], new_values[0])
        self.page_table, self.keys, self.values = page_table, key_pages[0], value_pages[0]

    def pack(self, waited):
        me = lax.axis_index("batch").reshape(1).astype(jnp.int32)
        blobs, self.particle, self.lengths, self.pick = pack(
            me, *self.rows, waited, self.count, self.capacity
        )
        return blobs

    def send(self, blobs):
        return lax.all_to_all(blobs, "batch", split_axis=0, concat_axis=0, tiled=True)

    def answer(self, arrived):
        return serve(
            self.particle, self.page_table, self.lengths, arrived, self.keys, self.values
        )

    def finish(self, returned, *waited):
        return pick_up(self.pick, returned, waited)[None]


def cut_kernel(me, weight, out, sem, *, back, other, y_count):
    share, width = out.shape
    core = 1 - me[2] if other else me[2]
    rows = pl.ds(pl.multiple_of(lax.rem(me[3] + back, y_count) * share, share), share)
    lanes = pl.ds(pl.multiple_of(core * width, width), width)
    copy = pltpu.make_async_copy(weight.at[rows, lanes], out, sem)
    copy.start()
    copy.wait()


def cut_share(me, weight, share, width, y_count, other, back):
    return pl.pallas_call(
        functools.partial(cut_kernel, back=back, other=other, y_count=y_count),
        out_shape=jax.ShapeDtypeStruct((share, width), weight.dtype),
        in_specs=[SMEM, ANY],
        out_specs=VMEM,
        scratch_shapes=[pltpu.SemaphoreType.DMA],
        cost_estimate=BRIEF,
        compiler_params=pltpu.CompilerParams(vmem_limit_bytes=VMEM_LIMIT),
    )(me, weight)


def power_kernel(x, waited, out):
    del waited
    rows, features = x.shape

    def body(i, carry):
        at = pl.ds(pl.multiple_of(i * HD, HD), HD)
        total = jnp.zeros((HD, HD), jnp.float32)
        for j in range(features // HD):
            v = x[at, j * HD : (j + 1) * HD].astype(jnp.float32)
            total = total + v * v
        out[pl.ds(i, 1), :] = jnp.sum(total.T, axis=0, keepdims=True)
        return carry

    lax.fori_loop(0, rows // HD, body, 0)


def row_power(x, waited):
    return pl.pallas_call(
        power_kernel,
        out_shape=jax.ShapeDtypeStruct((x.shape[0] // HD, HD), jnp.float32),
        in_specs=[VMEM, ANY],
        out_specs=VMEM,
        cost_estimate=BRIEF,
        compiler_params=pltpu.CompilerParams(vmem_limit_bytes=VMEM_LIMIT),
    )(x, waited)


def norm_kernel(me, x, *refs, total, count):
    powers, (gain, _, *outs) = refs[:count], refs[count:]
    rows, features = x.shape
    part = outs[0].shape[1]
    power = powers[0][...]
    for p in powers[1:]:
        power = power + p[...]
    scale = lax.rsqrt(power / total + 1e-06)
    start = me[0] * features

    for i in range(rows // HD):
        column = jnp.broadcast_to(scale[i : i + 1, :], (HD, HD)).T
        for j in range(features // HD):
            at = (slice(i * HD, (i + 1) * HD), slice(j * HD, (j + 1) * HD))
            lanes = pl.ds(pl.multiple_of(start + j * HD, HD), HD)
            value = (x[at].astype(jnp.float32) * column * gain[:, lanes]).astype(jnp.bfloat16)
            first = j * HD % part
            outs[j * HD // part][at[0], first : first + HD] = value


def normalise(me, x, powers, gain, pieces, waited):
    shape = (x.shape[0], x.shape[1] // pieces)
    return pl.pallas_call(
        functools.partial(
            norm_kernel, total=gain.shape[0], count=len(powers)
        ),
        out_shape=[jax.ShapeDtypeStruct(shape, jnp.bfloat16)] * pieces,
        in_specs=[SMEM] + [VMEM] * (2 + len(powers)) + [WAITED],
        out_specs=[VMEM] * pieces,
        cost_estimate=BRIEF,
        compiler_params=pltpu.CompilerParams(vmem_limit_bytes=VMEM_LIMIT),
    )(me, x, *powers, gain[None], waited)


class Layout:
    def __init__(self, order, x_count, y_count, block, features, part):
        self.order, self.x_count, self.y_count = order, x_count, y_count
        self.block, self.features, self.part = block, features, part
        self.share = block // y_count

    def place(self, me, run):
        hops, other, back, row = run
        x, z, s, y = me[0], me[1], me[2], me[3]
        count = len(self.order)
        owner = 0
        for i, at in enumerate(self.order):
            owner = owner + jnp.where(z == at, self.order[(i - hops) % count], 0)
        core = 1 - s if other else s
        feature = (2 * owner + core) * self.block + row
        if back is not None:
            group = y - back
            feature = feature + jnp.where(group < 0, group + self.y_count, group) * self.share
        per_device = self.features // self.part
        index = 0
        for i in range(1, self.x_count * per_device):
            index = index + (feature >= i * self.part).astype(jnp.int32)
        offset = feature - index * self.part
        index = index - x * per_device
        return self.rotated(index, per_device, self.x_count * per_device), offset

    def rotated(self, index, per_device, blocks):
        index = jnp.where(index < 0, index + blocks, index)
        place = 0
        for ahead in range(self.x_count):
            back = (self.x_count - ahead) % self.x_count
            inside = (index >= ahead * per_device) & (index < (ahead + 1) * per_device)
            place = place + jnp.where(inside, index + (back - ahead) * per_device, 0)
        return place


def carried(hops, back, share, first, count):
    runs = []
    for other in (False, True):
        low, high = max(first, other * share), min(first + count, (other + 1) * share)
        if low < high:
            runs.append(((hops, other, back, low - other * share), low - first, high - low))
    return runs


def merge_kernel(*refs, count):
    sources, out = refs[:count], refs[-1]
    at = 0
    for source in sources:
        out[at : at + source.shape[0]] = source[...]
        at += source.shape[0]


def merge(sources, waited):
    rows = sum(a.shape[0] for a in sources)
    return pl.pallas_call(
        functools.partial(merge_kernel, count=len(sources)),
        out_shape=jax.ShapeDtypeStruct((rows,) + sources[0].shape[1:], sources[0].dtype),
        in_specs=[VMEM] * len(sources) + [WAITED] * len(waited),
        out_specs=VMEM,
        cost_estimate=BRIEF,
        compiler_params=pltpu.CompilerParams(vmem_limit_bytes=VMEM_LIMIT),
    )(*sources, *waited)


def split_kernel(source, *refs, pieces):
    outs, sems = refs[-pieces - 1 : -1], refs[-1]
    rows = outs[0].shape[0]
    copies = [
        pltpu.make_async_copy(source.at[pl.ds(i * rows, rows)], out, sems.at[i])
        for i, out in enumerate(outs)
    ]
    for c in copies:
        c.start()
    for c in copies:
        c.wait()


def split(source, pieces, waited):
    shape = (source.shape[0] // pieces,) + source.shape[1:]
    return pl.pallas_call(
        functools.partial(split_kernel, pieces=pieces),
        out_shape=[jax.ShapeDtypeStruct(shape, source.dtype)] * pieces,
        in_specs=[ANY] + [WAITED] * len(waited),
        out_specs=[VMEM] * pieces,
        scratch_shapes=[pltpu.SemaphoreType.DMA((pieces,))],
        cost_estimate=BRIEF,
        compiler_params=pltpu.CompilerParams(vmem_limit_bytes=VMEM_LIMIT),
    )(source, *waited)


def gemm_kernel(me, *refs, parts, sources, runs, layout, has_acc, tile, via_hbm, later):
    refs = list(refs)
    halves = [refs[:parts], refs[parts : 2 * parts]]
    del refs[: 2 * parts]
    weights = refs[:sources]
    del refs[:sources]
    acc_in = refs.pop(0) if has_acc else None
    out, token = refs.pop(0), refs.pop(0)
    token[...] = jnp.zeros_like(token)
    ahead = refs.pop(0) if later else None
    x_v, w_v, sems, acc_v, acc_sem, later_sem = refs
    rows = halves[0][0].shape[0]
    width = w_v.shape[1]
    depths = [depth for _, _, _, depth in runs]
    starts = [sum(depths[:i]) for i in range(len(depths))]
    columns = pl.ds(pl.multiple_of(me[2] * width, width), width)

    def weight_copy(i):
        _, which, row, depth = runs[i]
        source = weights[which]
        lanes = slice(None) if source.shape[1] == width else columns
        source = source.at[row : row + depth, lanes]
        return pltpu.make_async_copy(source, w_v.at[pl.ds(starts[i], depths[i])], sems.at[i, 2])

    def row_copy(i, r, p, offset):
        return pltpu.make_async_copy(
            halves[r][p].at[:, pl.ds(offset, depths[i])],
            x_v.at[pl.ds(r * rows, rows), pl.ds(starts[i], depths[i])],
            sems.at[i, r],
        )

    for i, (run, _, _, _) in enumerate(runs):
        weight_copy(i).start()
        part, offset = layout.place(me, run)
        offset = pl.multiple_of(offset, HD)
        for r in range(2):
            for p in range(parts):
                pl.when(part == p)(row_copy(i, r, p, offset).start)
    held = acc_v if via_hbm else out
    if has_acc:
        pltpu.make_async_copy(acc_in, acc_v, acc_sem).start()
    first_lane = 0
    for run, depth in later:
        part, offset = layout.place(me, run)
        offset = pl.multiple_of(offset, HD)
        for r in range(2):
            for p in range(parts):
                copy = pltpu.make_async_copy(
                    halves[r][p].at[:, pl.ds(offset, depth)],
                    ahead.at[pl.ds(r * rows, rows), pl.ds(first_lane, depth)],
                    later_sem,
                )
                pl.when(part == p)(copy.start)
        first_lane += depth
    groups = []
    i = 0
    while i < len(runs):
        j, depth = i, 0
        while j < len(runs) and depth < 1024:
            depth += depths[j]
            j += 1
        groups.append((i, j))
        i = j
    for g, (first, last) in enumerate(groups):
        for i in range(first, last):
            weight_copy(i).wait()
            for r in range(2):
                row_copy(i, r, 0, 0).wait()
        if g == len(groups) - 1 and has_acc:
            pltpu.make_async_copy(acc_in, acc_v, acc_sem).wait()
        k0 = starts[first]
        k1 = starts[last - 1] + depths[last - 1]

        def body(m, carry):
            at = pl.ds(pl.multiple_of(m * tile, tile), tile)
            product = jnp.dot(x_v[at, k0:k1], w_v[k0:k1, :], preferred_element_type=jnp.float32)
            total = held[at, :] + product if g > 0 else product
            if has_acc and g == len(groups) - 1:
                total = total + acc_v[at, :]
            held[at, :] = total
            if via_hbm and g == len(groups) - 1:
                pltpu.make_async_copy(held.at[at, :], out.at[at, :], acc_sem).start()
            return carry

        lax.fori_loop(0, 2 * rows // tile, body, 0)
    if via_hbm:
        pltpu.make_async_copy(held, out, acc_sem).wait()
    if later:
        pltpu.make_async_copy(ahead, ahead, later_sem).wait()


def last_kernel(me, x, acc, *refs, tile):
    *weights, bias, class_weight, class_bias, kept, given, biased = refs
    rows, width = kept.shape[1], acc.shape[1]
    columns = pl.ds(pl.multiple_of(me[2] * width, width), width)
    classes = class_weight[1:2, columns] - class_weight[0:1, columns]
    for r, target in enumerate((kept, given)):

        def body(m, carry):
            at = pl.ds(pl.multiple_of(r * rows + m * tile, tile), tile)
            total = acc[at, :]
            first = 0
            for weight in weights:
                depth = weight.shape[0]
                total = total + jnp.dot(
                    x[at, first : first + depth], weight[...], preferred_element_type=jnp.float32
                )
                first += depth
            hidden = jnp.maximum(total + bias[:, columns], 0.0).astype(jnp.bfloat16)
            weighed = hidden.astype(jnp.float32) * classes
            folded = weighed[:, :HD]
            for j in range(1, width // HD):
                folded = folded + weighed[:, j * HD : (j + 1) * HD]
            for j in range(tile // HD):
                turned = folded[j * HD : (j + 1) * HD, :].T
                lanes = pl.ds(pl.multiple_of(m * tile + j * HD, HD), HD)
                target[:, lanes] = jnp.sum(turned, axis=0, keepdims=True)
            return carry

        lax.fori_loop(0, rows // tile, body, 0)
    biased[...] = kept[...] + (class_bias[1] - class_bias[0])


def last_phase(me, x, acc, weights, bias, class_weight, class_bias):
    rows = x.shape[0] // 2
    near = [pltpu.with_memory_space_constraint(a, pltpu.VMEM) for a in (x, acc)]
    return pl.pallas_call(
        functools.partial(last_kernel, tile=512),
        out_shape=[jax.ShapeDtypeStruct((1, rows), jnp.float32)] * 3,
        in_specs=[SMEM] + [VMEM] * (4 + len(weights)) + [SMEM],
        out_specs=[VMEM] * 3,
        cost_estimate=BRIEF,
        compiler_params=pltpu.CompilerParams(vmem_limit_bytes=VMEM_LIMIT),
    )(me, *near, *weights, bias, class_weight, class_bias)


def gemm(me, layout, halves, chunks, acc=None, later=()):
    weights = [w for w, _ in chunks]
    runs = [(run, i, row, d) for i, (_, found) in enumerate(chunks) for run, row, d in found]
    parts = len(halves[0])
    rows = halves[0][0].shape[0]
    depth = sum(d for _, _, _, d in runs)
    width = min(w.shape[1] for w in weights)
    args = [me, *in_hbm([*halves[0], *halves[1]]), *weights]
    if acc is not None:
        args += in_hbm([acc])
    space = pltpu.HBM if acc is None else pltpu.VMEM
    out_shape = [
        space((2 * rows, width), jnp.float32),
        jax.ShapeDtypeStruct((8, HD), jnp.float32),
    ]
    out_specs = [ANY if acc is None else VMEM, VMEM]
    if later:
        out_shape.append(pltpu.VMEM((2 * rows, sum(d for _, d in later)), jnp.bfloat16))
        out_specs.append(VMEM)
    return pl.pallas_call(
        functools.partial(
            gemm_kernel,
            parts=parts,
            sources=len(weights),
            runs=tuple(runs),
            layout=layout,
            has_acc=acc is not None,
            tile=512,
            via_hbm=acc is None,
            later=tuple(later),
        ),
        out_shape=out_shape,
        in_specs=[SMEM] + [ANY] * (len(args) - 1),
        out_specs=out_specs,
        scratch_shapes=[
            pltpu.VMEM((2 * rows, depth), jnp.bfloat16),
            pltpu.VMEM((depth, width), jnp.bfloat16),
            pltpu.SemaphoreType.DMA((len(runs), 3)),
            pltpu.VMEM((2 * rows, width), jnp.float32),
            pltpu.SemaphoreType.DMA,
            pltpu.SemaphoreType.DMA,
        ],
        cost_estimate=BRIEF,
        compiler_params=pltpu.CompilerParams(vmem_limit_bytes=VMEM_LIMIT),
    )(*args)


def both(attention, step_rows, norm_gain, head_weight, head_bias, class_weight, class_bias):
    z_count, x_count = lax.axis_size("batch"), lax.axis_size("mp")
    y_count = lax.axis_size("group")
    me = jnp.stack([lax.axis_index(a) for a in ("mp", "batch", "section", "group")]).astype(jnp.int32)
    swap = shift_pairs(2, 1)
    rows, features = step_rows.shape
    block, columns = head_weight.shape
    width = columns // 2
    share = block // y_count
    order = ring_order(z_count)
    ring = [(order[i], order[(i + 1) % z_count]) for i in range(z_count)]
    pieces, final_pieces = 2, 2
    layout = Layout(order, x_count, y_count, block, features, features // pieces)

    def forward(t):
        return lax.ppermute(t, "batch", ring)

    def over_group(t):
        return [lax.ppermute(t, "group", shift_pairs(y_count, k)) for k in range(1, y_count)]

    own = cut_share(me, head_weight, share, width, y_count, False, 0)
    given = [cut_share(me, head_weight, share, width, y_count, True, k) for k in range(y_count)]
    siblings = [lax.ppermute(g, "section", swap) for g in given]
    power = row_power(step_rows, own)
    merged = merge([own, siblings[0]], [power])
    whole = forward(merged)
    powers = [power] + [
        lax.ppermute(power, "mp", shift_pairs(x_count, k)) for k in range(1, x_count)
    ]
    mine = list(normalise(me, step_rows, powers, norm_gain, pieces, merged))
    raw = [
        lax.ppermute(part, "mp", shift_pairs(x_count, k))
        for k in range(1, x_count)
        for part in mine
    ]
    theirs = [lax.ppermute(part, "section", swap) for part in mine]
    blobs = attention.pack(siblings[0])
    arrived = attention.send(blobs)
    tail = [head_bias[None], class_weight.T.astype(jnp.float32), class_bias]
    chunks = [(head_weight, [((0, False, None, 0), 0, block)])] + [
        (t, [((0, True, (y_count - k) % y_count, 0), 0, share)]) for k, t in enumerate(siblings)
    ]
    waited = siblings[1:] + theirs
    for h in range(1, z_count - 2):
        if h > 1:
            whole = forward(whole)
        swapped = over_group(whole)
        chunks += [
            (t, carried(h, k, share, 0, 2 * share)) for k, t in enumerate([whole] + swapped)
        ]
        if h < z_count - 3:
            (whole,) = after([whole], waited)
            waited = swapped
    cuts = [forward(t) for t in split(whole, final_pieces, waited)]
    depth = 2 * share // final_pieces
    results = attention.answer(arrived)
    marks = [[blobs] + swapped + raw, [results]]
    second, last, travelled = [], [], []
    for j, t in enumerate(cuts):
        (t,) = after([t], marks[j])
        last.append(forward(t))
        swapped = over_group(t)
        if j + 1 < final_pieces:
            marks[j + 1] += swapped
        second += [
            (u, carried(z_count - 2, k, share, j * depth, depth))
            for k, u in enumerate([t] + swapped)
        ]
        travelled.append(t)
    for i, part in enumerate(raw):
        (part,) = after([part], [travelled[0]])
        mine.append(part)
        theirs.append(lax.ppermute(part, "section", swap))
    acc, early = gemm(me, layout, (mine, theirs), chunks)
    (results,) = after([results], [early])
    returned = attention.send(results)
    ends = []
    marks = [[], [early]]
    for j, t in enumerate(last):
        (t,) = after([t], marks[j])
        ends.append(
            [
                (u, carried(z_count - 1, k, share, j * depth, depth))
                for k, u in enumerate([t] + over_group(t))
            ]
        )
    attended = attention.finish(returned, early)
    middle = second + sum(ends[:-1], []) + ends[-1][:1]
    final = ends[-1][1:]
    later = [(run, d) for _, found in final for run, _, d in found]
    acc, _, ahead = gemm(me, layout, (mine, theirs), middle, acc, later)
    kept, given, total = last_phase(me, ahead, acc, [t for t, _ in final], *tail)
    total = total + lax.ppermute(given, "section", swap)
    for k in range(1, x_count):
        total = total + lax.ppermute(kept, "mp", shift_pairs(x_count, k))
        total = total + lax.ppermute(
            given,
            ("mp", "section"),
            [
                (i * 2 + c, ((i + k) % x_count) * 2 + 1 - c)
                for i in range(x_count)
                for c in range(2)
            ],
        )
    return attended, total[0]


def judge_gathered(step_rows, norm_gain, head_weight, head_bias, class_weight, class_bias):
    full_rows = lax.all_gather(step_rows, "mp", axis=1, tiled=True)
    row_values = full_rows.astype(jnp.float32)
    power = jnp.mean(row_values * row_values, axis=1, keepdims=True)
    normed = (row_values * lax.rsqrt(power + 1e-06) * norm_gain).astype(jnp.bfloat16)
    projected = jnp.dot(
        normed,
        lax.all_gather(head_weight, ("batch", "section"), axis=0, tiled=True),
        preferred_element_type=jnp.float32,
    )
    hidden = jnp.maximum(projected + head_bias, 0.0).astype(jnp.bfloat16)
    partial_logits = jnp.dot(hidden, class_weight, preferred_element_type=jnp.float32)
    logits = lax.psum(partial_logits, "mp") + class_bias
    return logits[:, 1] - logits[:, 0]


def per_device(
    queries,
    new_keys,
    new_values,
    key_pages,
    value_pages,
    page_table,
    ancestry,
    lengths,
    step_rows,
    norm_gain,
    head_weight,
    head_bias,
    class_weight,
    class_bias,
):
    attention = Attention(
        queries, new_keys, new_values, key_pages, value_pages, page_table, ancestry, lengths
    )
    verifier = (step_rows, norm_gain, head_weight, head_bias, class_weight, class_bias)
    ring_fits = (
        4 <= lax.axis_size("batch") <= 8
        and lax.axis_size("mp") > 1
        and lax.axis_size("section") == 2
        and head_weight.shape[0] % (128 * lax.axis_size("group")) == 0
        and step_rows.shape[1] % (2 * head_weight.shape[0]) == 0
        and step_rows.shape[0] % 512 == 0
        and head_weight.shape[1] % 256 == 0
        and step_rows.shape[1] % head_weight.shape[0] == 0
    )
    if ring_fits:
        return both(attention, *verifier)
    arrived = attention.send(attention.pack(step_rows))
    returned = attention.send(attention.answer(arrived))
    return attention.finish(returned), judge_gathered(*verifier)


def solution(mesh):
    placed = (
        P("section", ("group", "batch"), "mp"),
        P("section", ("group", "batch"), "mp"),
        P("section", ("group", "batch"), "mp"),
        P("section", ("group", "batch"), None, "mp"),
        P("section", ("group", "batch"), None, "mp"),
        P(("group", "batch"), None),
        P("group"),
        P("group"),
        P(("group", "batch", "section"), "mp"),
        P(),
        P(("batch", "section"), "mp"),
        P("mp"),
        P("mp", None),
        P(),
    )
    return jax.shard_map(
        per_device,
        mesh=mesh,
        in_specs=placed,
        out_specs=(P("section", ("group", "batch"), "mp"), P(("group", "batch", "section"))),
        check_vma=False,
    )
```
